32 devices in a mesh: seq: 8 (over y, x, core), head: 4 (over z).
Axes of the slice: x: 2, y: 2, z: 4, core: 2. Of those that a mesh axis runs over, the one named last changes fastest.
Arguments:
- queries: bfloat16 [1024, 4096], P(('seq', 'head')), may hold values from -6 to 6
- keys: bfloat16 [1024, 8192], P(('seq', 'head')), may hold values from -6 to 6
- values: bfloat16 [1024, 8192], P(('seq', 'head')), may hold values from -6 to 6
- betas: bfloat16 [1024, 64], P(('seq', 'head')), may hold values from 0 to 2
- log_gates: bfloat16 [1024, 32], P(('seq', 'head')), may hold values from -3 to 0, as said below
- starts: int32 [1024], P('seq'), may hold values 0 or 1
Outputs:
- readout: bfloat16 [1024, 4096], P('seq', 'head')
The draws below stay inside these ranges and needn't reach their ends.
Inputs may be any that keep to these rules, and one draw needn't show every extreme that they name: `log_gates`: log decays are negative.
All inputs are finite; a program needn't handle non-finite values. No bound on the sum of `starts` on one device may be relied on, other than what follows from the above.
Results may differ from the reference program's by a relative error of at most 0.001.
Values may be sent and summed in bfloat16 or wider, within the bound.
No kernel may reach another device: no remote copies, remote signals or barrier semaphores. Data moves between devices by JAX's collectives and lax.ppermute only.
A program may use at most 64 MiB of HBM per device.

```python
import math
import jax
import jax.numpy as jnp
from jax import lax

HEAD_TOTAL = 32
DK = 128
DV = 128
NH = 2
TOK_DEV = 32
SLAB_TOKENS = 1024


def draw_betas(key, part):
    first, second = jax.random.split(key, 2)
    scales = jnp.exp(jax.random.uniform(first, (1, HEAD_TOTAL, 1), jnp.float32, math.log(0.003), math.log(1.2)))
    spread = jax.random.uniform(second, (SLAB_TOKENS, HEAD_TOTAL, NH), jnp.float32, 0.5, 1.5)
    return (scales * spread).reshape(SLAB_TOKENS, HEAD_TOTAL * NH).astype(jnp.bfloat16)


def draw_log_gates(key, part):
    first, second, third_factor, fourth_factor = jax.random.split(key, 4)
    low_end = math.log(1.0 / (8.0 * SLAB_TOKENS))
    high_end = math.log(1.0 / 30.0)
    coarse_estimate = jax.random.uniform(second, (SLAB_TOKENS, HEAD_TOTAL), jnp.float32, 0.5, 1.5)
    decay_rates = jnp.exp(jax.random.uniform(first, (1, HEAD_TOTAL), jnp.float32, low_end, high_end))
    group_token_rows = (jax.random.uniform(third_factor, (SLAB_TOKENS, 1), jnp.float32) < 4.0 / SLAB_TOKENS).astype(jnp.float32)
    group_length = jax.random.uniform(fourth_factor, (SLAB_TOKENS, HEAD_TOTAL), jnp.float32, 0.2, 0.7)
    return (-(decay_rates * coarse_estimate) - group_token_rows * group_length).astype(jnp.bfloat16)


def touch_ends(array, key, low, high):
    place = [jax.random.randint(jax.random.fold_in(key, axis), (), 0, length) for axis, length in enumerate(array.shape)]
    longest = array.shape.index(max(array.shape))
    beside = place[:longest] + [(place[longest] + 1) % array.shape[longest]] + place[longest + 1:]
    return array.at[tuple(place)].set(low).at[tuple(beside)].set(high)


def level_of(stream_key, extent, cuts, low, high):
    def one(axis_at, parts):
        draws = jax.random.uniform(jax.random.fold_in(jax.random.fold_in(stream_key, 6), axis_at), (parts,), jnp.float32, low / len(cuts), high / len(cuts))
        return jnp.repeat(jnp.exp(draws), extent[axis_at] // parts).reshape((-1,) + (1,) * (len(extent) - axis_at - 1))

    gain = one(*cuts[0])
    for cut in cuts[1:]:
        gain = gain * one(*cut)
    return gain


def gaussian(key, extent, deviation, reach, pieces=(), held_as=jnp.bfloat16):
    array = deviation * jax.random.normal(key, extent, jnp.float32)
    if pieces:
        array = array * level_of(key, extent, pieces, -0.22, 0.18)
    return jnp.clip(array, -reach, reach).astype(held_as)


def setup_inputs(seed: int = 0) -> dict:
    key_list = jax.random.split(jax.random.key(seed), 7)
    queries = gaussian(key_list[0], (SLAB_TOKENS, HEAD_TOTAL * DK), 1.0, 6.0, ((0, 32),))
    keys = gaussian(key_list[1], (SLAB_TOKENS, HEAD_TOTAL * NH * DK), 1.0, 6.0, ((0, 32),))
    values = gaussian(key_list[2], (SLAB_TOKENS, HEAD_TOTAL * NH * DV), 1.0, 6.0, ((0, 32),))
    betas = draw_betas(jax.random.fold_in(key_list[6], 71), 0)
    log_gates = draw_log_gates(jax.random.fold_in(key_list[6], 71), 0)
    starts = touch_ends((jax.random.randint(key_list[5], (SLAB_TOKENS,), 0, TOK_DEV * 64) < 1).astype(jnp.int32), jax.random.fold_in(key_list[5], 1), 0, 1)
    return dict(queries=queries, keys=keys, values=values, betas=betas, log_gates=log_gates, starts=starts)


EPSILON = 1e-06
PRECISE = lax.Precision.HIGHEST

def reference(queries, keys, values, betas, log_gates, starts):
    query_all = queries.astype(jnp.float32).reshape(SLAB_TOKENS, HEAD_TOTAL, DK)
    key_all = keys.astype(jnp.float32).reshape(SLAB_TOKENS, HEAD_TOTAL, NH, DK)
    key_all = key_all * lax.rsqrt(lax.optimization_barrier(jnp.sum(key_all * key_all, -1, keepdims=True)) + EPSILON)
    value_all = values.astype(jnp.float32).reshape(SLAB_TOKENS, HEAD_TOTAL, NH, DV)
    beta_all = betas.astype(jnp.float32).reshape(SLAB_TOKENS, HEAD_TOTAL, NH)
    gate_all = jnp.exp(log_gates.astype(jnp.float32))

    def advance_token(memory, inputs_now):
        query_now, key_now, value_now, beta_now, gate_now, start_now = inputs_now
        retain = gate_now * (1 - start_now).astype(jnp.float32)
        memory = memory * retain[:, None, None]
        for householder in range(NH):
            key_step = key_now[:, householder]
            recalled = jnp.einsum('hd,hde->he', key_step, memory, precision=PRECISE)
            change = value_now[:, householder] - recalled
            memory = memory + beta_now[:, householder, None, None] * key_step[:, :, None] * change[:, None, :]
        readout = jnp.einsum('hd,hde->he', query_now, memory, precision=PRECISE)
        return (memory, readout)
    initial = jnp.zeros((HEAD_TOTAL, DK, DV), jnp.float32)
    _, readouts = lax.scan(advance_token, initial, (query_all, key_all, value_all, beta_all, gate_all, starts))
    return readouts.reshape(SLAB_TOKENS, HEAD_TOTAL * DV).astype(jnp.bfloat16)
```

```python
import jax
import jax.numpy as jnp
from jax import lax
from jax.experimental import pallas as pl
from jax.experimental.pallas import tpu as pltpu
from jax.sharding import Mesh
from jax.sharding import PartitionSpec as P

DK = 128
DV = 128
NH = 2
TOK = 32
CHUNK = 2 * TOK
REFL = CHUNK * NH
GROUP = 4
EPSILON = 1e-06

KEY_ROW = 0
VALUE_ROW = NH * TOK
QUERY_ROW = 2 * NH * TOK
SCALE_ROW = QUERY_ROW + TOK
SCALE_ROWS = 16
PACK_ROWS = SCALE_ROW + SCALE_ROWS

BF16 = jnp.bfloat16
F32 = jnp.float32
NT = (((1,), (1,)), ((), ()))


def iota(shape, axis):
    return lax.broadcasted_iota(jnp.int32, shape, axis)


def dot(left, right):
    return jnp.dot(left, right, preferred_element_type=F32)


def dot_nt(left, right):
    return lax.dot_general(left, right, NT, preferred_element_type=F32)


def split(value):
    high = value.astype(BF16)
    low = (value - high.astype(F32)).astype(BF16)
    return high, low


def beside(value):
    return jnp.concatenate(split(value), 1)


def twice(value):
    return jnp.concatenate([value, value], 0)


def factor(value):
    high, low = split(value)
    return jnp.concatenate(
        [jnp.concatenate([high, low], 1), jnp.concatenate([high, jnp.zeros_like(low)], 1)], 0
    )


def product(left_pair, right_factor):
    both = dot(left_pair, right_factor)
    half = both.shape[1] // 2
    return both[:, :half] + both[:, half:]


def pack_kernel(queries, keys, values, betas, log_gates, starts, out):
    heads = queries.shape[1] // DK
    for head in range(heads):
        for step in range(NH):
            column = (head * NH + step) * DK
            out[head, KEY_ROW + step * TOK : KEY_ROW + (step + 1) * TOK, :] = keys[
                :, column : column + DK
            ]
            out[head, VALUE_ROW + step * TOK : VALUE_ROW + (step + 1) * TOK, :] = values[
                :, column : column + DV
            ]
        out[head, QUERY_ROW : QUERY_ROW + TOK, :] = queries[:, head * DK : (head + 1) * DK]
    pieces = []
    for step in range(NH):
        pick = (iota((heads, heads * NH), 1) == iota((heads, heads * NH), 0) * NH + step).astype(
            BF16
        )
        pieces.append(dot_nt(pick, betas[...]))
    same = (iota((heads, heads), 0) == iota((heads, heads), 1)).astype(BF16)
    pieces.append(dot_nt(same, log_gates[...]))
    pieces.append(jnp.broadcast_to(starts[...].astype(F32), (heads, TOK)))
    scales = jnp.concatenate(pieces, 1).astype(BF16)
    for head in range(heads):
        out[head, SCALE_ROW:PACK_ROWS, :] = jnp.broadcast_to(
            scales[head : head + 1, :], (SCALE_ROWS, 4 * TOK)
        )


def pack(queries, keys, values, betas, log_gates, starts):
    heads = queries.shape[1] // DK
    return pl.pallas_call(
        pack_kernel,
        out_shape=jax.ShapeDtypeStruct((heads, PACK_ROWS, DK), BF16),
        compiler_params=pltpu.CompilerParams(vmem_limit_bytes=32 * 2**20),
        name="pack",
    )(queries, keys, values, betas, log_gates, starts)


def place(index):
    block = index // (NH * TOK)
    step = (index // TOK) % NH
    token = index % TOK
    return block, step, token, (block * TOK + token) * NH + step


def scale_maps():
    shape = (REFL, 8 * TOK)
    block, step, token, _ = place(iota(shape, 0))
    column = iota(shape, 1)
    source_block = column // (4 * TOK)
    kind = (column // TOK) % 4
    source = source_block * TOK + column % TOK
    now = block * TOK + token
    decay = (kind == NH) & (source <= now)
    segment = (kind == NH + 1) & (source <= now)
    beta = (kind == step) & (source == now)
    return jnp.concatenate([part.astype(F32) for part in (decay, segment, beta)], 0).astype(BF16)


def piece_rows(size):
    if size == TOK:
        return [slice(NH * TOK, 2 * NH * TOK)]
    return [
        slice(start, start + size)
        for part in range(2 * NH)
        for start in range(part * TOK + size, (part + 1) * TOK, 2 * size)
    ]


def taken(value, slices):
    return jnp.concatenate([value[each] for each in slices], 0) if len(slices) > 1 else value[slices[0]]


def put(base, rows, slices):
    pieces = []
    at = 0
    done = 0
    for each in slices:
        if each.start > at:
            pieces.append(base[at : each.start])
        size = each.stop - each.start
        pieces.append(base[each] + rows[done : done + size])
        done += size
        at = each.stop
    if at < REFL:
        pieces.append(base[at:])
    return jnp.concatenate(pieces, 0)


def inverses(lowers):
    small = 8
    count = len(lowers)
    lane = iota((small, REFL), 1)
    group_of = (lane // (NH * TOK)) * (TOK // small) + (lane % TOK) // small
    groups = [(block, piece) for block in range(2) for piece in range(TOK // small)]

    def start_row(block, step, piece):
        return block * NH * TOK + step * TOK + piece * small

    folded = []
    for lower in lowers:
        for step in range(NH):
            rows = jnp.zeros((small, REFL), F32)
            for number, (block, piece) in enumerate(groups):
                first = start_row(block, step, piece)
                rows = jnp.where(group_of == number, lower[first : first + small], rows)
            folded.append(rows)
    height = NH * small
    lower_fold = jnp.concatenate(folded, 0)
    wide = iota((count * height, REFL), 1)
    high = iota((count * height, REFL), 0) % height
    inverse = ((wide // TOK) % NH == high // small) & (wide % small == high % small)
    inverse = inverse.astype(F32).reshape(count, height, REFL)
    for token in range(small):
        for step in range(NH):
            if token == small - 1 and step == NH - 1:
                continue
            source = (wide // (NH * TOK)) * (NH * TOK) + step * TOK + (wide % TOK) // small * small + token
            column = jnp.take_along_axis(lower_fold, source, axis=1, mode="promise_in_bounds")
            row = step * small + token
            inverse = inverse - column.reshape(count, height, REFL) * inverse[:, row : row + 1, :]
    results = []
    for number in range(count):
        pieces = []
        for block in range(2):
            for step in range(NH):
                rows = inverse[number, step * small : (step + 1) * small]
                for piece in range(TOK // small):
                    mine = group_of == block * (TOK // small) + piece
                    pieces.append(jnp.where(mine, rows, 0.0))
        results.append(jnp.concatenate(pieces, 0))
    size = small
    zero = jnp.zeros((REFL, REFL), F32)
    while size < CHUNK:
        slices = piece_rows(size)
        row_block, _, row_token, _ = place(iota((REFL, REFL), 0))
        column_block, _, column_token, _ = place(iota((REFL, REFL), 1))
        row_piece = (row_block * TOK + row_token) // size
        column_piece = (column_block * TOK + column_token) // size
        linked = taken(row_piece, slices) == taken(column_piece, slices) + 1
        crossings = [
            product(beside(jnp.where(linked, taken(lower, slices), 0.0)), factor(result))
            for lower, result in zip(lowers, results)
        ]
        changes = [
            product(beside(taken(result, slices)), factor(put(zero, crossing, slices)))
            for crossing, result in zip(crossings, results)
        ]
        results = [put(result, -change, slices) for change, result in zip(changes, results)]
        size *= 2
    return results


def chunk_rows(packed, chunk, first, count):
    return jnp.concatenate(
        [packed[2 * chunk, first : first + count, :], packed[2 * chunk + 1, first : first + count, :]], 0
    )


def read_rows(value):
    return jnp.concatenate(
        [
            value[(NH - 1) * TOK : NH * TOK],
            value[(2 * NH - 1) * TOK : 2 * NH * TOK],
        ],
        0,
    )


def head_kernel(packed, *rest):
    entry, out, leave = rest if len(rest) == 3 else (None, rest[0], None)
    chunks = packed.shape[0] // 2
    scales = packed[:, SCALE_ROW:PACK_ROWS, :].reshape(2 * chunks * SCALE_ROWS, 4 * TOK)
    picks = []
    for block in range(2):
        shape = (chunks, 2 * chunks * SCALE_ROWS)
        pick = iota(shape, 1) == (2 * iota(shape, 0) + block) * SCALE_ROWS
        picks.append(dot(pick.astype(BF16), scales))
    by_chunk = jnp.concatenate(picks, 1).astype(BF16)
    maps = scale_maps()
    as_rows = dot_nt(by_chunk, maps)
    as_columns = dot_nt(maps, by_chunk)
    decay_row, segment_row, beta_row = (
        as_rows[:, number * REFL : (number + 1) * REFL] for number in range(3)
    )
    decay_column, segment_column, beta_column = (
        as_columns[number * REFL : (number + 1) * REFL] for number in range(3)
    )
    carried_row = jnp.exp(decay_row) * (segment_row == 0).astype(F32)
    carried_column = jnp.exp(decay_column) * (segment_column == 0).astype(F32)
    last = REFL - 1
    end_row = jnp.exp(decay_row[:, last:] - decay_row) * (segment_row[:, last:] == segment_row).astype(F32)
    square = (REFL, REFL)
    _, _, _, row_time = place(iota(square, 0))
    _, _, _, column_time = place(iota(square, 1))
    causal = row_time >= column_time
    strict = row_time > column_time
    diagonal = row_time == column_time
    state = jnp.zeros((DV, DK), F32) if entry is None else entry[...]
    for base in range(0, chunks, GROUP):
        members = range(base, min(base + GROUP, chunks))
        keys = [chunk_rows(packed, chunk, KEY_ROW, NH * TOK) for chunk in members]
        grams = [dot_nt(key, key) for key in keys]
        squares = [jnp.where(diagonal, gram, 0.0) for gram in grams]
        norm_rows = [lax.rsqrt(jnp.sum(each, 0, keepdims=True) + EPSILON) for each in squares]
        norm_columns = [lax.rsqrt(jnp.sum(each, 1, keepdims=True) + EPSILON) for each in squares]
        ratios = []
        lowers = []
        for number, chunk in enumerate(members):
            linked = causal & (segment_column[:, chunk : chunk + 1] == segment_row[chunk : chunk + 1])
            gap = decay_column[:, chunk : chunk + 1] - decay_row[chunk : chunk + 1]
            ratio = jnp.where(linked, jnp.exp(jnp.minimum(gap, 0.0)), 0.0) * norm_rows[number]
            ratios.append(read_rows(ratio))
            strengths = beta_column[:, chunk : chunk + 1] * norm_columns[number]
            lowers.append(jnp.where(strict, strengths * ratio * grams[number], 0.0))
        solved = inverses(lowers)
        factors = [factor(each) for each in solved]
        beta_rows = [beta_row[chunk : chunk + 1] for chunk in members]
        kept_rows = [
            beta_row[chunk : chunk + 1] * carried_row[chunk : chunk + 1] * norm
            for chunk, norm in zip(members, norm_rows)
        ]
        turned_keys = [key.T for key in keys]
        ends = [
            product(beside(turned.astype(F32) * (end_row[chunk : chunk + 1] * norm)), each)
            for chunk, turned, norm, each in zip(members, turned_keys, norm_rows, factors)
        ]
        same = (iota((DK, DK), 0) == iota((DK, DK), 1)).astype(F32)
        transitions = [
            carried_row[chunk : chunk + 1, last:] * same
            - dot_nt(jnp.concatenate([turned, turned], 1), beside(end * kept))
            for chunk, turned, end, kept in zip(members, turned_keys, ends, kept_rows)
        ]
        values = [chunk_rows(packed, chunk, VALUE_ROW, NH * TOK) for chunk in members]
        turned_values = [value.T for value in values]
        injects = [
            dot_nt(jnp.concatenate([turned, turned], 1), beside(end * beta))
            for turned, end, beta in zip(turned_values, ends, beta_rows)
        ]
        queries = [chunk_rows(packed, chunk, QUERY_ROW, TOK) for chunk in members]
        scores = [
            product(beside(dot_nt(query, key) * ratio), each)
            for query, key, ratio, each in zip(queries, keys, ratios, factors)
        ]
        inner = [
            dot(beside(score * beta), twice(value))
            for score, beta, value in zip(scores, beta_rows, values)
        ]
        readers = [
            read_rows(carried_column[:, chunk : chunk + 1]) * query.astype(F32)
            - dot(beside(score * kept), twice(key))
            for chunk, query, score, kept, key in zip(members, queries, scores, kept_rows, keys)
        ]
        for number, chunk in enumerate(members):
            high, low = split(state)
            turned = jnp.concatenate(
                [jnp.concatenate([high, high], 1), jnp.concatenate([low, jnp.zeros_like(low)], 1)], 0
            )
            both = dot_nt(beside(readers[number]), turned)
            result = inner[number] + both[:, :DV] + both[:, DV:]
            out[chunk * CHUNK : (chunk + 1) * CHUNK, :] = result.astype(BF16)
            state = product(jnp.concatenate([high, low], 1), factor(transitions[number])) + injects[number]
    if leave is not None:
        leave[...] = state


def head_recurrence(packed, entry=None):
    blocks = packed.shape[0]
    out = jax.ShapeDtypeStruct((blocks * TOK, DV), BF16)
    state = jax.ShapeDtypeStruct((DV, DK), F32)
    return pl.pallas_call(
        head_kernel,
        out_shape=out if entry is None else (out, state),
        compiler_params=pltpu.CompilerParams(vmem_limit_bytes=48 * 2**20),
        name="head_recurrence",
    )(*((packed,) if entry is None else (packed, entry)))


def local(queries, keys, values, betas, log_gates, starts):
    at = lax.axis_index("head") * TOK
    own_starts = lax.dynamic_slice(starts, (at,), (TOK,)).reshape(1, TOK)
    packed = pack(queries, keys, values, betas, log_gates, own_starts)
    groups = lax.axis_size("head")
    places = packed.shape[0] // groups
    packed = packed.reshape(groups, places, PACK_ROWS, DK).transpose(1, 0, 2, 3)
    packed = packed.reshape(groups * places, PACK_ROWS, DK)
    received = lax.all_to_all(packed, ("place", "head"), split_axis=0, concat_axis=0, tiled=True)
    spans = lax.axis_size("span")
    if spans == 1:
        out = head_recurrence(received)
    else:
        forward = [(index, index + 1) for index in range(spans - 1)]

        def advance(_, carry):
            entry, _ = carry
            out, leave = head_recurrence(received, entry)
            return lax.ppermute(leave, "span", forward), out

        nothing = jnp.zeros((received.shape[0] * TOK, DV), BF16)
        _, out = lax.fori_loop(0, spans, advance, (jnp.zeros((DV, DK), F32), nothing))
    out = out.reshape(places, out.shape[0] // places, DV)
    out = lax.all_to_all(out, "place", split_axis=0, concat_axis=0, tiled=True)
    return out.transpose(1, 0, 2).reshape(out.shape[1], places * DV)


def solution(mesh):
    groups = mesh.shape["head"]

    def run(queries, keys, values, betas, log_gates, starts):
        places = log_gates.shape[1] // groups
        spans = mesh.shape["seq"] // places
        split_mesh = Mesh(
            mesh.devices.reshape(spans, places, groups), ("span", "place", "head")
        )
        rows = P(("span", "place", "head"), None)
        return jax.shard_map(
            local,
            mesh=split_mesh,
            in_specs=(rows, rows, rows, rows, rows, P(("span", "place"))),
            out_specs=P(("span", "place"), "head"),
            check_vma=False,
        )(queries, keys, values, betas, log_gates, starts)

    return run
```

```python
import jax
import jax.numpy as jnp
from jax import lax
from jax.experimental import pallas as pl
from jax.experimental.pallas import tpu as pltpu
from jax.sharding import Mesh
from jax.sharding import PartitionSpec as P

DK = 128
DV = 128
NH = 2
TOK = 32
CHUNK = 2 * TOK
REFL = CHUNK * NH
GROUP = 8
EPSILON = 1e-06

KEY_ROWS = NH * TOK
SCALE_ROWS = 16

BF16 = jnp.bfloat16
F32 = jnp.float32
NT = (((1,), (1,)), ((), ()))


def iota(shape, axis):
    return lax.broadcasted_iota(jnp.int32, shape, axis)


def dot(left, right):
    return jnp.dot(left, right, preferred_element_type=F32)


def dot_nt(left, right):
    return lax.dot_general(left, right, NT, preferred_element_type=F32)


def split(value):
    high = value.astype(BF16)
    low = (value - high.astype(F32)).astype(BF16)
    return high, low


def beside(value):
    return jnp.concatenate(split(value), 1)


def twice(value):
    return jnp.concatenate([value, value], 0)


def factor(value):
    return factor_of(*split(value))


def factor_of(high, low):
    return jnp.concatenate(
        [jnp.concatenate([high, low], 1), jnp.concatenate([high, jnp.zeros_like(low)], 1)], 0
    )


def product(left_pair, right_factor):
    both = dot(left_pair, right_factor)
    half = both.shape[1] // 2
    return both[:, :half] + both[:, half:]


def place(index):
    block = index // (NH * TOK)
    step = (index // TOK) % NH
    token = index % TOK
    return block, step, token, (block * TOK + token) * NH + step


def scale_maps():
    shape = (REFL, 8 * TOK)
    block, step, token, _ = place(iota(shape, 0))
    column = iota(shape, 1)
    source_block = column // (4 * TOK)
    kind = (column // TOK) % 4
    source = source_block * TOK + column % TOK
    now = block * TOK + token
    decay = (kind == NH) & (source <= now)
    segment = (kind == NH + 1) & (source <= now)
    beta = (kind == step) & (source == now)
    return jnp.concatenate([part.astype(F32) for part in (decay, segment, beta)], 0).astype(BF16)


def piece_rows(size):
    if size == TOK:
        return [slice(NH * TOK, 2 * NH * TOK)]
    return [
        slice(start, start + size)
        for part in range(2 * NH)
        for start in range(part * TOK + size, (part + 1) * TOK, 2 * size)
    ]


def taken(value, slices):
    return jnp.concatenate([value[each] for each in slices], 0) if len(slices) > 1 else value[slices[0]]


def put(base, rows, slices):
    pieces = []
    at = 0
    done = 0
    for each in slices:
        if each.start > at:
            pieces.append(base[at : each.start])
        size = each.stop - each.start
        pieces.append(base[each] + rows[done : done + size])
        done += size
        at = each.stop
    if at < REFL:
        pieces.append(base[at:])
    return jnp.concatenate(pieces, 0)


def inverses(lowers):
    small = 8
    count = len(lowers)
    lane = iota((small, REFL), 1)
    group_of = (lane // (NH * TOK)) * (TOK // small) + (lane % TOK) // small
    groups = [(block, piece) for block in range(2) for piece in range(TOK // small)]

    def start_row(block, step, piece):
        return block * NH * TOK + step * TOK + piece * small

    folded = []
    for lower in lowers:
        for step in range(NH):
            rows = jnp.zeros((small, REFL), F32)
            for number, (block, piece) in enumerate(groups):
                first = start_row(block, step, piece)
                rows = jnp.where(group_of == number, lower[first : first + small], rows)
            folded.append(rows)
    height = NH * small
    lower_fold = jnp.concatenate(folded, 0)
    wide = iota((count * height, REFL), 1)
    high = iota((count * height, REFL), 0) % height
    inverse = ((wide // TOK) % NH == high // small) & (wide % small == high % small)
    inverse = inverse.astype(F32).reshape(count, height, REFL)
    for token in range(small):
        for step in range(NH):
            if token == small - 1 and step == NH - 1:
                continue
            source = (wide // (NH * TOK)) * (NH * TOK) + step * TOK + (wide % TOK) // small * small + token
            column = jnp.take_along_axis(lower_fold, source, axis=1, mode="promise_in_bounds")
            row = step * small + token
            inverse = inverse - column.reshape(count, height, REFL) * inverse[:, row : row + 1, :]
    results = []
    for number in range(count):
        pieces = []
        for block in range(2):
            for step in range(NH):
                rows = inverse[number, step * small : (step + 1) * small]
                for piece in range(TOK // small):
                    mine = group_of == block * (TOK // small) + piece
                    pieces.append(jnp.where(mine, rows, 0.0))
        results.append(jnp.concatenate(pieces, 0))
    size = small
    zero = jnp.zeros((REFL, REFL), F32)
    while size < CHUNK:
        slices = piece_rows(size)
        row_block, _, row_token, _ = place(iota((REFL, REFL), 0))
        column_block, _, column_token, _ = place(iota((REFL, REFL), 1))
        row_piece = (row_block * TOK + row_token) // size
        column_piece = (column_block * TOK + column_token) // size
        linked = taken(row_piece, slices) == taken(column_piece, slices) + 1
        crossings = [
            product(beside(jnp.where(linked, taken(lower, slices), 0.0)), factor(result))
            for lower, result in zip(lowers, results)
        ]
        changes = [
            product(beside(taken(result, slices)), factor(put(zero, crossing, slices)))
            for crossing, result in zip(crossings, results)
        ]
        results = [put(result, -change, slices) for change, result in zip(changes, results)]
        size *= 2
    return results


def read_rows(value):
    return jnp.concatenate(
        [
            value[(NH - 1) * TOK : NH * TOK],
            value[(2 * NH - 1) * TOK : 2 * NH * TOK],
        ],
        0,
    )


def call(kernel, outs, *args, scratch=(), flops=0, name=None):
    return pl.pallas_call(
        kernel,
        out_shape=outs,
        scratch_shapes=scratch,
        compiler_params=pltpu.CompilerParams(vmem_limit_bytes=24 * 2**20),
        cost_estimate=pl.CostEstimate(flops=flops, bytes_accessed=0, transcendentals=0),
        name=name,
    )(*args)


def shape(*sizes, dtype=BF16):
    return jax.ShapeDtypeStruct(sizes, dtype)


def axis_index(axis):
    return lax.axis_index(axis).astype(jnp.int32)


class Sizes:
    def __init__(self, groups, group_heads, chips):
        self.groups = groups
        self.group_heads = group_heads
        self.heads = group_heads // 2
        self.chips = chips
        self.units = self.heads * groups
        self.swapped = chips == self.heads and chips & (chips - 1) == 0

    def unit(self, number):
        return number // self.groups, number % self.groups


def shifted(index, by, size):
    moved = index + by
    return jnp.where(moved >= size, moved - size, moved)


def block_columns(source, first, count):
    return [
        source[:, pl.ds(pl.multiple_of(first + number * DK, DK), DK)] for number in range(count)
    ]


def pack_keys(sizes, keys, betas, log_gates, starts):
    rows = sizes.heads * KEY_ROWS
    count = sizes.heads * NH

    def kernel(keys, betas, log_gates, starts, *outs):
        z = axis_index("head")
        core = axis_index("core")
        heads = log_gates.shape[1]
        pieces = []
        for step in range(NH):
            extent = (heads, heads * NH)
            pick = iota(extent, 1) == iota(extent, 0) * NH + step
            pieces.append(dot_nt(pick.astype(BF16), betas[...]))
        same = iota((heads, heads), 0) == iota((heads, heads), 1)
        pieces.append(dot_nt(same.astype(BF16), log_gates[...]))
        pieces.append(jnp.broadcast_to(starts[...].astype(F32), (heads, TOK)))
        scales = jnp.concatenate(pieces, 1).astype(BF16)
        for ahead, out in enumerate(outs):
            target = shifted(z, ahead, sizes.groups)
            for side in range(2):
                owner = jnp.bitwise_xor(core, side)
                first = ((target * 2 + owner) * sizes.heads) * NH * DK
                for number, piece in enumerate(block_columns(keys, first, count)):
                    at = side * rows + number * TOK
                    out[at : at + TOK, :] = piece
            extent = (SCALE_ROWS, heads)
            pick = (iota(extent, 1) == target * sizes.group_heads + iota(extent, 0)) & (
                iota(extent, 0) < sizes.group_heads
            )
            out[2 * rows :, :] = dot(pick.astype(BF16), scales).astype(BF16)

    outs = [shape(2 * rows + SCALE_ROWS, DK)] * sizes.groups
    return call(kernel, outs, keys, betas, log_gates, starts, name="pack_keys")


def swap_keys(sizes, arrived):
    rows = sizes.heads * KEY_ROWS

    def kernel(*refs):
        out = refs[-1]
        z = axis_index("head")
        for behind, piece in enumerate(refs[:-1]):
            source = shifted(z, sizes.groups - behind, sizes.groups) if behind else z
            out[source] = piece[rows:, :]

    return call(kernel, shape(sizes.groups, rows + SCALE_ROWS, DK), *arrived, name="swap_keys")


def pack_reads(sizes, values, queries):
    value_rows = sizes.heads * KEY_ROWS
    rows = value_rows + sizes.heads * TOK

    def kernel(values, queries, kept, sent):
        z = axis_index("head")
        core = axis_index("core")
        for ahead in range(sizes.groups):
            target = shifted(z, ahead, sizes.groups)
            for side, out in enumerate((kept, sent)):
                first = (target * 2 + jnp.bitwise_xor(core, side)) * sizes.heads * DK
                pieces = block_columns(values, first * NH, sizes.heads * NH)
                pieces += block_columns(queries, first, sizes.heads)
                for number, piece in enumerate(pieces):
                    out[ahead, number * TOK : (number + 1) * TOK, :] = piece

    return call(
        kernel, [shape(sizes.groups, rows, DK)] * 2, values, queries, name="pack_reads"
    )


def merge_reads(sizes, kept, swapped):
    value_rows = sizes.heads * KEY_ROWS
    query_rows = sizes.heads * TOK

    def kernel(kept, swapped, *outs):
        for ahead in range(sizes.groups):
            for side, source in enumerate((kept, swapped)):
                outs[ahead][side] = source[ahead, :value_rows, :]
                outs[sizes.groups + ahead][side] = source[ahead, value_rows:, :]

    outs = [shape(2, value_rows, DK)] * sizes.groups + [shape(2, query_rows, DK)] * sizes.groups
    merged = call(kernel, outs, kept, swapped, name="merge_reads")
    return merged[: sizes.groups], merged[sizes.groups :]


def gather(sizes, pieces, scratch):
    z = axis_index("head")
    core = axis_index("core")
    for behind, piece in enumerate(pieces):
        source = shifted(z, sizes.groups - behind, sizes.groups) if behind else z
        for side in range(2):
            scratch[jnp.bitwise_xor(core, side) * sizes.groups + source] = piece[side]


def unit_rows(scratch, head, chunk, count):
    first = head * count
    return jnp.concatenate(
        [
            scratch[2 * chunk, first : first + count, :],
            scratch[2 * chunk + 1, first : first + count, :],
        ],
        0,
    )


def key_stage(sizes, arrived, swapped):
    rows = sizes.heads * KEY_ROWS
    units = sizes.units
    groups = sizes.groups

    def kernel(*refs):
        pieces = refs[:groups]
        swapped = refs[groups]
        keys_out, inverse_out, end_out, ratio_out, row_out, step_out, prefix_out = refs[
            groups + 1 : groups + 8
        ]
        totals = refs[groups + 8 : groups + 8 + sizes.heads]
        blocks, scales, every = refs[groups + 8 + sizes.heads :]
        z = axis_index("head")
        core = axis_index("core")
        for behind, piece in enumerate(pieces):
            source = shifted(z, groups - behind, groups) if behind else z
            blocks[core * groups + source] = piece[:rows, :]
            scales[core * groups + source] = piece[2 * rows :, :]
        other = (1 - core) * groups
        for source in range(groups):
            blocks[other + source] = swapped[source, :rows, :]
            scales[other + source] = swapped[source, rows:, :]
        flat = scales[...].reshape(2 * groups * SCALE_ROWS, 4 * TOK)
        picks = []
        for block in range(2):
            extent = (units, 2 * groups * SCALE_ROWS)
            unit = iota(extent, 0)
            row = (unit % groups * 2 + block) * SCALE_ROWS + unit // groups
            pick = iota(extent, 1) == row + core * sizes.heads
            picks.append(dot(pick.astype(BF16), flat))
        by_unit = jnp.concatenate(picks, 1).astype(BF16)
        maps = scale_maps()
        as_rows = dot_nt(by_unit, maps)
        as_columns = dot_nt(maps, by_unit)
        decay_row, segment_row, beta_row = (
            as_rows[:, number * REFL : (number + 1) * REFL] for number in range(3)
        )
        decay_column, segment_column, beta_column = (
            as_columns[number * REFL : (number + 1) * REFL] for number in range(3)
        )
        carried_row = jnp.exp(decay_row) * (segment_row == 0).astype(F32)
        last = REFL - 1
        end_row = jnp.exp(decay_row[:, last:] - decay_row)
        end_row = end_row * (segment_row[:, last:] == segment_row).astype(F32)
        square = (REFL, REFL)
        _, _, _, row_time = place(iota(square, 0))
        _, _, _, column_time = place(iota(square, 1))
        causal = row_time >= column_time
        strict = row_time > column_time
        diagonal = row_time == column_time
        same = (iota((DK, DK), 0) == iota((DK, DK), 1)).astype(F32)
        row_out[0] = beta_row
        row_out[2] = carried_row
        for base in range(0, units, GROUP):
            members = range(base, min(base + GROUP, units))
            keys = [unit_rows(blocks, *sizes.unit(unit), KEY_ROWS) for unit in members]
            grams = [dot_nt(key, key) for key in keys]
            squares = [jnp.where(diagonal, gram, 0.0) for gram in grams]
            norm_rows = [lax.rsqrt(jnp.sum(each, 0, keepdims=True) + EPSILON) for each in squares]
            norm_columns = [
                lax.rsqrt(jnp.sum(each, 1, keepdims=True) + EPSILON) for each in squares
            ]
            lowers = []
            for number, unit in enumerate(members):
                keys_out[unit] = keys[number]
                one = slice(unit, unit + 1)
                linked = causal & (segment_column[:, one] == segment_row[one])
                gap = decay_column[:, one] - decay_row[one]
                ratio = jnp.where(linked, jnp.exp(jnp.minimum(gap, 0.0)), 0.0) * norm_rows[number]
                ratio_out[unit] = read_rows(ratio)
                strengths = beta_column[:, one] * norm_columns[number]
                lowers.append(jnp.where(strict, strengths * ratio * grams[number], 0.0))
            solved = inverses(lowers)
            pairs = [split(each) for each in solved]
            kept_rows = [
                beta_row[unit : unit + 1] * carried_row[unit : unit + 1] * norm
                for unit, norm in zip(members, norm_rows)
            ]
            turned_keys = [key.T for key in keys]
            ends = []
            for number, unit in enumerate(members):
                high, low = pairs[number]
                inverse_out[unit] = jnp.concatenate([high, low], 1)
                row_out[1, unit : unit + 1, :] = kept_rows[number]
                weights = end_row[unit : unit + 1] * norm_rows[number]
                ends.append(
                    product(
                        beside(turned_keys[number].astype(F32) * weights), factor_of(high, low)
                    )
                )
            for number, unit in enumerate(members):
                turned = turned_keys[number]
                end_out[unit] = beside(ends[number] * beta_row[unit : unit + 1])
                every[unit] = carried_row[unit : unit + 1, last:] * same - dot_nt(
                    jnp.concatenate([turned, turned], 1), beside(ends[number] * kept_rows[number])
                )
        prefixes = [same] * sizes.heads
        for chunk in range(groups):
            for head in range(sizes.heads):
                unit = head * groups + chunk
                step = every[unit]
                high, low = split(step)
                step_out[unit] = jnp.concatenate([high, low], 1)
                prefix_out[unit] = prefixes[head]
                if chunk == 0:
                    prefixes[head] = step
                else:
                    prefixes[head] = product(beside(prefixes[head]), factor_of(high, low))
        if sizes.swapped:
            for head in range(sizes.heads):
                every[head] = prefixes[head]
            chip = axis_index("chip")
            for number in range(sizes.heads):
                totals[number][...] = every[jnp.bitwise_xor(chip, number)]
        else:
            for head in range(sizes.heads):
                totals[head][...] = prefixes[head]

    outs = [
        shape(units, REFL, DK),
        shape(units, REFL, 2 * REFL),
        shape(units, DK, 2 * REFL),
        shape(units, CHUNK, REFL, dtype=F32),
        shape(3, units, REFL, dtype=F32),
        shape(units, DK, 2 * DK),
        shape(units, DK, DK, dtype=F32),
    ] + [shape(DK, DK, dtype=F32)] * sizes.heads
    scratch = [
        pltpu.VMEM((2 * groups, rows, DK), BF16),
        pltpu.VMEM((2 * groups, SCALE_ROWS, DK), BF16),
        pltpu.VMEM((units, DK, DK), F32),
    ]
    results = call(
        kernel, outs, *arrived, swapped, scratch=scratch, flops=6_000_000_000, name="key_stage"
    )
    return results[:7], results[7:]


def value_stage(sizes, pieces, ends, steps):
    groups = sizes.groups

    def kernel(*refs):
        pieces = refs[:groups]
        ends, steps, values_out, before_out = refs[groups : groups + 4]
        totals = refs[groups + 4 : groups + 4 + sizes.heads]
        blocks, every = refs[groups + 4 + sizes.heads :]
        gather(sizes, pieces, blocks)
        injects = []
        for unit in range(sizes.units):
            value = unit_rows(blocks, *sizes.unit(unit), KEY_ROWS)
            values_out[unit] = value
            turned = value.T
            injects.append(dot_nt(jnp.concatenate([turned, turned], 1), ends[unit]))
        sums = [jnp.zeros((DV, DK), F32)] * sizes.heads
        for chunk in range(groups):
            for head in range(sizes.heads):
                unit = head * groups + chunk
                before_out[unit] = sums[head]
                if chunk == 0:
                    sums[head] = injects[unit]
                else:
                    step = steps[unit]
                    sums[head] = injects[unit] + product(
                        beside(sums[head]), factor_of(step[:, :DK], step[:, DK:])
                    )
        if sizes.swapped:
            for head in range(sizes.heads):
                every[head] = sums[head]
            chip = axis_index("chip")
            for number in range(sizes.heads):
                totals[number][...] = every[jnp.bitwise_xor(chip, number)]
        else:
            for head in range(sizes.heads):
                totals[head][...] = sums[head]

    outs = [shape(sizes.units, REFL, DV), shape(sizes.units, DV, DK, dtype=F32)]
    outs += [shape(DV, DK, dtype=F32)] * sizes.heads
    scratch = [
        pltpu.VMEM((2 * groups, sizes.heads * KEY_ROWS, DV), BF16),
        pltpu.VMEM((sizes.heads, DV, DK), F32),
    ]
    results = call(
        kernel, outs, *pieces, ends, steps, scratch=scratch, flops=2_000_000_000, name="value_stage"
    )
    return results[0], results[1], results[2:]


def scan_states(sizes, transitions, injects):
    chips = sizes.chips

    def kernel(*refs):
        transitions = refs[:chips]
        injects = refs[chips : 2 * chips]
        outs = refs[2 * chips : 3 * chips]
        step, inject, entry = refs[3 * chips :]
        chip = axis_index("chip")
        for number in range(chips):
            source = jnp.bitwise_xor(chip, number)
            step[source] = transitions[number][...]
            inject[source] = injects[number][...]
        state = jnp.zeros((DV, DK), F32)
        for index in range(chips):
            entry[index] = state
            if index == 0:
                state = inject[index]
            elif index < chips - 1:
                state = product(beside(state), factor(step[index])) + inject[index]
        for number in range(chips):
            outs[number][...] = entry[jnp.bitwise_xor(chip, number)]

    scratch = [pltpu.VMEM((chips, DV, DK), F32)] * 3
    return call(
        kernel,
        [shape(DV, DK, dtype=F32)] * chips,
        *transitions,
        *injects,
        scratch=scratch,
        name="scan_states",
    )


def exchanged(sizes, parts):
    return [parts[0]] + [
        lax.ppermute(part, "chip", [(chip, chip ^ number) for chip in range(sizes.chips)])
        for number, part in enumerate(parts)
        if number
    ]


def entry_states(sizes, transitions, injects):
    if sizes.swapped:
        arrived = exchanged(sizes, transitions), exchanged(sizes, injects)
        return exchanged(sizes, scan_states(sizes, *arrived))
    transition = jnp.stack(transitions)
    inject = jnp.stack(injects)
    forward = [(chip, chip + 1) for chip in range(sizes.chips - 1)]

    def advance(_, entry):
        left = jnp.einsum("hvd,hde->hve", entry, transition, precision=lax.Precision.HIGHEST)
        return lax.ppermute(left + inject, "chip", forward)

    entry = lax.fori_loop(0, sizes.chips - 1, advance, jnp.zeros_like(inject))
    return [entry[head] for head in range(sizes.heads)]


def query_stage(sizes, pieces, values, before, keys, inverses_, ratios, rows, prefixes):
    groups = sizes.groups

    def kernel(*refs):
        pieces = refs[:groups]
        values, before, keys, inverse, ratio, rows, prefix, reader_out, inner_out, blocks = refs[
            groups:
        ]
        gather(sizes, pieces, blocks)
        for base in range(0, sizes.units, GROUP):
            members = range(base, min(base + GROUP, sizes.units))
            queries = [unit_rows(blocks, *sizes.unit(unit), TOK) for unit in members]
            scores = []
            for number, unit in enumerate(members):
                pair = inverse[unit]
                score = dot_nt(queries[number], keys[unit]) * ratio[unit]
                scores.append(product(beside(score), factor_of(pair[:, :REFL], pair[:, REFL:])))
            for number, unit in enumerate(members):
                one = slice(unit, unit + 1)
                inner = dot(beside(scores[number] * rows[0, one, :]), twice(values[unit]))
                carried = read_rows(jnp.broadcast_to(rows[2, one, :], (DK, REFL)).T)
                reader = carried * queries[number].astype(F32) - dot(
                    beside(scores[number] * rows[1, one, :]), twice(keys[unit])
                )
                high, low = split(jnp.concatenate([prefix[unit], before[unit]], 0))
                pair = beside(reader)
                both = dot_nt(pair, jnp.concatenate([high, high], 1)) + dot_nt(pair[:, :DK], low)
                reader_out[unit] = beside(both[:, :DK])
                inner_out[unit] = inner + both[:, DK:]

    outs = [
        shape(sizes.units, CHUNK, 2 * DK),
        shape(sizes.units, CHUNK, DV, dtype=F32),
    ]
    scratch = [pltpu.VMEM((2 * groups, sizes.heads * TOK, DK), BF16)]
    return call(
        kernel,
        outs,
        *pieces,
        values,
        before,
        keys,
        inverses_,
        ratios,
        rows,
        prefixes,
        scratch=scratch,
        flops=3_000_000_000,
        name="query_stage",
    )


def read_states(sizes, states, readers, inners):
    groups = sizes.groups
    half = groups // 2

    def kernel(*refs):
        states = refs[: sizes.heads]
        readers, inners, own, other, entry = refs[sizes.heads :]
        core = axis_index("core")
        chip = axis_index("chip") if sizes.swapped else 0
        for number in range(sizes.heads):
            place_ = jnp.bitwise_xor(chip, number) if sizes.swapped else number
            entry[place_] = states[number][...]
        for head in range(sizes.heads):
            high, low = split(entry[head])
            stack = jnp.concatenate(
                [
                    jnp.concatenate([high, high], 1),
                    jnp.concatenate([low, jnp.zeros_like(low)], 1),
                ],
                0,
            )
            for side, out in enumerate((own, other)):
                first = head * groups + jnp.bitwise_xor(core, side) * half
                pair = readers[pl.ds(first, half)].reshape(half * CHUNK, 2 * DK)
                both = dot_nt(pair, stack)
                inner = inners[pl.ds(first, half)].reshape(half * CHUNK, DV)
                result = inner + both[:, :DV] + both[:, DV:]
                out[:, head * DV : (head + 1) * DV] = result.astype(BF16)

    outs = [shape(half * CHUNK, sizes.heads * DV)] * 2
    scratch = [pltpu.VMEM((sizes.heads, DV, DK), F32)]
    return call(kernel, outs, *states, readers, inners, scratch=scratch, name="read_states")


def join(sizes, own, other):
    width = sizes.heads * DV

    def kernel(own, other, out):
        first = axis_index("core") * width
        out[:, pl.ds(pl.multiple_of(first, width), width)] = own[...]
        out[:, pl.ds(pl.multiple_of(width - first, width), width)] = other[...]

    return call(kernel, shape(own.shape[0], 2 * width), own, other, name="join")


def local(queries, keys, values, betas, log_gates, starts):
    groups = lax.axis_size("head")
    sizes = Sizes(groups, log_gates.shape[1] // groups, lax.axis_size("chip"))
    own_starts = lax.dynamic_slice(starts, (axis_index("head") * TOK,), (TOK,)).reshape(1, TOK)

    def spread(parts):
        return [parts[0]] + [
            lax.ppermute(part, "head", [(z, (z + ahead) % groups) for z in range(groups)])
            for ahead, part in enumerate(parts)
            if ahead
        ]

    def swapped(part):
        return lax.ppermute(part, "core", [(0, 1), (1, 0)])

    arrived = spread(pack_keys(sizes, keys, betas, log_gates, own_starts))
    kept, sent = pack_reads(sizes, values, queries)
    value_parts, query_parts = merge_reads(sizes, kept, swapped(sent))
    value_parts = spread(value_parts)
    query_parts = spread(query_parts)
    other_keys = swapped(swap_keys(sizes, arrived))
    (unit_keys, inverse, ends, ratios, rows, steps, prefixes), transitions = key_stage(
        sizes, arrived, other_keys
    )
    unit_values, before, injects = value_stage(sizes, value_parts, ends, steps)
    states = entry_states(sizes, transitions, injects)
    readers, inners = query_stage(
        sizes, query_parts, unit_values, before, unit_keys, inverse, ratios, rows, prefixes
    )
    own, other = read_states(sizes, states, readers, inners)
    return join(sizes, own, swapped(other))


def solution(mesh):
    devices = mesh.devices
    rows = P(("chip", "core", "head"), None)
    return jax.shard_map(
        local,
        mesh=Mesh(
            devices.reshape(devices.shape[0] // 2, 2, devices.shape[1]), ("chip", "core", "head")
        ),
        in_specs=(rows, rows, rows, rows, rows, P(("chip", "core"))),
        out_specs=P(("chip", "core"), "head"),
        check_vma=False,
    )
```

```python
import jax
import jax.numpy as jnp
from jax import lax
from jax.experimental import pallas as pl
from jax.experimental.pallas import tpu as pltpu
from jax.sharding import Mesh
from jax.sharding import PartitionSpec as P

DK = 128
DV = 128
NH = 2
TOK = 32
CHUNK = 2 * TOK
REFL = CHUNK * NH
GROUP = 8
EPSILON = 1e-06

KEY_ROWS = NH * TOK
SCALE_ROWS = 16

BF16 = jnp.bfloat16
F32 = jnp.float32
NT = (((1,), (1,)), ((), ()))


def iota(shape, axis):
    return lax.broadcasted_iota(jnp.int32, shape, axis)


def dot(left, right):
    return jnp.dot(left, right, preferred_element_type=F32)


def dot_nt(left, right):
    return lax.dot_general(left, right, NT, preferred_element_type=F32)


def split(value):
    high = value.astype(BF16)
    low = (value - high.astype(F32)).astype(BF16)
    return high, low


def beside(value):
    return jnp.concatenate(split(value), 1)


def twice(value):
    return jnp.concatenate([value, value], 0)


def factor(value):
    return factor_of(*split(value))


def factor_of(high, low):
    return jnp.concatenate(
        [jnp.concatenate([high, low], 1), jnp.concatenate([high, jnp.zeros_like(low)], 1)], 0
    )


def product(left_pair, right_factor):
    both = dot(left_pair, right_factor)
    half = both.shape[1] // 2
    return both[:, :half] + both[:, half:]


def place(index):
    block = index // (NH * TOK)
    step = (index // TOK) % NH
    token = index % TOK
    return block, step, token, (block * TOK + token) * NH + step


def scale_maps():
    shape = (REFL, 8 * TOK)
    block, step, token, _ = place(iota(shape, 0))
    column = iota(shape, 1)
    source_block = column // (4 * TOK)
    kind = (column // TOK) % 4
    source = source_block * TOK + column % TOK
    now = block * TOK + token
    decay = (kind == NH) & (source <= now)
    segment = (kind == NH + 1) & (source <= now)
    beta = (kind == step) & (source == now)
    return jnp.concatenate([part.astype(F32) for part in (decay, segment, beta)], 0).astype(BF16)


def piece_rows(size):
    if size == TOK:
        return [slice(NH * TOK, 2 * NH * TOK)]
    return [
        slice(start, start + size)
        for part in range(2 * NH)
        for start in range(part * TOK + size, (part + 1) * TOK, 2 * size)
    ]


def taken(value, slices):
    return jnp.concatenate([value[each] for each in slices], 0) if len(slices) > 1 else value[slices[0]]


def put(base, rows, slices):
    pieces = []
    at = 0
    done = 0
    for each in slices:
        if each.start > at:
            pieces.append(base[at : each.start])
        size = each.stop - each.start
        pieces.append(base[each] + rows[done : done + size])
        done += size
        at = each.stop
    if at < REFL:
        pieces.append(base[at:])
    return jnp.concatenate(pieces, 0)


def inverses(lowers):
    small = 8
    count = len(lowers)
    lane = iota((small, REFL), 1)
    group_of = (lane // (NH * TOK)) * (TOK // small) + (lane % TOK) // small
    groups = [(block, piece) for block in range(2) for piece in range(TOK // small)]

    def start_row(block, step, piece):
        return block * NH * TOK + step * TOK + piece * small

    folded = []
    for lower in lowers:
        for step in range(NH):
            rows = jnp.zeros((small, REFL), F32)
            for number, (block, piece) in enumerate(groups):
                first = start_row(block, step, piece)
                rows = jnp.where(group_of == number, lower[first : first + small], rows)
            folded.append(rows)
    height = NH * small
    lower_fold = jnp.concatenate(folded, 0)
    wide = iota((count * height, REFL), 1)
    high = iota((count * height, REFL), 0) % height
    inverse = ((wide // TOK) % NH == high // small) & (wide % small == high % small)
    inverse = inverse.astype(F32).reshape(count, height, REFL)
    for token in range(small):
        for step in range(NH):
            if token == small - 1 and step == NH - 1:
                continue
            source = (wide // (NH * TOK)) * (NH * TOK) + step * TOK + (wide % TOK) // small * small + token
            column = jnp.take_along_axis(lower_fold, source, axis=1, mode="promise_in_bounds")
            row = step * small + token
            inverse = inverse - column.reshape(count, height, REFL) * inverse[:, row : row + 1, :]
    results = []
    for number in range(count):
        pieces = []
        for block in range(2):
            for step in range(NH):
                rows = inverse[number, step * small : (step + 1) * small]
                for piece in range(TOK // small):
                    mine = group_of == block * (TOK // small) + piece
                    pieces.append(jnp.where(mine, rows, 0.0))
        results.append(jnp.concatenate(pieces, 0))
    size = small
    zero = jnp.zeros((REFL, REFL), F32)
    while size < CHUNK:
        slices = piece_rows(size)
        row_block, _, row_token, _ = place(iota((REFL, REFL), 0))
        column_block, _, column_token, _ = place(iota((REFL, REFL), 1))
        row_piece = (row_block * TOK + row_token) // size
        column_piece = (column_block * TOK + column_token) // size
        linked = taken(row_piece, slices) == taken(column_piece, slices) + 1
        crossings = [
            product(beside(jnp.where(linked, taken(lower, slices), 0.0)), factor(result))
            for lower, result in zip(lowers, results)
        ]
        changes = [
            product(beside(taken(result, slices)), factor(put(zero, crossing, slices)))
            for crossing, result in zip(crossings, results)
        ]
        results = [put(result, -change, slices) for change, result in zip(changes, results)]
        size *= 2
    return results


def read_rows(value):
    return jnp.concatenate(
        [
            value[(NH - 1) * TOK : NH * TOK],
            value[(2 * NH - 1) * TOK : 2 * NH * TOK],
        ],
        0,
    )


def call(kernel, outs, *args, scratch=(), after=(), name=None):
    count = len(args)

    def body(*refs):
        kernel(*refs[:count], *refs[count + len(after) :])

    specs = [pl.BlockSpec(memory_space=pltpu.VMEM)] * count
    specs += [pl.BlockSpec(memory_space=pl.ANY)] * len(after)
    return pl.pallas_call(
        body,
        out_shape=outs,
        in_specs=specs,
        scratch_shapes=scratch,
        compiler_params=pltpu.CompilerParams(vmem_limit_bytes=24 * 2**20),
        cost_estimate=pl.CostEstimate(flops=0, bytes_accessed=0, transcendentals=0),
        name=name,
    )(*args, *after)


def shape(*sizes, dtype=BF16):
    return jax.ShapeDtypeStruct(sizes, dtype)


def axis_index(axis):
    return lax.axis_index(axis).astype(jnp.int32)


class Sizes:
    def __init__(self, groups, group_heads, chips):
        self.groups = groups
        self.group_heads = group_heads
        self.heads = group_heads // 2
        self.chips = chips
        self.units = self.heads * groups
        self.swapped = chips == self.heads and chips & (chips - 1) == 0

    def unit(self, number):
        return number // self.groups, number % self.groups


def shifted(index, by, size):
    moved = index + by
    return jnp.where(moved >= size, moved - size, moved)


def block_columns(source, first, count):
    return [
        source[:, pl.ds(pl.multiple_of(first + number * DK, DK), DK)] for number in range(count)
    ]


def pack_keys(sizes, keys, betas, log_gates, starts):
    rows = sizes.heads * KEY_ROWS
    count = sizes.heads * NH

    def kernel(keys, betas, log_gates, starts, kept, sent):
        z = axis_index("head")
        core = axis_index("core")
        heads = log_gates.shape[1]
        pieces = []
        for step in range(NH):
            extent = (heads, heads * NH)
            pick = iota(extent, 1) == iota(extent, 0) * NH + step
            pieces.append(dot_nt(pick.astype(BF16), betas[...]))
        same = iota((heads, heads), 0) == iota((heads, heads), 1)
        pieces.append(dot_nt(same.astype(BF16), log_gates[...]))
        pieces.append(jnp.broadcast_to(starts[...].astype(F32), (heads, TOK)))
        scales = jnp.concatenate(pieces, 1).astype(BF16)
        for ahead in range(sizes.groups):
            target = shifted(z, ahead, sizes.groups)
            extent = (SCALE_ROWS, heads)
            pick = (iota(extent, 1) == target * sizes.group_heads + iota(extent, 0)) & (
                iota(extent, 0) < sizes.group_heads
            )
            scale = dot(pick.astype(BF16), scales).astype(BF16)
            for side, out in enumerate((kept, sent)):
                owner = jnp.bitwise_xor(core, side)
                first = ((target * 2 + owner) * sizes.heads) * NH * DK
                for number, piece in enumerate(block_columns(keys, first, count)):
                    out[ahead, number * TOK : (number + 1) * TOK, :] = piece
                out[ahead, rows:, :] = scale

    outs = [shape(sizes.groups, rows + SCALE_ROWS, DK)] * 2
    return call(kernel, outs, keys, betas, log_gates, starts, name="pack_keys")


def pack_reads(sizes, values, queries, after):
    value_rows = sizes.heads * KEY_ROWS
    rows = value_rows + sizes.heads * TOK

    def kernel(values, queries, kept, sent):
        z = axis_index("head")
        core = axis_index("core")
        for ahead in range(sizes.groups):
            target = shifted(z, ahead, sizes.groups)
            for side, out in enumerate((kept, sent)):
                first = (target * 2 + jnp.bitwise_xor(core, side)) * sizes.heads * DK
                pieces = block_columns(values, first * NH, sizes.heads * NH)
                pieces += block_columns(queries, first, sizes.heads)
                for number, piece in enumerate(pieces):
                    out[ahead, number * TOK : (number + 1) * TOK, :] = piece

    return call(
        kernel,
        [shape(sizes.groups, rows, DK)] * 2,
        values,
        queries,
        after=after,
        name="pack_reads",
    )


def merge(sizes, kept, swapped, name):
    def kernel(kept, swapped, *outs):
        for ahead in range(sizes.groups):
            for side, source in enumerate((kept, swapped)):
                outs[ahead][side] = source[ahead]

    outs = [shape(2, *kept.shape[1:])] * sizes.groups
    return call(kernel, outs, kept, swapped, name=name)


def gather(sizes, pieces, first, count, scratch):
    z = axis_index("head")
    core = axis_index("core")
    for behind, piece in enumerate(pieces):
        source = shifted(z, sizes.groups - behind, sizes.groups) if behind else z
        for side in range(2):
            scratch[jnp.bitwise_xor(core, side) * sizes.groups + source] = piece[
                side, first : first + count, :
            ]


def unit_rows(scratch, head, chunk, count):
    first = head * count
    return jnp.concatenate(
        [
            scratch[2 * chunk, first : first + count, :],
            scratch[2 * chunk + 1, first : first + count, :],
        ],
        0,
    )


def key_stage(sizes, pieces):
    rows = sizes.heads * KEY_ROWS
    units = sizes.units
    groups = sizes.groups

    def kernel(*refs):
        pieces = refs[:groups]
        keys_out, inverse_out, end_out, ratio_out, row_out, step_out, prefix_out = refs[
            groups : groups + 7
        ]
        totals = refs[groups + 7 : groups + 7 + sizes.heads]
        blocks, scales, every = refs[groups + 7 + sizes.heads :]
        core = axis_index("core")
        gather(sizes, pieces, 0, rows, blocks)
        gather(sizes, pieces, rows, SCALE_ROWS, scales)
        flat = scales[...].reshape(2 * groups * SCALE_ROWS, 4 * TOK)
        picks = []
        for block in range(2):
            extent = (units, 2 * groups * SCALE_ROWS)
            unit = iota(extent, 0)
            row = (unit % groups * 2 + block) * SCALE_ROWS + unit // groups
            pick = iota(extent, 1) == row + core * sizes.heads
            picks.append(dot(pick.astype(BF16), flat))
        by_unit = jnp.concatenate(picks, 1).astype(BF16)
        maps = scale_maps()
        as_rows = dot_nt(by_unit, maps)
        as_columns = dot_nt(maps, by_unit)
        decay_row, segment_row, beta_row = (
            as_rows[:, number * REFL : (number + 1) * REFL] for number in range(3)
        )
        decay_column, segment_column, beta_column = (
            as_columns[number * REFL : (number + 1) * REFL] for number in range(3)
        )
        carried_row = jnp.exp(decay_row) * (segment_row == 0).astype(F32)
        last = REFL - 1
        end_row = jnp.exp(decay_row[:, last:] - decay_row)
        end_row = end_row * (segment_row[:, last:] == segment_row).astype(F32)
        square = (REFL, REFL)
        _, _, _, row_time = place(iota(square, 0))
        _, _, _, column_time = place(iota(square, 1))
        causal = row_time >= column_time
        strict = row_time > column_time
        diagonal = row_time == column_time
        same = (iota((DK, DK), 0) == iota((DK, DK), 1)).astype(F32)
        row_out[0] = beta_row
        row_out[2] = carried_row
        for base in range(0, units, GROUP):
            members = range(base, min(base + GROUP, units))
            keys = [unit_rows(blocks, *sizes.unit(unit), KEY_ROWS) for unit in members]
            grams = [dot_nt(key, key) for key in keys]
            squares = [jnp.where(diagonal, gram, 0.0) for gram in grams]
            norm_rows = [lax.rsqrt(jnp.sum(each, 0, keepdims=True) + EPSILON) for each in squares]
            norm_columns = [
                lax.rsqrt(jnp.sum(each, 1, keepdims=True) + EPSILON) for each in squares
            ]
            lowers = []
            for number, unit in enumerate(members):
                keys_out[unit] = keys[number]
                one = slice(unit, unit + 1)
                linked = causal & (segment_column[:, one] == segment_row[one])
                gap = decay_column[:, one] - decay_row[one]
                ratio = jnp.where(linked, jnp.exp(jnp.minimum(gap, 0.0)), 0.0) * norm_rows[number]
                ratio_out[unit] = read_rows(ratio)
                strengths = beta_column[:, one] * norm_columns[number]
                lowers.append(jnp.where(strict, strengths * ratio * grams[number], 0.0))
            solved = inverses(lowers)
            pairs = [split(each) for each in solved]
            kept_rows = [
                beta_row[unit : unit + 1] * carried_row[unit : unit + 1] * norm
                for unit, norm in zip(members, norm_rows)
            ]
            turned_keys = [key.T for key in keys]
            ends = []
            for number, unit in enumerate(members):
                high, low = pairs[number]
                inverse_out[unit] = jnp.concatenate([high, low], 1)
                row_out[1, unit : unit + 1, :] = kept_rows[number]
                weights = end_row[unit : unit + 1] * norm_rows[number]
                ends.append(
                    product(
                        beside(turned_keys[number].astype(F32) * weights), factor_of(high, low)
                    )
                )
            for number, unit in enumerate(members):
                turned = turned_keys[number]
                end_out[unit] = beside(ends[number] * beta_row[unit : unit + 1])
                every[unit] = carried_row[unit : unit + 1, last:] * same - dot_nt(
                    jnp.concatenate([turned, turned], 1), beside(ends[number] * kept_rows[number])
                )
        prefixes = [same] * sizes.heads
        for chunk in range(groups):
            for head in range(sizes.heads):
                unit = head * groups + chunk
                step = every[unit]
                high, low = split(step)
                step_out[unit] = jnp.concatenate([high, low], 1)
                prefix_out[unit] = prefixes[head]
                if chunk == 0:
                    prefixes[head] = step
                else:
                    prefixes[head] = product(beside(prefixes[head]), factor_of(high, low))
        if sizes.swapped:
            for head in range(sizes.heads):
                every[head] = prefixes[head]
            chip = axis_index("chip")
            for number in range(sizes.heads):
                totals[number][...] = every[jnp.bitwise_xor(chip, number)]
        else:
            for head in range(sizes.heads):
                totals[head][...] = prefixes[head]

    outs = [
        shape(units, REFL, DK),
        shape(units, REFL, 2 * REFL),
        shape(units, DK, 2 * REFL),
        shape(units, CHUNK, REFL, dtype=F32),
        shape(3, units, REFL, dtype=F32),
        shape(units, DK, 2 * DK),
        shape(units, DK, DK, dtype=F32),
    ] + [shape(DK, DK, dtype=F32)] * sizes.heads
    scratch = [
        pltpu.VMEM((2 * groups, rows, DK), BF16),
        pltpu.VMEM((2 * groups, SCALE_ROWS, DK), BF16),
        pltpu.VMEM((units, DK, DK), F32),
    ]
    results = call(
        kernel, outs, *pieces, scratch=scratch, name="key_stage"
    )
    return results[:7], results[7:]


def value_stage(sizes, pieces, ends, steps):
    groups = sizes.groups

    def kernel(*refs):
        pieces = refs[:groups]
        ends, steps, values_out, before_out = refs[groups : groups + 4]
        totals = refs[groups + 4 : groups + 4 + sizes.heads]
        blocks, every = refs[groups + 4 + sizes.heads :]
        gather(sizes, pieces, 0, sizes.heads * KEY_ROWS, blocks)
        injects = []
        for unit in range(sizes.units):
            value = unit_rows(blocks, *sizes.unit(unit), KEY_ROWS)
            values_out[unit] = value
            turned = value.T
            injects.append(dot_nt(jnp.concatenate([turned, turned], 1), ends[unit]))
        sums = [jnp.zeros((DV, DK), F32)] * sizes.heads
        for chunk in range(groups):
            for head in range(sizes.heads):
                unit = head * groups + chunk
                before_out[unit] = sums[head]
                if chunk == 0:
                    sums[head] = injects[unit]
                else:
                    step = steps[unit]
                    sums[head] = injects[unit] + product(
                        beside(sums[head]), factor_of(step[:, :DK], step[:, DK:])
                    )
        if sizes.swapped:
            for head in range(sizes.heads):
                every[head] = sums[head]
            chip = axis_index("chip")
            for number in range(sizes.heads):
                totals[number][...] = every[jnp.bitwise_xor(chip, number)]
        else:
            for head in range(sizes.heads):
                totals[head][...] = sums[head]

    outs = [shape(sizes.units, REFL, DV), shape(sizes.units, DV, DK, dtype=F32)]
    outs += [shape(DV, DK, dtype=F32)] * sizes.heads
    scratch = [
        pltpu.VMEM((2 * groups, sizes.heads * KEY_ROWS, DV), BF16),
        pltpu.VMEM((sizes.heads, DV, DK), F32),
    ]
    results = call(
        kernel, outs, *pieces, ends, steps, scratch=scratch, name="value_stage"
    )
    return results[0], results[1], results[2:]


def scan_states(sizes, transitions, injects):
    chips = sizes.chips

    def kernel(*refs):
        transitions = refs[:chips]
        injects = refs[chips : 2 * chips]
        outs = refs[2 * chips : 3 * chips]
        step, inject, entry = refs[3 * chips :]
        chip = axis_index("chip")
        for number in range(chips):
            source = jnp.bitwise_xor(chip, number)
            step[source] = transitions[number][...]
            inject[source] = injects[number][...]
        state = jnp.zeros((DV, DK), F32)
        for index in range(chips):
            entry[index] = state
            if index == 0:
                state = inject[index]
            elif index < chips - 1:
                state = product(beside(state), factor(step[index])) + inject[index]
        for number in range(chips):
            outs[number][...] = entry[jnp.bitwise_xor(chip, number)]

    scratch = [pltpu.VMEM((chips, DV, DK), F32)] * 3
    return call(
        kernel,
        [shape(DV, DK, dtype=F32)] * chips,
        *transitions,
        *injects,
        scratch=scratch,
        name="scan_states",
    )


def exchanged(sizes, parts):
    return [parts[0]] + [
        lax.ppermute(part, "chip", [(chip, chip ^ number) for chip in range(sizes.chips)])
        for number, part in enumerate(parts)
        if number
    ]


def entry_states(sizes, transitions, injects):
    if sizes.swapped:
        arrived = exchanged(sizes, transitions), exchanged(sizes, injects)
        return exchanged(sizes, scan_states(sizes, *arrived))
    transition = jnp.stack(transitions)
    inject = jnp.stack(injects)
    forward = [(chip, chip + 1) for chip in range(sizes.chips - 1)]

    def advance(_, entry):
        left = jnp.einsum("hvd,hde->hve", entry, transition, precision=lax.Precision.HIGHEST)
        return lax.ppermute(left + inject, "chip", forward)

    entry = lax.fori_loop(0, sizes.chips - 1, advance, jnp.zeros_like(inject))
    return [entry[head] for head in range(sizes.heads)]


def query_stage(sizes, pieces, values, before, keys, inverses_, ratios, rows, prefixes):
    groups = sizes.groups

    def kernel(*refs):
        pieces = refs[:groups]
        values, before, keys, inverse, ratio, rows, prefix, reader_out, inner_out, blocks = refs[
            groups:
        ]
        gather(sizes, pieces, sizes.heads * KEY_ROWS, sizes.heads * TOK, blocks)
        for base in range(0, sizes.units, GROUP):
            members = range(base, min(base + GROUP, sizes.units))
            queries = [unit_rows(blocks, *sizes.unit(unit), TOK) for unit in members]
            scores = []
            for number, unit in enumerate(members):
                pair = inverse[unit]
                score = dot_nt(queries[number], keys[unit]) * ratio[unit]
                scores.append(product(beside(score), factor_of(pair[:, :REFL], pair[:, REFL:])))
            for number, unit in enumerate(members):
                one = slice(unit, unit + 1)
                inner = dot(beside(scores[number] * rows[0, one, :]), twice(values[unit]))
                carried = read_rows(jnp.broadcast_to(rows[2, one, :], (DK, REFL)).T)
                reader = carried * queries[number].astype(F32) - dot(
                    beside(scores[number] * rows[1, one, :]), twice(keys[unit])
                )
                high, low = split(jnp.concatenate([prefix[unit], before[unit]], 0))
                pair = beside(reader)
                both = dot_nt(pair, jnp.concatenate([high, high], 1)) + dot_nt(pair[:, :DK], low)
                reader_out[unit] = beside(both[:, :DK])
                inner_out[unit] = inner + both[:, DK:]

    outs = [
        shape(sizes.units, CHUNK, 2 * DK),
        shape(sizes.units, CHUNK, DV, dtype=F32),
    ]
    scratch = [pltpu.VMEM((2 * groups, sizes.heads * TOK, DK), BF16)]
    return call(
        kernel,
        outs,
        *pieces,
        values,
        before,
        keys,
        inverses_,
        ratios,
        rows,
        prefixes,
        scratch=scratch,
        name="query_stage",
    )


def read_states(sizes, states, readers, inners):
    groups = sizes.groups
    half = groups // 2

    def kernel(*refs):
        states = refs[: sizes.heads]
        readers, inners, own, other, entry = refs[sizes.heads :]
        core = axis_index("core")
        chip = axis_index("chip") if sizes.swapped else 0
        for number in range(sizes.heads):
            place_ = jnp.bitwise_xor(chip, number) if sizes.swapped else number
            entry[place_] = states[number][...]
        for head in range(sizes.heads):
            high, low = split(entry[head])
            stack = jnp.concatenate(
                [
                    jnp.concatenate([high, high], 1),
                    jnp.concatenate([low, jnp.zeros_like(low)], 1),
                ],
                0,
            )
            for side, out in enumerate((own, other)):
                first = head * groups + jnp.bitwise_xor(core, side) * half
                pair = readers[pl.ds(first, half)].reshape(half * CHUNK, 2 * DK)
                both = dot_nt(pair, stack)
                inner = inners[pl.ds(first, half)].reshape(half * CHUNK, DV)
                result = inner + both[:, :DV] + both[:, DV:]
                out[:, head * DV : (head + 1) * DV] = result.astype(BF16)

    outs = [shape(half * CHUNK, sizes.heads * DV)] * 2
    scratch = [pltpu.VMEM((sizes.heads, DV, DK), F32)]
    return call(kernel, outs, *states, readers, inners, scratch=scratch, name="read_states")


def join(sizes, own, other):
    width = sizes.heads * DV

    def kernel(own, other, out):
        first = axis_index("core") * width
        out[:, pl.ds(pl.multiple_of(first, width), width)] = own[...]
        out[:, pl.ds(pl.multiple_of(width - first, width), width)] = other[...]

    return call(kernel, shape(own.shape[0], 2 * width), own, other, name="join")


def local(queries, keys, values, betas, log_gates, starts):
    groups = lax.axis_size("head")
    sizes = Sizes(groups, log_gates.shape[1] // groups, lax.axis_size("chip"))
    own_starts = lax.dynamic_slice(starts, (axis_index("head") * TOK,), (TOK,)).reshape(1, TOK)

    def spread(parts):
        return [parts[0]] + [
            lax.ppermute(part, "head", [(z, (z + ahead) % groups) for z in range(groups)])
            for ahead, part in enumerate(parts)
            if ahead
        ]

    def swapped(part):
        return lax.ppermute(part, "core", [(0, 1), (1, 0)])

    kept_keys, sent_keys = pack_keys(sizes, keys, betas, log_gates, own_starts)
    key_parts = spread(merge(sizes, kept_keys, swapped(sent_keys), "merge_keys"))
    kept, sent = pack_reads(sizes, values, queries, after=(kept_keys,))
    reads = spread(merge(sizes, kept, swapped(sent), "merge_reads"))
    (unit_keys, inverse, ends, ratios, rows, steps, prefixes), transitions = key_stage(
        sizes, key_parts
    )
    unit_values, before, injects = value_stage(sizes, reads, ends, steps)
    states = entry_states(sizes, transitions, injects)
    readers, inners = query_stage(
        sizes, reads, unit_values, before, unit_keys, inverse, ratios, rows, prefixes
    )
    own, other = read_states(sizes, states, readers, inners)
    return join(sizes, own, swapped(other))


def solution(mesh):
    devices = mesh.devices
    rows = P(("chip", "core", "head"), None)
    return jax.shard_map(
        local,
        mesh=Mesh(
            devices.reshape(devices.shape[0] // 2, 2, devices.shape[1]), ("chip", "core", "head")
        ),
        in_specs=(rows, rows, rows, rows, rows, P(("chip", "core"))),
        out_specs=P(("chip", "core"), "head"),
        check_vma=False,
    )
```

```python
import jax
import jax.numpy as jnp
from jax import lax
from jax.experimental import pallas as pl
from jax.experimental.pallas import tpu as pltpu
from jax.sharding import Mesh
from jax.sharding import PartitionSpec as P

DK = 128
DV = 128
NH = 2
TOK = 32
CHUNK = 2 * TOK
REFL = CHUNK * NH
GROUP = 8
EPSILON = 1e-06

KEY_ROWS = NH * TOK
SCALE_ROWS = 16

BF16 = jnp.bfloat16
F32 = jnp.float32
NT = (((1,), (1,)), ((), ()))


def iota(shape, axis):
    return lax.broadcasted_iota(jnp.int32, shape, axis)


def dot(left, right):
    return jnp.dot(left, right, preferred_element_type=F32)


def dot_nt(left, right):
    return lax.dot_general(left, right, NT, preferred_element_type=F32)


def split(value):
    high = value.astype(BF16)
    low = (value - high.astype(F32)).astype(BF16)
    return high, low


def beside(value):
    return jnp.concatenate(split(value), 1)


def twice(value):
    return jnp.concatenate([value, value], 0)


def factor(value):
    return factor_of(*split(value))


def factor_of(high, low):
    return jnp.concatenate(
        [jnp.concatenate([high, low], 1), jnp.concatenate([high, jnp.zeros_like(low)], 1)], 0
    )


def product(left_pair, right_factor):
    both = dot(left_pair, right_factor)
    half = both.shape[1] // 2
    return both[:, :half] + both[:, half:]


def place(index):
    block = index // (NH * TOK)
    step = (index // TOK) % NH
    token = index % TOK
    return block, step, token, (block * TOK + token) * NH + step


def scale_maps():
    shape = (REFL, 8 * TOK)
    block, step, token, _ = place(iota(shape, 0))
    column = iota(shape, 1)
    source_block = column // (4 * TOK)
    kind = (column // TOK) % 4
    source = source_block * TOK + column % TOK
    now = block * TOK + token
    decay = (kind == NH) & (source <= now)
    segment = (kind == NH + 1) & (source <= now)
    beta = (kind == step) & (source == now)
    return jnp.concatenate([part.astype(F32) for part in (decay, segment, beta)], 0).astype(BF16)


def piece_rows(size):
    if size == TOK:
        return [slice(NH * TOK, 2 * NH * TOK)]
    return [
        slice(start, start + size)
        for part in range(2 * NH)
        for start in range(part * TOK + size, (part + 1) * TOK, 2 * size)
    ]


def taken(value, slices):
    return jnp.concatenate([value[each] for each in slices], 0) if len(slices) > 1 else value[slices[0]]


def put(base, rows, slices):
    pieces = []
    at = 0
    done = 0
    for each in slices:
        if each.start > at:
            pieces.append(base[at : each.start])
        size = each.stop - each.start
        pieces.append(base[each] + rows[done : done + size])
        done += size
        at = each.stop
    if at < REFL:
        pieces.append(base[at:])
    return jnp.concatenate(pieces, 0)


def inverses(lowers):
    small = 8
    count = len(lowers)
    lane = iota((small, REFL), 1)
    group_of = (lane // (NH * TOK)) * (TOK // small) + (lane % TOK) // small
    groups = [(block, piece) for block in range(2) for piece in range(TOK // small)]

    def start_row(block, step, piece):
        return block * NH * TOK + step * TOK + piece * small

    folded = []
    for lower in lowers:
        for step in range(NH):
            rows = jnp.zeros((small, REFL), F32)
            for number, (block, piece) in enumerate(groups):
                first = start_row(block, step, piece)
                rows = jnp.where(group_of == number, lower[first : first + small], rows)
            folded.append(rows)
    height = NH * small
    lower_fold = jnp.concatenate(folded, 0)
    wide = iota((count * height, REFL), 1)
    high = iota((count * height, REFL), 0) % height
    inverse = ((wide // TOK) % NH == high // small) & (wide % small == high % small)
    inverse = inverse.astype(F32).reshape(count, height, REFL)
    for token in range(small):
        for step in range(NH):
            if token == small - 1 and step == NH - 1:
                continue
            source = (wide // (NH * TOK)) * (NH * TOK) + step * TOK + (wide % TOK) // small * small + token
            column = jnp.take_along_axis(lower_fold, source, axis=1, mode="promise_in_bounds")
            row = step * small + token
            inverse = inverse - column.reshape(count, height, REFL) * inverse[:, row : row + 1, :]
    results = []
    for number in range(count):
        pieces = []
        for block in range(2):
            for step in range(NH):
                rows = inverse[number, step * small : (step + 1) * small]
                for piece in range(TOK // small):
                    mine = group_of == block * (TOK // small) + piece
                    pieces.append(jnp.where(mine, rows, 0.0))
        results.append(jnp.concatenate(pieces, 0))
    size = small
    zero = jnp.zeros((REFL, REFL), F32)
    while size < CHUNK:
        slices = piece_rows(size)
        row_block, _, row_token, _ = place(iota((REFL, REFL), 0))
        column_block, _, column_token, _ = place(iota((REFL, REFL), 1))
        row_piece = (row_block * TOK + row_token) // size
        column_piece = (column_block * TOK + column_token) // size
        linked = taken(row_piece, slices) == taken(column_piece, slices) + 1
        crossings = [
            product(beside(jnp.where(linked, taken(lower, slices), 0.0)), factor(result))
            for lower, result in zip(lowers, results)
        ]
        changes = [
            product(beside(taken(result, slices)), factor(put(zero, crossing, slices)))
            for crossing, result in zip(crossings, results)
        ]
        results = [put(result, -change, slices) for change, result in zip(changes, results)]
        size *= 2
    return results


def read_rows(value):
    return jnp.concatenate(
        [
            value[(NH - 1) * TOK : NH * TOK],
            value[(2 * NH - 1) * TOK : 2 * NH * TOK],
        ],
        0,
    )


def call(kernel, outs, *args, scratch=(), after=(), name=None):
    count = len(args)

    def body(*refs):
        kernel(*refs[:count], *refs[count + len(after) :])

    specs = [pl.BlockSpec(memory_space=pltpu.VMEM)] * count
    specs += [pl.BlockSpec(memory_space=pl.ANY)] * len(after)
    return pl.pallas_call(
        body,
        out_shape=outs,
        in_specs=specs,
        scratch_shapes=scratch,
        compiler_params=pltpu.CompilerParams(vmem_limit_bytes=24 * 2**20),
        cost_estimate=pl.CostEstimate(flops=0, bytes_accessed=0, transcendentals=0),
        name=name,
    )(*args, *after)


def shape(*sizes, dtype=BF16):
    return jax.ShapeDtypeStruct(sizes, dtype)


def axis_index(axis):
    return lax.axis_index(axis).astype(jnp.int32)


class Sizes:
    def __init__(self, groups, group_heads, chips):
        self.groups = groups
        self.group_heads = group_heads
        self.heads = group_heads // 2
        self.chips = chips
        self.units = self.heads * groups
        self.swapped = chips == self.heads and chips & (chips - 1) == 0

    def unit(self, number):
        return number // self.groups, number % self.groups


def shifted(index, by, size):
    moved = index + by
    return jnp.where(moved >= size, moved - size, moved)


def block_columns(source, first, count):
    return [
        source[:, pl.ds(pl.multiple_of(first + number * DK, DK), DK)] for number in range(count)
    ]


def pack_keys(sizes, keys, betas, log_gates, starts):
    rows = sizes.heads * KEY_ROWS
    count = sizes.heads * NH

    def kernel(keys, betas, log_gates, starts, kept, sent):
        z = axis_index("head")
        core = axis_index("core")
        heads = log_gates.shape[1]
        pieces = []
        for step in range(NH):
            extent = (heads, heads * NH)
            pick = iota(extent, 1) == iota(extent, 0) * NH + step
            pieces.append(dot_nt(pick.astype(BF16), betas[...]))
        same = iota((heads, heads), 0) == iota((heads, heads), 1)
        pieces.append(dot_nt(same.astype(BF16), log_gates[...]))
        pieces.append(jnp.broadcast_to(starts[...].astype(F32), (heads, TOK)))
        scales = jnp.concatenate(pieces, 1).astype(BF16)
        for ahead in range(sizes.groups):
            target = shifted(z, ahead, sizes.groups)
            extent = (SCALE_ROWS, heads)
            pick = (iota(extent, 1) == target * sizes.group_heads + iota(extent, 0)) & (
                iota(extent, 0) < sizes.group_heads
            )
            scale = dot(pick.astype(BF16), scales).astype(BF16)
            for side, out in enumerate((kept, sent)):
                owner = jnp.bitwise_xor(core, side)
                first = ((target * 2 + owner) * sizes.heads) * NH * DK
                for number, piece in enumerate(block_columns(keys, first, count)):
                    out[ahead, number * TOK : (number + 1) * TOK, :] = piece
                out[ahead, rows:, :] = scale

    outs = [shape(sizes.groups, rows + SCALE_ROWS, DK)] * 2
    return call(kernel, outs, keys, betas, log_gates, starts, name="pack_keys")


def pack_reads(sizes, values, queries, after):
    value_rows = sizes.heads * KEY_ROWS
    rows = value_rows + sizes.heads * TOK

    def kernel(values, queries, kept, sent):
        z = axis_index("head")
        core = axis_index("core")
        for ahead in range(sizes.groups):
            target = shifted(z, ahead, sizes.groups)
            for side, out in enumerate((kept, sent)):
                first = (target * 2 + jnp.bitwise_xor(core, side)) * sizes.heads * DK
                pieces = block_columns(values, first * NH, sizes.heads * NH)
                pieces += block_columns(queries, first, sizes.heads)
                for number, piece in enumerate(pieces):
                    out[ahead, number * TOK : (number + 1) * TOK, :] = piece

    return call(
        kernel,
        [shape(sizes.groups, rows, DK)] * 2,
        values,
        queries,
        after=after,
        name="pack_reads",
    )


def merge(sizes, kept, swapped, name):
    def kernel(kept, swapped, *outs):
        for ahead in range(sizes.groups):
            for side, source in enumerate((kept, swapped)):
                outs[ahead][side] = source[ahead]

    outs = [shape(2, *kept.shape[1:])] * sizes.groups
    return call(kernel, outs, kept, swapped, name=name)


def merge_reads(sizes, kept, swapped):
    value_rows = sizes.heads * KEY_ROWS
    query_rows = sizes.heads * TOK

    def kernel(kept, swapped, *outs):
        for ahead in range(sizes.groups):
            for side, source in enumerate((kept, swapped)):
                outs[ahead][side] = source[ahead, :value_rows, :]
                outs[sizes.groups + ahead][side] = source[ahead, value_rows:, :]

    outs = [shape(2, value_rows, DK)] * sizes.groups + [shape(2, query_rows, DK)] * sizes.groups
    merged = call(kernel, outs, kept, swapped, name="merge_reads")
    return merged[: sizes.groups], merged[sizes.groups :]


def gather(sizes, pieces, first, count, scratch):
    z = axis_index("head")
    core = axis_index("core")
    for behind, piece in enumerate(pieces):
        source = shifted(z, sizes.groups - behind, sizes.groups) if behind else z
        for side in range(2):
            scratch[jnp.bitwise_xor(core, side) * sizes.groups + source] = piece[
                side, first : first + count, :
            ]


def unit_rows(scratch, head, chunk, count):
    first = head * count
    return jnp.concatenate(
        [
            scratch[2 * chunk, first : first + count, :],
            scratch[2 * chunk + 1, first : first + count, :],
        ],
        0,
    )


def key_stage(sizes, pieces):
    rows = sizes.heads * KEY_ROWS
    units = sizes.units
    groups = sizes.groups

    def kernel(*refs):
        pieces = refs[:groups]
        keys_out, inverse_out, end_out, ratio_out, row_out, step_out, prefix_out = refs[
            groups : groups + 7
        ]
        totals = refs[groups + 7 : groups + 7 + sizes.heads]
        blocks, scales, every = refs[groups + 7 + sizes.heads :]
        core = axis_index("core")
        gather(sizes, pieces, 0, rows, blocks)
        gather(sizes, pieces, rows, SCALE_ROWS, scales)
        flat = scales[...].reshape(2 * groups * SCALE_ROWS, 4 * TOK)
        picks = []
        for block in range(2):
            extent = (units, 2 * groups * SCALE_ROWS)
            unit = iota(extent, 0)
            row = (unit % groups * 2 + block) * SCALE_ROWS + unit // groups
            pick = iota(extent, 1) == row + core * sizes.heads
            picks.append(dot(pick.astype(BF16), flat))
        by_unit = jnp.concatenate(picks, 1).astype(BF16)
        maps = scale_maps()
        as_rows = dot_nt(by_unit, maps)
        as_columns = dot_nt(maps, by_unit)
        decay_row, segment_row, beta_row = (
            as_rows[:, number * REFL : (number + 1) * REFL] for number in range(3)
        )
        decay_column, segment_column, beta_column = (
            as_columns[number * REFL : (number + 1) * REFL] for number in range(3)
        )
        carried_row = jnp.exp(decay_row) * (segment_row == 0).astype(F32)
        last = REFL - 1
        end_row = jnp.exp(decay_row[:, last:] - decay_row)
        end_row = end_row * (segment_row[:, last:] == segment_row).astype(F32)
        square = (REFL, REFL)
        _, _, _, row_time = place(iota(square, 0))
        _, _, _, column_time = place(iota(square, 1))
        causal = row_time >= column_time
        strict = row_time > column_time
        diagonal = row_time == column_time
        same = (iota((DK, DK), 0) == iota((DK, DK), 1)).astype(F32)
        row_out[0] = beta_row
        row_out[2] = carried_row
        for base in range(0, units, GROUP):
            members = range(base, min(base + GROUP, units))
            keys = [unit_rows(blocks, *sizes.unit(unit), KEY_ROWS) for unit in members]
            grams = [dot_nt(key, key) for key in keys]
            squares = [jnp.where(diagonal, gram, 0.0) for gram in grams]
            norm_rows = [lax.rsqrt(jnp.sum(each, 0, keepdims=True) + EPSILON) for each in squares]
            norm_columns = [
                lax.rsqrt(jnp.sum(each, 1, keepdims=True) + EPSILON) for each in squares
            ]
            lowers = []
            for number, unit in enumerate(members):
                keys_out[unit] = keys[number]
                one = slice(unit, unit + 1)
                linked = causal & (segment_column[:, one] == segment_row[one])
                gap = decay_column[:, one] - decay_row[one]
                ratio = jnp.where(linked, jnp.exp(jnp.minimum(gap, 0.0)), 0.0) * norm_rows[number]
                ratio_out[unit] = read_rows(ratio)
                strengths = beta_column[:, one] * norm_columns[number]
                lowers.append(jnp.where(strict, strengths * ratio * grams[number], 0.0))
            solved = inverses(lowers)
            pairs = [split(each) for each in solved]
            kept_rows = [
                beta_row[unit : unit + 1] * carried_row[unit : unit + 1] * norm
                for unit, norm in zip(members, norm_rows)
            ]
            turned_keys = [key.T for key in keys]
            ends = []
            for number, unit in enumerate(members):
                high, low = pairs[number]
                inverse_out[unit] = jnp.concatenate([high, low], 1)
                row_out[1, unit : unit + 1, :] = kept_rows[number]
                weights = end_row[unit : unit + 1] * norm_rows[number]
                ends.append(
                    product(
                        beside(turned_keys[number].astype(F32) * weights), factor_of(high, low)
                    )
                )
            for number, unit in enumerate(members):
                turned = turned_keys[number]
                end_out[unit] = beside(ends[number] * beta_row[unit : unit + 1])
                every[unit] = carried_row[unit : unit + 1, last:] * same - dot_nt(
                    jnp.concatenate([turned, turned], 1), beside(ends[number] * kept_rows[number])
                )
        prefixes = [same] * sizes.heads
        for chunk in range(groups):
            for head in range(sizes.heads):
                unit = head * groups + chunk
                step = every[unit]
                high, low = split(step)
                step_out[unit] = jnp.concatenate([high, low], 1)
                prefix_out[unit] = prefixes[head]
                if chunk == 0:
                    prefixes[head] = step
                else:
                    prefixes[head] = product(beside(prefixes[head]), factor_of(high, low))
        if sizes.swapped:
            for head in range(sizes.heads):
                every[head] = prefixes[head]
            chip = axis_index("chip")
            for number in range(sizes.heads):
                totals[number][...] = every[jnp.bitwise_xor(chip, number)]
        else:
            for head in range(sizes.heads):
                totals[head][...] = prefixes[head]

    outs = [
        shape(units, REFL, DK),
        shape(units, REFL, 2 * REFL),
        shape(units, DK, 2 * REFL),
        shape(units, CHUNK, REFL, dtype=F32),
        shape(3, units, REFL, dtype=F32),
        shape(units, DK, 2 * DK),
        shape(units, DK, DK, dtype=F32),
    ] + [shape(DK, DK, dtype=F32)] * sizes.heads
    scratch = [
        pltpu.VMEM((2 * groups, rows, DK), BF16),
        pltpu.VMEM((2 * groups, SCALE_ROWS, DK), BF16),
        pltpu.VMEM((units, DK, DK), F32),
    ]
    results = call(
        kernel, outs, *pieces, scratch=scratch, name="key_stage"
    )
    return results[:7], results[7:]


def value_stage(sizes, pieces, ends, steps):
    groups = sizes.groups

    def kernel(*refs):
        pieces = refs[:groups]
        ends, steps, values_out, before_out = refs[groups : groups + 4]
        totals = refs[groups + 4 : groups + 4 + sizes.heads]
        blocks, every = refs[groups + 4 + sizes.heads :]
        gather(sizes, pieces, 0, sizes.heads * KEY_ROWS, blocks)
        injects = []
        for unit in range(sizes.units):
            value = unit_rows(blocks, *sizes.unit(unit), KEY_ROWS)
            values_out[unit] = value
            turned = value.T
            injects.append(dot_nt(jnp.concatenate([turned, turned], 1), ends[unit]))
        sums = [jnp.zeros((DV, DK), F32)] * sizes.heads
        for chunk in range(groups):
            for head in range(sizes.heads):
                unit = head * groups + chunk
                before_out[unit] = sums[head]
                if chunk == 0:
                    sums[head] = injects[unit]
                else:
                    step = steps[unit]
                    sums[head] = injects[unit] + product(
                        beside(sums[head]), factor_of(step[:, :DK], step[:, DK:])
                    )
        if sizes.swapped:
            for head in range(sizes.heads):
                every[head] = sums[head]
            chip = axis_index("chip")
            for number in range(sizes.heads):
                totals[number][...] = every[jnp.bitwise_xor(chip, number)]
        else:
            for head in range(sizes.heads):
                totals[head][...] = sums[head]

    outs = [shape(sizes.units, REFL, DV), shape(sizes.units, DV, DK, dtype=F32)]
    outs += [shape(DV, DK, dtype=F32)] * sizes.heads
    scratch = [
        pltpu.VMEM((2 * groups, sizes.heads * KEY_ROWS, DV), BF16),
        pltpu.VMEM((sizes.heads, DV, DK), F32),
    ]
    results = call(
        kernel, outs, *pieces, ends, steps, scratch=scratch, name="value_stage"
    )
    return results[0], results[1], results[2:]


def scan_states(sizes, transitions, injects):
    chips = sizes.chips

    def kernel(*refs):
        transitions = refs[:chips]
        injects = refs[chips : 2 * chips]
        outs = refs[2 * chips : 3 * chips]
        step, inject, entry = refs[3 * chips :]
        chip = axis_index("chip")
        for number in range(chips):
            source = jnp.bitwise_xor(chip, number)
            step[source] = transitions[number][...]
            inject[source] = injects[number][...]
        state = jnp.zeros((DV, DK), F32)
        for index in range(chips):
            entry[index] = state
            if index == 0:
                state = inject[index]
            elif index < chips - 1:
                state = product(beside(state), factor(step[index])) + inject[index]
        for number in range(chips):
            outs[number][...] = entry[jnp.bitwise_xor(chip, number)]

    scratch = [pltpu.VMEM((chips, DV, DK), F32)] * 3
    return call(
        kernel,
        [shape(DV, DK, dtype=F32)] * chips,
        *transitions,
        *injects,
        scratch=scratch,
        name="scan_states",
    )


def exchanged(sizes, parts):
    return [parts[0]] + [
        lax.ppermute(part, "chip", [(chip, chip ^ number) for chip in range(sizes.chips)])
        for number, part in enumerate(parts)
        if number
    ]


def entry_states(sizes, transitions, injects):
    if sizes.swapped:
        arrived = exchanged(sizes, transitions), exchanged(sizes, injects)
        return exchanged(sizes, scan_states(sizes, *arrived))
    transition = jnp.stack(transitions)
    inject = jnp.stack(injects)
    forward = [(chip, chip + 1) for chip in range(sizes.chips - 1)]

    def advance(_, entry):
        left = jnp.einsum("hvd,hde->hve", entry, transition, precision=lax.Precision.HIGHEST)
        return lax.ppermute(left + inject, "chip", forward)

    entry = lax.fori_loop(0, sizes.chips - 1, advance, jnp.zeros_like(inject))
    return [entry[head] for head in range(sizes.heads)]


def query_stage(sizes, pieces, values, before, keys, inverses_, ratios, rows, prefixes):
    groups = sizes.groups

    def kernel(*refs):
        pieces = refs[:groups]
        values, before, keys, inverse, ratio, rows, prefix, reader_out, inner_out, blocks = refs[
            groups:
        ]
        gather(sizes, pieces, 0, sizes.heads * TOK, blocks)
        for base in range(0, sizes.units, GROUP):
            members = range(base, min(base + GROUP, sizes.units))
            queries = [unit_rows(blocks, *sizes.unit(unit), TOK) for unit in members]
            scores = []
            for number, unit in enumerate(members):
                pair = inverse[unit]
                score = dot_nt(queries[number], keys[unit]) * ratio[unit]
                scores.append(product(beside(score), factor_of(pair[:, :REFL], pair[:, REFL:])))
            for number, unit in enumerate(members):
                one = slice(unit, unit + 1)
                inner = dot(beside(scores[number] * rows[0, one, :]), twice(values[unit]))
                carried = read_rows(jnp.broadcast_to(rows[2, one, :], (DK, REFL)).T)
                reader = carried * queries[number].astype(F32) - dot(
                    beside(scores[number] * rows[1, one, :]), twice(keys[unit])
                )
                high, low = split(jnp.concatenate([prefix[unit], before[unit]], 0))
                pair = beside(reader)
                both = dot_nt(pair, jnp.concatenate([high, high], 1)) + dot_nt(pair[:, :DK], low)
                reader_out[unit] = beside(both[:, :DK])
                inner_out[unit] = inner + both[:, DK:]

    outs = [
        shape(sizes.units, CHUNK, 2 * DK),
        shape(sizes.units, CHUNK, DV, dtype=F32),
    ]
    scratch = [pltpu.VMEM((2 * groups, sizes.heads * TOK, DK), BF16)]
    return call(
        kernel,
        outs,
        *pieces,
        values,
        before,
        keys,
        inverses_,
        ratios,
        rows,
        prefixes,
        scratch=scratch,
        name="query_stage",
    )


def read_states(sizes, states, readers, inners):
    groups = sizes.groups
    half = groups // 2

    def kernel(*refs):
        states = refs[: sizes.heads]
        readers, inners, own, other, entry = refs[sizes.heads :]
        core = axis_index("core")
        chip = axis_index("chip") if sizes.swapped else 0
        for number in range(sizes.heads):
            place_ = jnp.bitwise_xor(chip, number) if sizes.swapped else number
            entry[place_] = states[number][...]
        for head in range(sizes.heads):
            high, low = split(entry[head])
            stack = jnp.concatenate(
                [
                    jnp.concatenate([high, high], 1),
                    jnp.concatenate([low, jnp.zeros_like(low)], 1),
                ],
                0,
            )
            for side, out in enumerate((own, other)):
                first = head * groups + jnp.bitwise_xor(core, side) * half
                pair = readers[pl.ds(first, half)].reshape(half * CHUNK, 2 * DK)
                both = dot_nt(pair, stack)
                inner = inners[pl.ds(first, half)].reshape(half * CHUNK, DV)
                result = inner + both[:, :DV] + both[:, DV:]
                out[:, head * DV : (head + 1) * DV] = result.astype(BF16)

    outs = [shape(half * CHUNK, sizes.heads * DV)] * 2
    scratch = [pltpu.VMEM((sizes.heads, DV, DK), F32)]
    return call(kernel, outs, *states, readers, inners, scratch=scratch, name="read_states")


def join(sizes, own, other):
    width = sizes.heads * DV

    def kernel(own, other, out):
        first = axis_index("core") * width
        out[:, pl.ds(pl.multiple_of(first, width), width)] = own[...]
        out[:, pl.ds(pl.multiple_of(width - first, width), width)] = other[...]

    return call(kernel, shape(own.shape[0], 2 * width), own, other, name="join")


def local(queries, keys, values, betas, log_gates, starts):
    groups = lax.axis_size("head")
    sizes = Sizes(groups, log_gates.shape[1] // groups, lax.axis_size("chip"))
    own_starts = lax.dynamic_slice(starts, (axis_index("head") * TOK,), (TOK,)).reshape(1, TOK)

    def spread(parts):
        return [parts[0]] + [
            lax.ppermute(part, "head", [(z, (z + ahead) % groups) for z in range(groups)])
            for ahead, part in enumerate(parts)
            if ahead
        ]

    def swapped(part):
        return lax.ppermute(part, "core", [(0, 1), (1, 0)])

    kept_keys, sent_keys = pack_keys(sizes, keys, betas, log_gates, own_starts)
    key_parts = spread(merge(sizes, kept_keys, swapped(sent_keys), "merge_keys"))
    kept, sent = pack_reads(sizes, values, queries, after=(kept_keys,))
    value_parts, query_parts = merge_reads(sizes, kept, swapped(sent))
    value_parts = spread(value_parts)
    query_parts = spread(query_parts)
    (unit_keys, inverse, ends, ratios, rows, steps, prefixes), transitions = key_stage(
        sizes, key_parts
    )
    unit_values, before, injects = value_stage(sizes, value_parts, ends, steps)
    states = entry_states(sizes, transitions, injects)
    readers, inners = query_stage(
        sizes, query_parts, unit_values, before, unit_keys, inverse, ratios, rows, prefixes
    )
    own, other = read_states(sizes, states, readers, inners)
    return join(sizes, own, swapped(other))


def solution(mesh):
    devices = mesh.devices
    rows = P(("chip", "core", "head"), None)
    return jax.shard_map(
        local,
        mesh=Mesh(
            devices.reshape(devices.shape[0] // 2, 2, devices.shape[1]), ("chip", "core", "head")
        ),
        in_specs=(rows, rows, rows, rows, rows, P(("chip", "core"))),
        out_specs=P(("chip", "core"), "head"),
        check_vma=False,
    )
```

```python
import jax
import jax.numpy as jnp
from jax import lax
from jax.experimental import pallas as pl
from jax.experimental.pallas import tpu as pltpu
from jax.sharding import Mesh
from jax.sharding import PartitionSpec as P

DK = 128
DV = 128
NH = 2
TOK = 32
CHUNK = 2 * TOK
REFL = CHUNK * NH
GROUP = 8
EPSILON = 1e-06

KEY_ROWS = NH * TOK
SCALE_ROWS = 16

BF16 = jnp.bfloat16
F32 = jnp.float32
NT = (((1,), (1,)), ((), ()))


def iota(shape, axis):
    return lax.broadcasted_iota(jnp.int32, shape, axis)


def dot(left, right):
    return jnp.dot(left, right, preferred_element_type=F32)


def dot_nt(left, right):
    return lax.dot_general(left, right, NT, preferred_element_type=F32)


def split(value):
    high = value.astype(BF16)
    low = (value - high.astype(F32)).astype(BF16)
    return high, low


def beside(value):
    return jnp.concatenate(split(value), 1)


def twice(value):
    return jnp.concatenate([value, value], 0)


def factor(value):
    return factor_of(*split(value))


def factor_of(high, low):
    return jnp.concatenate(
        [jnp.concatenate([high, low], 1), jnp.concatenate([high, jnp.zeros_like(low)], 1)], 0
    )


def product(left_pair, right_factor):
    both = dot(left_pair, right_factor)
    half = both.shape[1] // 2
    return both[:, :half] + both[:, half:]


def place(index):
    block = index // (NH * TOK)
    step = (index // TOK) % NH
    token = index % TOK
    return block, step, token, (block * TOK + token) * NH + step


def scale_maps():
    shape = (REFL, 8 * TOK)
    block, step, token, _ = place(iota(shape, 0))
    column = iota(shape, 1)
    source_block = column // (4 * TOK)
    kind = (column // TOK) % 4
    source = source_block * TOK + column % TOK
    now = block * TOK + token
    decay = (kind == NH) & (source <= now)
    segment = (kind == NH + 1) & (source <= now)
    beta = (kind == step) & (source == now)
    return jnp.concatenate([part.astype(F32) for part in (decay, segment, beta)], 0).astype(BF16)


def piece_rows(size):
    if size == TOK:
        return [slice(NH * TOK, 2 * NH * TOK)]
    return [
        slice(start, start + size)
        for part in range(2 * NH)
        for start in range(part * TOK + size, (part + 1) * TOK, 2 * size)
    ]


def taken(value, slices):
    return jnp.concatenate([value[each] for each in slices], 0) if len(slices) > 1 else value[slices[0]]


def put(base, rows, slices):
    pieces = []
    at = 0
    done = 0
    for each in slices:
        if each.start > at:
            pieces.append(base[at : each.start])
        size = each.stop - each.start
        pieces.append(base[each] + rows[done : done + size])
        done += size
        at = each.stop
    if at < REFL:
        pieces.append(base[at:])
    return jnp.concatenate(pieces, 0)


def inverses(lowers):
    small = 8
    count = len(lowers)
    lane = iota((small, REFL), 1)
    group_of = (lane // (NH * TOK)) * (TOK // small) + (lane % TOK) // small
    groups = [(block, piece) for block in range(2) for piece in range(TOK // small)]

    def start_row(block, step, piece):
        return block * NH * TOK + step * TOK + piece * small

    folded = []
    for lower in lowers:
        for step in range(NH):
            rows = jnp.zeros((small, REFL), F32)
            for number, (block, piece) in enumerate(groups):
                first = start_row(block, step, piece)
                rows = jnp.where(group_of == number, lower[first : first + small], rows)
            folded.append(rows)
    height = NH * small
    lower_fold = jnp.concatenate(folded, 0)
    wide = iota((count * height, REFL), 1)
    high = iota((count * height, REFL), 0) % height
    inverse = ((wide // TOK) % NH == high // small) & (wide % small == high % small)
    inverse = inverse.astype(F32).reshape(count, height, REFL)
    for token in range(small):
        for step in range(NH):
            if token == small - 1 and step == NH - 1:
                continue
            source = (wide // (NH * TOK)) * (NH * TOK) + step * TOK + (wide % TOK) // small * small + token
            column = jnp.take_along_axis(lower_fold, source, axis=1, mode="promise_in_bounds")
            row = step * small + token
            inverse = inverse - column.reshape(count, height, REFL) * inverse[:, row : row + 1, :]
    results = []
    for number in range(count):
        pieces = []
        for block in range(2):
            for step in range(NH):
                rows = inverse[number, step * small : (step + 1) * small]
                for piece in range(TOK // small):
                    mine = group_of == block * (TOK // small) + piece
                    pieces.append(jnp.where(mine, rows, 0.0))
        results.append(jnp.concatenate(pieces, 0))
    size = small
    zero = jnp.zeros((REFL, REFL), F32)
    while size < CHUNK:
        slices = piece_rows(size)
        row_block, _, row_token, _ = place(iota((REFL, REFL), 0))
        column_block, _, column_token, _ = place(iota((REFL, REFL), 1))
        row_piece = (row_block * TOK + row_token) // size
        column_piece = (column_block * TOK + column_token) // size
        linked = taken(row_piece, slices) == taken(column_piece, slices) + 1
        crossings = [
            product(beside(jnp.where(linked, taken(lower, slices), 0.0)), factor(result))
            for lower, result in zip(lowers, results)
        ]
        changes = [
            product(beside(taken(result, slices)), factor(put(zero, crossing, slices)))
            for crossing, result in zip(crossings, results)
        ]
        results = [put(result, -change, slices) for change, result in zip(changes, results)]
        size *= 2
    return results


def read_rows(value):
    return jnp.concatenate(
        [
            value[(NH - 1) * TOK : NH * TOK],
            value[(2 * NH - 1) * TOK : 2 * NH * TOK],
        ],
        0,
    )


def call(kernel, outs, *args, scratch=(), flops=0, name=None):
    return pl.pallas_call(
        kernel,
        out_shape=outs,
        scratch_shapes=scratch,
        compiler_params=pltpu.CompilerParams(vmem_limit_bytes=24 * 2**20),
        cost_estimate=pl.CostEstimate(flops=flops, bytes_accessed=0, transcendentals=0),
        name=name,
    )(*args)


def shape(*sizes, dtype=BF16):
    return jax.ShapeDtypeStruct(sizes, dtype)


def axis_index(axis):
    return lax.axis_index(axis).astype(jnp.int32)


class Sizes:
    def __init__(self, groups, group_heads, chips):
        self.groups = groups
        self.group_heads = group_heads
        self.heads = group_heads // 2
        self.chips = chips
        self.units = self.heads * groups
        self.swapped = chips == self.heads and chips & (chips - 1) == 0

    def unit(self, number):
        return number // self.groups, number % self.groups


def shifted(index, by, size):
    moved = index + by
    return jnp.where(moved >= size, moved - size, moved)


def block_columns(source, first, count):
    return [
        source[:, pl.ds(pl.multiple_of(first + number * DK, DK), DK)] for number in range(count)
    ]


def pack_keys(sizes, keys, scalars, starts):
    rows = sizes.heads * KEY_ROWS
    count = sizes.heads * NH

    def kernel(keys, scalars, starts, *outs):
        z = axis_index("head")
        core = axis_index("core")
        width = scalars.shape[1]
        heads = width // (NH + 1)
        extent = (heads, width)
        pieces = []
        for step in range(NH):
            pick = iota(extent, 1) == iota(extent, 0) * NH + step
            pieces.append(dot_nt(pick.astype(BF16), scalars[...]))
        pick = iota(extent, 1) == iota(extent, 0) + heads * NH
        pieces.append(dot_nt(pick.astype(BF16), scalars[...]))
        pieces.append(jnp.broadcast_to(starts[...].astype(F32), (heads, TOK)))
        scales = jnp.concatenate(pieces, 1).astype(BF16)
        for ahead, out in enumerate(outs):
            target = shifted(z, ahead, sizes.groups)
            for side in range(2):
                owner = jnp.bitwise_xor(core, side)
                first = ((target * 2 + owner) * sizes.heads) * NH * DK
                for number, piece in enumerate(block_columns(keys, first, count)):
                    at = side * rows + number * TOK
                    out[at : at + TOK, :] = piece
            extent = (SCALE_ROWS, heads)
            pick = (iota(extent, 1) == target * sizes.group_heads + iota(extent, 0)) & (
                iota(extent, 0) < sizes.group_heads
            )
            out[2 * rows :, :] = dot(pick.astype(BF16), scales).astype(BF16)

    outs = [shape(2 * rows + SCALE_ROWS, DK)] * sizes.groups
    return call(kernel, outs, keys, scalars, starts, name="pack_keys")


def swap_keys(sizes, arrived):
    rows = sizes.heads * KEY_ROWS

    def kernel(*refs):
        out = refs[-1]
        z = axis_index("head")
        for behind, piece in enumerate(refs[:-1]):
            source = shifted(z, sizes.groups - behind, sizes.groups) if behind else z
            out[source] = piece[rows:, :]

    return call(kernel, shape(sizes.groups, rows + SCALE_ROWS, DK), *arrived, name="swap_keys")


def pack_reads(sizes, values, queries):
    value_rows = sizes.heads * KEY_ROWS
    rows = value_rows + sizes.heads * TOK

    def kernel(values, queries, kept, sent):
        z = axis_index("head")
        core = axis_index("core")
        for ahead in range(sizes.groups):
            target = shifted(z, ahead, sizes.groups)
            for side, out in enumerate((kept, sent)):
                first = (target * 2 + jnp.bitwise_xor(core, side)) * sizes.heads * DK
                pieces = block_columns(values, first * NH, sizes.heads * NH)
                pieces += block_columns(queries, first, sizes.heads)
                for number, piece in enumerate(pieces):
                    out[ahead, number * TOK : (number + 1) * TOK, :] = piece

    return call(
        kernel, [shape(sizes.groups, rows, DK)] * 2, values, queries, name="pack_reads"
    )


def merge_reads(sizes, kept, swapped):
    value_rows = sizes.heads * KEY_ROWS
    query_rows = sizes.heads * TOK

    def kernel(kept, swapped, *outs):
        for ahead in range(sizes.groups):
            for side, source in enumerate((kept, swapped)):
                outs[ahead][side] = source[ahead, :value_rows, :]
                outs[sizes.groups + ahead][side] = source[ahead, value_rows:, :]

    outs = [shape(2, value_rows, DK)] * sizes.groups + [shape(2, query_rows, DK)] * sizes.groups
    merged = call(kernel, outs, kept, swapped, name="merge_reads")
    return merged[: sizes.groups], merged[sizes.groups :]


def gather(sizes, pieces, scratch):
    z = axis_index("head")
    core = axis_index("core")
    for behind, piece in enumerate(pieces):
        source = shifted(z, sizes.groups - behind, sizes.groups) if behind else z
        for side in range(2):
            scratch[jnp.bitwise_xor(core, side) * sizes.groups + source] = piece[side]


def unit_rows(scratch, head, chunk, count):
    first = head * count
    return jnp.concatenate(
        [
            scratch[2 * chunk, first : first + count, :],
            scratch[2 * chunk + 1, first : first + count, :],
        ],
        0,
    )


def key_stage(sizes, arrived, swapped):
    rows = sizes.heads * KEY_ROWS
    units = sizes.units
    groups = sizes.groups

    def kernel(*refs):
        pieces = refs[:groups]
        swapped = refs[groups]
        keys_out, inverse_out, end_out, ratio_out, row_out, step_out, prefix_out = refs[
            groups + 1 : groups + 8
        ]
        totals = refs[groups + 8 : groups + 8 + sizes.heads]
        blocks, scales, every = refs[groups + 8 + sizes.heads :]
        z = axis_index("head")
        core = axis_index("core")
        for behind, piece in enumerate(pieces):
            source = shifted(z, groups - behind, groups) if behind else z
            blocks[core * groups + source] = piece[:rows, :]
            scales[core * groups + source] = piece[2 * rows :, :]
        other = (1 - core) * groups
        for source in range(groups):
            blocks[other + source] = swapped[source, :rows, :]
            scales[other + source] = swapped[source, rows:, :]
        flat = scales[...].reshape(2 * groups * SCALE_ROWS, 4 * TOK)
        picks = []
        for block in range(2):
            extent = (units, 2 * groups * SCALE_ROWS)
            unit = iota(extent, 0)
            row = (unit % groups * 2 + block) * SCALE_ROWS + unit // groups
            pick = iota(extent, 1) == row + core * sizes.heads
            picks.append(dot(pick.astype(BF16), flat))
        by_unit = jnp.concatenate(picks, 1).astype(BF16)
        maps = scale_maps()
        as_rows = dot_nt(by_unit, maps)
        as_columns = dot_nt(maps, by_unit)
        decay_row, segment_row, beta_row = (
            as_rows[:, number * REFL : (number + 1) * REFL] for number in range(3)
        )
        decay_column, segment_column, beta_column = (
            as_columns[number * REFL : (number + 1) * REFL] for number in range(3)
        )
        carried_row = jnp.exp(decay_row) * (segment_row == 0).astype(F32)
        last = REFL - 1
        end_row = jnp.exp(decay_row[:, last:] - decay_row)
        end_row = end_row * (segment_row[:, last:] == segment_row).astype(F32)
        square = (REFL, REFL)
        _, _, _, row_time = place(iota(square, 0))
        _, _, _, column_time = place(iota(square, 1))
        causal = row_time >= column_time
        strict = row_time > column_time
        diagonal = row_time == column_time
        same = (iota((DK, DK), 0) == iota((DK, DK), 1)).astype(F32)
        row_out[0] = beta_row
        row_out[2] = carried_row
        for base in range(0, units, GROUP):
            members = range(base, min(base + GROUP, units))
            keys = [unit_rows(blocks, *sizes.unit(unit), KEY_ROWS) for unit in members]
            grams = [dot_nt(key, key) for key in keys]
            squares = [jnp.where(diagonal, gram, 0.0) for gram in grams]
            norm_rows = [lax.rsqrt(jnp.sum(each, 0, keepdims=True) + EPSILON) for each in squares]
            norm_columns = [
                lax.rsqrt(jnp.sum(each, 1, keepdims=True) + EPSILON) for each in squares
            ]
            lowers = []
            for number, unit in enumerate(members):
                keys_out[unit] = keys[number]
                one = slice(unit, unit + 1)
                linked = causal & (segment_column[:, one] == segment_row[one])
                gap = decay_column[:, one] - decay_row[one]
                ratio = jnp.where(linked, jnp.exp(jnp.minimum(gap, 0.0)), 0.0) * norm_rows[number]
                ratio_out[unit] = read_rows(ratio)
                strengths = beta_column[:, one] * norm_columns[number]
                lowers.append(jnp.where(strict, strengths * ratio * grams[number], 0.0))
            solved = inverses(lowers)
            pairs = [split(each) for each in solved]
            kept_rows = [
                beta_row[unit : unit + 1] * carried_row[unit : unit + 1] * norm
                for unit, norm in zip(members, norm_rows)
            ]
            turned_keys = [key.T for key in keys]
            ends = []
            for number, unit in enumerate(members):
                high, low = pairs[number]
                inverse_out[unit] = jnp.concatenate([high, low], 1)
                row_out[1, unit : unit + 1, :] = kept_rows[number]
                weights = end_row[unit : unit + 1] * norm_rows[number]
                ends.append(
                    product(
                        beside(turned_keys[number].astype(F32) * weights), factor_of(high, low)
                    )
                )
            for number, unit in enumerate(members):
                turned = turned_keys[number]
                end_out[unit] = beside(ends[number] * beta_row[unit : unit + 1])
                every[unit] = carried_row[unit : unit + 1, last:] * same - dot_nt(
                    jnp.concatenate([turned, turned], 1), beside(ends[number] * kept_rows[number])
                )
        prefixes = [same] * sizes.heads
        for chunk in range(groups):
            for head in range(sizes.heads):
                unit = head * groups + chunk
                step = every[unit]
                high, low = split(step)
                step_out[unit] = jnp.concatenate([high, low], 1)
                prefix_out[unit] = prefixes[head]
                if chunk == 0:
                    prefixes[head] = step
                else:
                    prefixes[head] = product(beside(prefixes[head]), factor_of(high, low))
        if sizes.swapped:
            for head in range(sizes.heads):
                every[head] = prefixes[head]
            chip = axis_index("chip")
            for number in range(sizes.heads):
                totals[number][...] = every[jnp.bitwise_xor(chip, number)]
        else:
            for head in range(sizes.heads):
                totals[head][...] = prefixes[head]

    outs = [
        shape(units, REFL, DK),
        shape(units, REFL, 2 * REFL),
        shape(units, DK, 2 * REFL),
        shape(units, CHUNK, REFL, dtype=F32),
        shape(3, units, REFL, dtype=F32),
        shape(units, DK, 2 * DK),
        shape(units, DK, DK, dtype=F32),
    ] + [shape(DK, DK, dtype=F32)] * sizes.heads
    scratch = [
        pltpu.VMEM((2 * groups, rows, DK), BF16),
        pltpu.VMEM((2 * groups, SCALE_ROWS, DK), BF16),
        pltpu.VMEM((units, DK, DK), F32),
    ]
    results = call(
        kernel, outs, *arrived, swapped, scratch=scratch, flops=6_000_000_000, name="key_stage"
    )
    return results[:7], results[7:]


def value_stage(sizes, pieces, ends, steps):
    groups = sizes.groups

    def kernel(*refs):
        pieces = refs[:groups]
        ends, steps, values_out, before_out = refs[groups : groups + 4]
        totals = refs[groups + 4 : groups + 4 + sizes.heads]
        blocks, every = refs[groups + 4 + sizes.heads :]
        gather(sizes, pieces, blocks)
        injects = []
        for unit in range(sizes.units):
            value = unit_rows(blocks, *sizes.unit(unit), KEY_ROWS)
            values_out[unit] = value
            turned = value.T
            injects.append(dot_nt(jnp.concatenate([turned, turned], 1), ends[unit]))
        sums = [jnp.zeros((DV, DK), F32)] * sizes.heads
        for chunk in range(groups):
            for head in range(sizes.heads):
                unit = head * groups + chunk
                before_out[unit] = sums[head]
                if chunk == 0:
                    sums[head] = injects[unit]
                else:
                    step = steps[unit]
                    sums[head] = injects[unit] + product(
                        beside(sums[head]), factor_of(step[:, :DK], step[:, DK:])
                    )
        if sizes.swapped:
            for head in range(sizes.heads):
                every[head] = sums[head]
            chip = axis_index("chip")
            for number in range(sizes.heads):
                totals[number][...] = every[jnp.bitwise_xor(chip, number)]
        else:
            for head in range(sizes.heads):
                totals[head][...] = sums[head]

    outs = [shape(sizes.units, REFL, DV), shape(sizes.units, DV, DK, dtype=F32)]
    outs += [shape(DV, DK, dtype=F32)] * sizes.heads
    scratch = [
        pltpu.VMEM((2 * groups, sizes.heads * KEY_ROWS, DV), BF16),
        pltpu.VMEM((sizes.heads, DV, DK), F32),
    ]
    results = call(
        kernel, outs, *pieces, ends, steps, scratch=scratch, flops=2_000_000_000, name="value_stage"
    )
    return results[0], results[1], results[2:]


def scan_states(sizes, transitions, injects):
    chips = sizes.chips

    def kernel(*refs):
        transitions = refs[:chips]
        injects = refs[chips : 2 * chips]
        outs = refs[2 * chips : 3 * chips]
        step, inject, entry = refs[3 * chips :]
        chip = axis_index("chip")
        for number in range(chips):
            source = jnp.bitwise_xor(chip, number)
            step[source] = transitions[number][...]
            inject[source] = injects[number][...]
        state = jnp.zeros((DV, DK), F32)
        for index in range(chips):
            entry[index] = state
            if index == 0:
                state = inject[index]
            elif index < chips - 1:
                state = product(beside(state), factor(step[index])) + inject[index]
        for number in range(chips):
            outs[number][...] = entry[jnp.bitwise_xor(chip, number)]

    scratch = [pltpu.VMEM((chips, DV, DK), F32)] * 3
    return call(
        kernel,
        [shape(DV, DK, dtype=F32)] * chips,
        *transitions,
        *injects,
        scratch=scratch,
        name="scan_states",
    )


def exchanged(sizes, parts):
    return [parts[0]] + [
        lax.ppermute(part, "chip", [(chip, chip ^ number) for chip in range(sizes.chips)])
        for number, part in enumerate(parts)
        if number
    ]


def entry_states(sizes, transitions, injects):
    if sizes.swapped:
        arrived = exchanged(sizes, transitions), exchanged(sizes, injects)
        return exchanged(sizes, scan_states(sizes, *arrived))
    transition = jnp.stack(transitions)
    inject = jnp.stack(injects)
    forward = [(chip, chip + 1) for chip in range(sizes.chips - 1)]

    def advance(_, entry):
        left = jnp.einsum("hvd,hde->hve", entry, transition, precision=lax.Precision.HIGHEST)
        return lax.ppermute(left + inject, "chip", forward)

    entry = lax.fori_loop(0, sizes.chips - 1, advance, jnp.zeros_like(inject))
    return [entry[head] for head in range(sizes.heads)]


def query_stage(sizes, pieces, values, before, keys, inverses_, ratios, rows, prefixes):
    groups = sizes.groups

    def kernel(*refs):
        pieces = refs[:groups]
        values, before, keys, inverse, ratio, rows, prefix, reader_out, inner_out, blocks = refs[
            groups:
        ]
        gather(sizes, pieces, blocks)
        extent = (CHUNK, REFL)
        block, step, token, _ = place(iota(extent, 1))
        read_places = (step == NH - 1) & (block * TOK + token == iota(extent, 0))
        for base in range(0, sizes.units, GROUP):
            members = range(base, min(base + GROUP, sizes.units))
            queries = [unit_rows(blocks, *sizes.unit(unit), TOK) for unit in members]
            scores = []
            for number, unit in enumerate(members):
                pair = inverse[unit]
                score = dot_nt(queries[number], keys[unit]) * ratio[unit]
                scores.append(product(beside(score), factor_of(pair[:, :REFL], pair[:, REFL:])))
            for number, unit in enumerate(members):
                one = slice(unit, unit + 1)
                inner = dot(beside(scores[number] * rows[0, one, :]), twice(values[unit]))
                query = queries[number]
                halves = [query[:TOK]] * NH + [query[TOK:]] * NH
                carried = jnp.where(read_places, rows[2, one, :], 0.0)
                reader = dot(
                    jnp.concatenate(
                        [beside(carried), beside(scores[number] * -rows[1, one, :])], 1
                    ),
                    jnp.concatenate([twice(jnp.concatenate(halves, 0)), twice(keys[unit])], 0),
                )
                high, low = split(jnp.concatenate([prefix[unit], before[unit]], 0))
                pair = beside(reader)
                both = dot_nt(pair, jnp.concatenate([high, high], 1)) + dot_nt(pair[:, :DK], low)
                reader_out[unit] = beside(both[:, :DK])
                inner_out[unit] = inner + both[:, DK:]

    outs = [
        shape(sizes.units, CHUNK, 2 * DK),
        shape(sizes.units, CHUNK, DV, dtype=F32),
    ]
    scratch = [pltpu.VMEM((2 * groups, sizes.heads * TOK, DK), BF16)]
    return call(
        kernel,
        outs,
        *pieces,
        values,
        before,
        keys,
        inverses_,
        ratios,
        rows,
        prefixes,
        scratch=scratch,
        flops=3_000_000_000,
        name="query_stage",
    )


def read_states(sizes, states, readers, inners):
    groups = sizes.groups
    half = groups // 2

    def kernel(*refs):
        states = refs[: sizes.heads]
        readers, inners, own, other, entry = refs[sizes.heads :]
        core = axis_index("core")
        chip = axis_index("chip") if sizes.swapped else 0
        for number in range(sizes.heads):
            place_ = jnp.bitwise_xor(chip, number) if sizes.swapped else number
            entry[place_] = states[number][...]
        for head in range(sizes.heads):
            high, low = split(entry[head])
            stack = jnp.concatenate(
                [
                    jnp.concatenate([high, high], 1),
                    jnp.concatenate([low, jnp.zeros_like(low)], 1),
                ],
                0,
            )
            for side, out in enumerate((own, other)):
                first = head * groups + jnp.bitwise_xor(core, side) * half
                pair = readers[pl.ds(first, half)].reshape(half * CHUNK, 2 * DK)
                both = dot_nt(pair, stack)
                inner = inners[pl.ds(first, half)].reshape(half * CHUNK, DV)
                result = inner + both[:, :DV] + both[:, DV:]
                out[:, head * DV : (head + 1) * DV] = result.astype(BF16)

    outs = [shape(half * CHUNK, sizes.heads * DV)] * 2
    scratch = [pltpu.VMEM((sizes.heads, DV, DK), F32)]
    return call(kernel, outs, *states, readers, inners, scratch=scratch, name="read_states")


def join(sizes, own, other):
    width = sizes.heads * DV

    def kernel(own, other, out):
        first = axis_index("core") * width
        out[:, pl.ds(pl.multiple_of(first, width), width)] = own[...]
        out[:, pl.ds(pl.multiple_of(width - first, width), width)] = other[...]

    return call(kernel, shape(own.shape[0], 2 * width), own, other, name="join")


def local(queries, keys, values, betas, log_gates, starts):
    groups = lax.axis_size("head")
    sizes = Sizes(groups, log_gates.shape[1] // groups, lax.axis_size("chip"))
    own_starts = lax.dynamic_slice(starts, (axis_index("head") * TOK,), (TOK,)).reshape(1, TOK)

    def spread(parts):
        return [parts[0]] + [
            lax.ppermute(part, "head", [(z, (z + ahead) % groups) for z in range(groups)])
            for ahead, part in enumerate(parts)
            if ahead
        ]

    def swapped(part):
        return lax.ppermute(part, "core", [(0, 1), (1, 0)])

    arrived = spread(pack_keys(sizes, keys, jnp.concatenate([betas, log_gates], 1), own_starts))
    kept, sent = pack_reads(sizes, values, queries)
    value_parts, query_parts = merge_reads(sizes, kept, swapped(sent))
    value_parts = spread(value_parts)
    query_parts = spread(query_parts)
    other_keys = swapped(swap_keys(sizes, arrived))
    (unit_keys, inverse, ends, ratios, rows, steps, prefixes), transitions = key_stage(
        sizes, arrived, other_keys
    )
    unit_values, before, injects = value_stage(sizes, value_parts, ends, steps)
    states = entry_states(sizes, transitions, injects)
    readers, inners = query_stage(
        sizes, query_parts, unit_values, before, unit_keys, inverse, ratios, rows, prefixes
    )
    own, other = read_states(sizes, states, readers, inners)
    return join(sizes, own, swapped(other))


def solution(mesh):
    devices = mesh.devices
    rows = P(("chip", "core", "head"), None)
    return jax.shard_map(
        local,
        mesh=Mesh(
            devices.reshape(devices.shape[0] // 2, 2, devices.shape[1]), ("chip", "core", "head")
        ),
        in_specs=(rows, rows, rows, rows, rows, P(("chip", "core"))),
        out_specs=P(("chip", "core"), "head"),
        check_vma=False,
    )
```

```python
import jax
import jax.numpy as jnp
from jax import lax
from jax.experimental import pallas as pl
from jax.experimental.pallas import tpu as pltpu
from jax.sharding import Mesh
from jax.sharding import PartitionSpec as P

DK = 128
DV = 128
NH = 2
TOK = 32
CHUNK = 2 * TOK
REFL = CHUNK * NH
GROUP = 8
EPSILON = 1e-06

KEY_ROWS = NH * TOK
SCALE_ROWS = 16

BF16 = jnp.bfloat16
F32 = jnp.float32
NT = (((1,), (1,)), ((), ()))


def iota(shape, axis):
    return lax.broadcasted_iota(jnp.int32, shape, axis)


def dot(left, right):
    return jnp.dot(left, right, preferred_element_type=F32)


def dot_nt(left, right):
    return lax.dot_general(left, right, NT, preferred_element_type=F32)


def split(value):
    high = value.astype(BF16)
    low = (value - high.astype(F32)).astype(BF16)
    return high, low


def beside(value):
    return jnp.concatenate(split(value), 1)


def twice(value):
    return jnp.concatenate([value, value], 0)


def factor(value):
    return factor_of(*split(value))


def factor_of(high, low):
    return jnp.concatenate(
        [jnp.concatenate([high, low], 1), jnp.concatenate([high, jnp.zeros_like(low)], 1)], 0
    )


def product(left_pair, right_factor):
    both = dot(left_pair, right_factor)
    half = both.shape[1] // 2
    return both[:, :half] + both[:, half:]


def place(index):
    block = index // (NH * TOK)
    step = (index // TOK) % NH
    token = index % TOK
    return block, step, token, (block * TOK + token) * NH + step


def scale_maps():
    shape = (REFL, 8 * TOK)
    block, step, token, _ = place(iota(shape, 0))
    column = iota(shape, 1)
    source_block = column // (4 * TOK)
    kind = (column // TOK) % 4
    source = source_block * TOK + column % TOK
    now = block * TOK + token
    decay = (kind == NH) & (source <= now)
    segment = (kind == NH + 1) & (source <= now)
    beta = (kind == step) & (source == now)
    return jnp.concatenate([part.astype(F32) for part in (decay, segment, beta)], 0).astype(BF16)


def piece_rows(size):
    if size == TOK:
        return [slice(NH * TOK, 2 * NH * TOK)]
    return [
        slice(start, start + size)
        for part in range(2 * NH)
        for start in range(part * TOK + size, (part + 1) * TOK, 2 * size)
    ]


def taken(value, slices):
    return jnp.concatenate([value[each] for each in slices], 0) if len(slices) > 1 else value[slices[0]]


def put(base, rows, slices):
    pieces = []
    at = 0
    done = 0
    for each in slices:
        if each.start > at:
            pieces.append(base[at : each.start])
        size = each.stop - each.start
        pieces.append(base[each] + rows[done : done + size])
        done += size
        at = each.stop
    if at < REFL:
        pieces.append(base[at:])
    return jnp.concatenate(pieces, 0)


def inverses(lowers):
    small = 8
    count = len(lowers)
    lane = iota((small, REFL), 1)
    group_of = (lane // (NH * TOK)) * (TOK // small) + (lane % TOK) // small
    groups = [(block, piece) for block in range(2) for piece in range(TOK // small)]

    def start_row(block, step, piece):
        return block * NH * TOK + step * TOK + piece * small

    folded = []
    for lower in lowers:
        for step in range(NH):
            rows = jnp.zeros((small, REFL), F32)
            for number, (block, piece) in enumerate(groups):
                first = start_row(block, step, piece)
                rows = jnp.where(group_of == number, lower[first : first + small], rows)
            folded.append(rows)
    height = NH * small
    lower_fold = jnp.concatenate(folded, 0)
    wide = iota((count * height, REFL), 1)
    high = iota((count * height, REFL), 0) % height
    inverse = ((wide // TOK) % NH == high // small) & (wide % small == high % small)
    inverse = inverse.astype(F32).reshape(count, height, REFL)
    for token in range(small):
        for step in range(NH):
            if token == small - 1 and step == NH - 1:
                continue
            source = (wide // (NH * TOK)) * (NH * TOK) + step * TOK + (wide % TOK) // small * small + token
            column = jnp.take_along_axis(lower_fold, source, axis=1, mode="promise_in_bounds")
            row = step * small + token
            inverse = inverse - column.reshape(count, height, REFL) * inverse[:, row : row + 1, :]
    results = []
    for number in range(count):
        pieces = []
        for block in range(2):
            for step in range(NH):
                rows = inverse[number, step * small : (step + 1) * small]
                for piece in range(TOK // small):
                    mine = group_of == block * (TOK // small) + piece
                    pieces.append(jnp.where(mine, rows, 0.0))
        results.append(jnp.concatenate(pieces, 0))
    size = small
    zero = jnp.zeros((REFL, REFL), F32)
    while size < CHUNK:
        slices = piece_rows(size)
        row_block, _, row_token, _ = place(iota((REFL, REFL), 0))
        column_block, _, column_token, _ = place(iota((REFL, REFL), 1))
        row_piece = (row_block * TOK + row_token) // size
        column_piece = (column_block * TOK + column_token) // size
        linked = taken(row_piece, slices) == taken(column_piece, slices) + 1
        crossings = [
            product(beside(jnp.where(linked, taken(lower, slices), 0.0)), factor(result))
            for lower, result in zip(lowers, results)
        ]
        changes = [
            product(beside(taken(result, slices)), factor(put(zero, crossing, slices)))
            for crossing, result in zip(crossings, results)
        ]
        results = [put(result, -change, slices) for change, result in zip(changes, results)]
        size *= 2
    return results


def read_rows(value):
    return jnp.concatenate(
        [
            value[(NH - 1) * TOK : NH * TOK],
            value[(2 * NH - 1) * TOK : 2 * NH * TOK],
        ],
        0,
    )


def call(kernel, outs, *args, scratch=(), flops=0, name=None):
    return pl.pallas_call(
        kernel,
        out_shape=outs,
        scratch_shapes=scratch,
        compiler_params=pltpu.CompilerParams(vmem_limit_bytes=24 * 2**20),
        cost_estimate=pl.CostEstimate(flops=flops, bytes_accessed=0, transcendentals=0),
        name=name,
    )(*args)


def shape(*sizes, dtype=BF16):
    return jax.ShapeDtypeStruct(sizes, dtype)


def axis_index(axis):
    return lax.axis_index(axis).astype(jnp.int32)


class Sizes:
    def __init__(self, groups, group_heads, chips):
        self.groups = groups
        self.group_heads = group_heads
        self.heads = group_heads // 2
        self.chips = chips
        self.units = self.heads * groups
        self.paired = chips == 4

    def unit(self, number):
        return number // self.groups, number % self.groups


def shifted(index, by, size):
    moved = index + by
    return jnp.where(moved >= size, moved - size, moved)


def block_columns(source, first, count):
    return [
        source[:, pl.ds(pl.multiple_of(first + number * DK, DK), DK)] for number in range(count)
    ]


def pack_keys(sizes, keys, scalars, starts):
    rows = sizes.heads * KEY_ROWS
    count = sizes.heads * NH

    def kernel(keys, scalars, starts, *outs):
        z = axis_index("head")
        core = axis_index("core")
        width = scalars.shape[1]
        heads = width // (NH + 1)
        extent = (heads, width)
        pieces = []
        for step in range(NH):
            pick = iota(extent, 1) == iota(extent, 0) * NH + step
            pieces.append(dot_nt(pick.astype(BF16), scalars[...]))
        pick = iota(extent, 1) == iota(extent, 0) + heads * NH
        pieces.append(dot_nt(pick.astype(BF16), scalars[...]))
        pieces.append(jnp.broadcast_to(starts[...].astype(F32), (heads, TOK)))
        scales = jnp.concatenate(pieces, 1).astype(BF16)
        for ahead, out in enumerate(outs):
            target = shifted(z, ahead, sizes.groups)
            for side in range(2):
                owner = jnp.bitwise_xor(core, side)
                first = ((target * 2 + owner) * sizes.heads) * NH * DK
                for number, piece in enumerate(block_columns(keys, first, count)):
                    at = side * rows + number * TOK
                    out[at : at + TOK, :] = piece
            extent = (SCALE_ROWS, heads)
            pick = (iota(extent, 1) == target * sizes.group_heads + iota(extent, 0)) & (
                iota(extent, 0) < sizes.group_heads
            )
            out[2 * rows :, :] = dot(pick.astype(BF16), scales).astype(BF16)

    outs = [shape(2 * rows + SCALE_ROWS, DK)] * sizes.groups
    return call(kernel, outs, keys, scalars, starts, name="pack_keys")


def swap_keys(sizes, arrived):
    rows = sizes.heads * KEY_ROWS

    def kernel(*refs):
        out = refs[-1]
        z = axis_index("head")
        for behind, piece in enumerate(refs[:-1]):
            source = shifted(z, sizes.groups - behind, sizes.groups) if behind else z
            out[source] = piece[rows:, :]

    return call(kernel, shape(sizes.groups, rows + SCALE_ROWS, DK), *arrived, name="swap_keys")


def pack_reads(sizes, values, queries):
    value_rows = sizes.heads * KEY_ROWS
    rows = value_rows + sizes.heads * TOK

    def kernel(values, queries, kept, sent):
        z = axis_index("head")
        core = axis_index("core")
        for ahead in range(sizes.groups):
            target = shifted(z, ahead, sizes.groups)
            for side, out in enumerate((kept, sent)):
                first = (target * 2 + jnp.bitwise_xor(core, side)) * sizes.heads * DK
                pieces = block_columns(values, first * NH, sizes.heads * NH)
                pieces += block_columns(queries, first, sizes.heads)
                for number, piece in enumerate(pieces):
                    out[ahead, number * TOK : (number + 1) * TOK, :] = piece

    return call(
        kernel, [shape(sizes.groups, rows, DK)] * 2, values, queries, name="pack_reads"
    )


def merge_reads(sizes, kept, swapped):
    value_rows = sizes.heads * KEY_ROWS
    query_rows = sizes.heads * TOK

    def kernel(kept, swapped, *outs):
        for ahead in range(sizes.groups):
            for side, source in enumerate((kept, swapped)):
                outs[ahead][side] = source[ahead, :value_rows, :]
                outs[sizes.groups + ahead][side] = source[ahead, value_rows:, :]

    outs = [shape(2, value_rows, DK)] * sizes.groups + [shape(2, query_rows, DK)] * sizes.groups
    merged = call(kernel, outs, kept, swapped, name="merge_reads")
    return merged[: sizes.groups], merged[sizes.groups :]


def gather(sizes, pieces, scratch):
    z = axis_index("head")
    core = axis_index("core")
    for behind, piece in enumerate(pieces):
        source = shifted(z, sizes.groups - behind, sizes.groups) if behind else z
        for side in range(2):
            scratch[jnp.bitwise_xor(core, side) * sizes.groups + source] = piece[side]


def unit_rows(scratch, head, chunk, count):
    first = head * count
    return jnp.concatenate(
        [
            scratch[2 * chunk, first : first + count, :],
            scratch[2 * chunk + 1, first : first + count, :],
        ],
        0,
    )


def key_stage(sizes, arrived, swapped):
    rows = sizes.heads * KEY_ROWS
    units = sizes.units
    groups = sizes.groups

    def kernel(*refs):
        pieces = refs[:groups]
        swapped = refs[groups]
        keys_out, inverse_out, end_out, ratio_out, row_out, step_out, prefix_out = refs[
            groups + 1 : groups + 8
        ]
        total_out, blocks, scales, every = refs[groups + 8 :]
        z = axis_index("head")
        core = axis_index("core")
        for behind, piece in enumerate(pieces):
            source = shifted(z, groups - behind, groups) if behind else z
            blocks[core * groups + source] = piece[:rows, :]
            scales[core * groups + source] = piece[2 * rows :, :]
        other = (1 - core) * groups
        for source in range(groups):
            blocks[other + source] = swapped[source, :rows, :]
            scales[other + source] = swapped[source, rows:, :]
        flat = scales[...].reshape(2 * groups * SCALE_ROWS, 4 * TOK)
        picks = []
        for block in range(2):
            extent = (units, 2 * groups * SCALE_ROWS)
            unit = iota(extent, 0)
            row = (unit % groups * 2 + block) * SCALE_ROWS + unit // groups
            pick = iota(extent, 1) == row + core * sizes.heads
            picks.append(dot(pick.astype(BF16), flat))
        by_unit = jnp.concatenate(picks, 1).astype(BF16)
        maps = scale_maps()
        as_rows = dot_nt(by_unit, maps)
        as_columns = dot_nt(maps, by_unit)
        decay_row, segment_row, beta_row = (
            as_rows[:, number * REFL : (number + 1) * REFL] for number in range(3)
        )
        decay_column, segment_column, beta_column = (
            as_columns[number * REFL : (number + 1) * REFL] for number in range(3)
        )
        carried_row = jnp.exp(decay_row) * (segment_row == 0).astype(F32)
        last = REFL - 1
        end_row = jnp.exp(decay_row[:, last:] - decay_row)
        end_row = end_row * (segment_row[:, last:] == segment_row).astype(F32)
        square = (REFL, REFL)
        _, _, _, row_time = place(iota(square, 0))
        _, _, _, column_time = place(iota(square, 1))
        causal = row_time >= column_time
        strict = row_time > column_time
        diagonal = row_time == column_time
        same = (iota((DK, DK), 0) == iota((DK, DK), 1)).astype(F32)
        row_out[0] = beta_row
        row_out[2] = carried_row
        for base in range(0, units, GROUP):
            members = range(base, min(base + GROUP, units))
            keys = [unit_rows(blocks, *sizes.unit(unit), KEY_ROWS) for unit in members]
            grams = [dot_nt(key, key) for key in keys]
            squares = [jnp.where(diagonal, gram, 0.0) for gram in grams]
            norm_rows = [lax.rsqrt(jnp.sum(each, 0, keepdims=True) + EPSILON) for each in squares]
            norm_columns = [
                lax.rsqrt(jnp.sum(each, 1, keepdims=True) + EPSILON) for each in squares
            ]
            lowers = []
            for number, unit in enumerate(members):
                keys_out[unit] = keys[number]
                one = slice(unit, unit + 1)
                linked = causal & (segment_column[:, one] == segment_row[one])
                gap = decay_column[:, one] - decay_row[one]
                ratio = jnp.where(linked, jnp.exp(jnp.minimum(gap, 0.0)), 0.0) * norm_rows[number]
                ratio_out[unit] = read_rows(ratio)
                strengths = beta_column[:, one] * norm_columns[number]
                lowers.append(jnp.where(strict, strengths * ratio * grams[number], 0.0))
            solved = inverses(lowers)
            pairs = [split(each) for each in solved]
            kept_rows = [
                beta_row[unit : unit + 1] * carried_row[unit : unit + 1] * norm
                for unit, norm in zip(members, norm_rows)
            ]
            turned_keys = [key.T for key in keys]
            ends = []
            for number, unit in enumerate(members):
                high, low = pairs[number]
                inverse_out[unit] = jnp.concatenate([high, low], 1)
                row_out[1, unit : unit + 1, :] = kept_rows[number]
                weights = end_row[unit : unit + 1] * norm_rows[number]
                ends.append(
                    product(
                        beside(turned_keys[number].astype(F32) * weights), factor_of(high, low)
                    )
                )
            for number, unit in enumerate(members):
                turned = turned_keys[number]
                end_out[unit] = beside(ends[number] * beta_row[unit : unit + 1])
                every[unit] = carried_row[unit : unit + 1, last:] * same - dot_nt(
                    jnp.concatenate([turned, turned], 1), beside(ends[number] * kept_rows[number])
                )
        prefixes = [same] * sizes.heads
        for chunk in range(groups):
            for head in range(sizes.heads):
                unit = head * groups + chunk
                step = every[unit]
                high, low = split(step)
                step_out[unit] = jnp.concatenate([high, low], 1)
                prefix_out[unit] = prefixes[head]
                if chunk == 0:
                    prefixes[head] = step
                else:
                    prefixes[head] = product(beside(prefixes[head]), factor_of(high, low))
        for head in range(sizes.heads):
            total_out[head] = prefixes[head]

    outs = [
        shape(units, REFL, DK),
        shape(units, REFL, 2 * REFL),
        shape(units, DK, 2 * REFL),
        shape(units, CHUNK, REFL, dtype=F32),
        shape(3, units, REFL, dtype=F32),
        shape(units, DK, 2 * DK),
        shape(units, DK, DK, dtype=F32),
        shape(sizes.heads, DK, DK, dtype=F32),
    ]
    scratch = [
        pltpu.VMEM((2 * groups, rows, DK), BF16),
        pltpu.VMEM((2 * groups, SCALE_ROWS, DK), BF16),
        pltpu.VMEM((units, DK, DK), F32),
    ]
    results = call(
        kernel, outs, *arrived, swapped, scratch=scratch, flops=6_000_000_000, name="key_stage"
    )
    return results[:7], results[7]


def value_stage(sizes, pieces, ends, steps):
    groups = sizes.groups

    def kernel(*refs):
        pieces = refs[:groups]
        ends, steps, values_out, before_out, total_out, blocks = refs[groups:]
        gather(sizes, pieces, blocks)
        injects = []
        for unit in range(sizes.units):
            value = unit_rows(blocks, *sizes.unit(unit), KEY_ROWS)
            values_out[unit] = value
            turned = value.T
            injects.append(dot_nt(jnp.concatenate([turned, turned], 1), ends[unit]))
        sums = [jnp.zeros((DV, DK), F32)] * sizes.heads
        for chunk in range(groups):
            for head in range(sizes.heads):
                unit = head * groups + chunk
                before_out[unit] = sums[head]
                if chunk == 0:
                    sums[head] = injects[unit]
                else:
                    step = steps[unit]
                    sums[head] = injects[unit] + product(
                        beside(sums[head]), factor_of(step[:, :DK], step[:, DK:])
                    )
        for head in range(sizes.heads):
            total_out[head] = sums[head]

    outs = [shape(sizes.units, REFL, DV), shape(sizes.units, DV, DK, dtype=F32)]
    outs += [shape(sizes.heads, DV, DK, dtype=F32)]
    scratch = [pltpu.VMEM((2 * groups, sizes.heads * KEY_ROWS, DV), BF16)]
    return call(
        kernel, outs, *pieces, ends, steps, scratch=scratch, flops=2_000_000_000, name="value_stage"
    )


def pair_injects(sizes, transitions, injects):
    def kernel(own_step, step, own, other, out):
        first = axis_index("chip") % 2 == 0
        for head in range(sizes.heads):
            later_step = jnp.where(first, step[head], own_step[head])
            earlier = jnp.where(first, own[head], other[head])
            later = jnp.where(first, other[head], own[head])
            out[head] = product(beside(earlier), factor(later_step)) + later

    return call(
        kernel, shape(sizes.heads, DV, DK, dtype=F32), *transitions, *injects, name="pair_injects"
    )


def partnered(sizes, part, bit):
    return lax.ppermute(part, "chip", [(chip, chip ^ bit) for chip in range(sizes.chips)])


def entry_states(sizes, transitions, injects):
    if sizes.paired:
        step = partnered(sizes, transitions, 1)
        inject = partnered(sizes, injects, 1)
        pair = pair_injects(sizes, (transitions, step), (injects, inject))
        return partnered(sizes, pair, 2), step, inject
    forward = [(chip, chip + 1) for chip in range(sizes.chips - 1)]

    def advance(_, entry):
        left = jnp.einsum("hvd,hde->hve", entry, transitions, precision=lax.Precision.HIGHEST)
        return lax.ppermute(left + injects, "chip", forward)

    return (lax.fori_loop(0, sizes.chips - 1, advance, jnp.zeros_like(injects)),)


def query_stage(sizes, pieces, values, before, keys, inverses_, ratios, rows, prefixes):
    groups = sizes.groups

    def kernel(*refs):
        pieces = refs[:groups]
        values, before, keys, inverse, ratio, rows, prefix, reader_out, inner_out, blocks = refs[
            groups:
        ]
        gather(sizes, pieces, blocks)
        extent = (CHUNK, REFL)
        block, step, token, _ = place(iota(extent, 1))
        read_places = (step == NH - 1) & (block * TOK + token == iota(extent, 0))
        for base in range(0, sizes.units, GROUP):
            members = range(base, min(base + GROUP, sizes.units))
            queries = [unit_rows(blocks, *sizes.unit(unit), TOK) for unit in members]
            scores = []
            for number, unit in enumerate(members):
                pair = inverse[unit]
                score = dot_nt(queries[number], keys[unit]) * ratio[unit]
                scores.append(product(beside(score), factor_of(pair[:, :REFL], pair[:, REFL:])))
            for number, unit in enumerate(members):
                one = slice(unit, unit + 1)
                inner = dot(beside(scores[number] * rows[0, one, :]), twice(values[unit]))
                query = queries[number]
                halves = [query[:TOK]] * NH + [query[TOK:]] * NH
                carried = jnp.where(read_places, rows[2, one, :], 0.0)
                reader = dot(
                    jnp.concatenate(
                        [beside(carried), beside(scores[number] * -rows[1, one, :])], 1
                    ),
                    jnp.concatenate([twice(jnp.concatenate(halves, 0)), twice(keys[unit])], 0),
                )
                high, low = split(jnp.concatenate([prefix[unit], before[unit]], 0))
                pair = beside(reader)
                both = dot_nt(pair, jnp.concatenate([high, high], 1)) + dot_nt(pair[:, :DK], low)
                reader_out[unit] = beside(both[:, :DK])
                inner_out[unit] = inner + both[:, DK:]

    outs = [
        shape(sizes.units, CHUNK, 2 * DK),
        shape(sizes.units, CHUNK, DV, dtype=F32),
    ]
    scratch = [pltpu.VMEM((2 * groups, sizes.heads * TOK, DK), BF16)]
    return call(
        kernel,
        outs,
        *pieces,
        values,
        before,
        keys,
        inverses_,
        ratios,
        rows,
        prefixes,
        scratch=scratch,
        flops=3_000_000_000,
        name="query_stage",
    )


def read_states(sizes, states_, readers, inners):
    groups = sizes.groups
    half = groups // 2

    def kernel(*refs):
        states = refs[: len(states_)]
        readers, inners, own, other = refs[len(states_) :]
        core = axis_index("core")
        chip = axis_index("chip")
        for head in range(sizes.heads):
            entry = states[0][head]
            if sizes.paired:
                entry = jnp.where(chip >= 2, entry, 0.0)
                further = product(beside(entry), factor(states[1][head])) + states[2][head]
                entry = jnp.where(chip % 2 == 0, entry, further)
            high, low = split(entry)
            stack = jnp.concatenate(
                [
                    jnp.concatenate([high, high], 1),
                    jnp.concatenate([low, jnp.zeros_like(low)], 1),
                ],
                0,
            )
            for side, out in enumerate((own, other)):
                first = head * groups + jnp.bitwise_xor(core, side) * half
                pair = readers[pl.ds(first, half)].reshape(half * CHUNK, 2 * DK)
                both = dot_nt(pair, stack)
                inner = inners[pl.ds(first, half)].reshape(half * CHUNK, DV)
                result = inner + both[:, :DV] + both[:, DV:]
                out[:, head * DV : (head + 1) * DV] = result.astype(BF16)

    outs = [shape(half * CHUNK, sizes.heads * DV)] * 2
    return call(kernel, outs, *states_, readers, inners, name="read_states")


def join(sizes, own, other):
    width = sizes.heads * DV

    def kernel(own, other, out):
        first = axis_index("core") * width
        out[:, pl.ds(pl.multiple_of(first, width), width)] = own[...]
        out[:, pl.ds(pl.multiple_of(width - first, width), width)] = other[...]

    return call(kernel, shape(own.shape[0], 2 * width), own, other, name="join")


def local(queries, keys, values, betas, log_gates, starts):
    groups = lax.axis_size("head")
    sizes = Sizes(groups, log_gates.shape[1] // groups, lax.axis_size("chip"))
    own_starts = lax.dynamic_slice(starts, (axis_index("head") * TOK,), (TOK,)).reshape(1, TOK)

    def spread(parts):
        return [parts[0]] + [
            lax.ppermute(part, "head", [(z, (z + ahead) % groups) for z in range(groups)])
            for ahead, part in enumerate(parts)
            if ahead
        ]

    def swapped(part):
        return lax.ppermute(part, "core", [(0, 1), (1, 0)])

    arrived = spread(pack_keys(sizes, keys, jnp.concatenate([betas, log_gates], 1), own_starts))
    kept, sent = pack_reads(sizes, values, queries)
    value_parts, query_parts = merge_reads(sizes, kept, swapped(sent))
    value_parts = spread(value_parts)
    query_parts = spread(query_parts)
    other_keys = swapped(swap_keys(sizes, arrived))
    (unit_keys, inverse, ends, ratios, rows, steps, prefixes), transitions = key_stage(
        sizes, arrived, other_keys
    )
    unit_values, before, injects = value_stage(sizes, value_parts, ends, steps)
    states = entry_states(sizes, transitions, injects)
    readers, inners = query_stage(
        sizes, query_parts, unit_values, before, unit_keys, inverse, ratios, rows, prefixes
    )
    own, other = read_states(sizes, states, readers, inners)
    return join(sizes, own, swapped(other))


def solution(mesh):
    devices = mesh.devices
    rows = P(("chip", "core", "head"), None)
    return jax.shard_map(
        local,
        mesh=Mesh(
            devices.reshape(devices.shape[0] // 2, 2, devices.shape[1]), ("chip", "core", "head")
        ),
        in_specs=(rows, rows, rows, rows, rows, P(("chip", "core"))),
        out_specs=P(("chip", "core"), "head"),
        check_vma=False,
    )
```

```python
import jax
import jax.numpy as jnp
from jax import lax
from jax.experimental import pallas as pl
from jax.experimental.pallas import tpu as pltpu
from jax.sharding import Mesh
from jax.sharding import PartitionSpec as P

DK = 128
DV = 128
NH = 2
TOK = 32
CHUNK = 2 * TOK
REFL = CHUNK * NH
GROUP = 8
EPSILON = 1e-06

KEY_ROWS = NH * TOK
SCALE_ROWS = 16

BF16 = jnp.bfloat16
F32 = jnp.float32
NT = (((1,), (1,)), ((), ()))


def iota(shape, axis):
    return lax.broadcasted_iota(jnp.int32, shape, axis)


def dot(left, right):
    return jnp.dot(left, right, preferred_element_type=F32)


def dot_nt(left, right):
    return lax.dot_general(left, right, NT, preferred_element_type=F32)


def split(value):
    high = value.astype(BF16)
    low = (value - high.astype(F32)).astype(BF16)
    return high, low


def beside(value):
    return jnp.concatenate(split(value), 1)


def twice(value):
    return jnp.concatenate([value, value], 0)


def factor(value):
    return factor_of(*split(value))


def factor_of(high, low):
    return jnp.concatenate(
        [jnp.concatenate([high, low], 1), jnp.concatenate([high, jnp.zeros_like(low)], 1)], 0
    )


def product(left_pair, right_factor):
    both = dot(left_pair, right_factor)
    half = both.shape[1] // 2
    return both[:, :half] + both[:, half:]


def place(index):
    block = index // (NH * TOK)
    step = (index // TOK) % NH
    token = index % TOK
    return block, step, token, (block * TOK + token) * NH + step


def scale_maps():
    shape = (REFL, 8 * TOK)
    block, step, token, _ = place(iota(shape, 0))
    column = iota(shape, 1)
    source_block = column // (4 * TOK)
    kind = (column // TOK) % 4
    source = source_block * TOK + column % TOK
    now = block * TOK + token
    decay = (kind == NH) & (source <= now)
    segment = (kind == NH + 1) & (source <= now)
    beta = (kind == step) & (source == now)
    return jnp.concatenate([part.astype(F32) for part in (decay, segment, beta)], 0).astype(BF16)


def piece_rows(size):
    if size == TOK:
        return [slice(NH * TOK, 2 * NH * TOK)]
    return [
        slice(start, start + size)
        for part in range(2 * NH)
        for start in range(part * TOK + size, (part + 1) * TOK, 2 * size)
    ]


def taken(value, slices):
    return jnp.concatenate([value[each] for each in slices], 0) if len(slices) > 1 else value[slices[0]]


def put(base, rows, slices):
    pieces = []
    at = 0
    done = 0
    for each in slices:
        if each.start > at:
            pieces.append(base[at : each.start])
        size = each.stop - each.start
        pieces.append(base[each] + rows[done : done + size])
        done += size
        at = each.stop
    if at < REFL:
        pieces.append(base[at:])
    return jnp.concatenate(pieces, 0)


def inverses(lowers):
    small = 8
    count = len(lowers)
    lane = iota((small, REFL), 1)
    group_of = (lane // (NH * TOK)) * (TOK // small) + (lane % TOK) // small
    groups = [(block, piece) for block in range(2) for piece in range(TOK // small)]

    def start_row(block, step, piece):
        return block * NH * TOK + step * TOK + piece * small

    folded = []
    for lower in lowers:
        for step in range(NH):
            rows = jnp.zeros((small, REFL), F32)
            for number, (block, piece) in enumerate(groups):
                first = start_row(block, step, piece)
                rows = jnp.where(group_of == number, lower[first : first + small], rows)
            folded.append(rows)
    height = NH * small
    lower_fold = jnp.concatenate(folded, 0)
    wide = iota((count * height, REFL), 1)
    high = iota((count * height, REFL), 0) % height
    inverse = ((wide // TOK) % NH == high // small) & (wide % small == high % small)
    inverse = inverse.astype(F32).reshape(count, height, REFL)
    for token in range(small):
        for step in range(NH):
            if token == small - 1 and step == NH - 1:
                continue
            source = (wide // (NH * TOK)) * (NH * TOK) + step * TOK + (wide % TOK) // small * small + token
            column = jnp.take_along_axis(lower_fold, source, axis=1, mode="promise_in_bounds")
            row = step * small + token
            inverse = inverse - column.reshape(count, height, REFL) * inverse[:, row : row + 1, :]
    results = []
    for number in range(count):
        pieces = []
        for block in range(2):
            for step in range(NH):
                rows = inverse[number, step * small : (step + 1) * small]
                for piece in range(TOK // small):
                    mine = group_of == block * (TOK // small) + piece
                    pieces.append(jnp.where(mine, rows, 0.0))
        results.append(jnp.concatenate(pieces, 0))
    size = small
    zero = jnp.zeros((REFL, REFL), F32)
    while size < CHUNK:
        slices = piece_rows(size)
        row_block, _, row_token, _ = place(iota((REFL, REFL), 0))
        column_block, _, column_token, _ = place(iota((REFL, REFL), 1))
        row_piece = (row_block * TOK + row_token) // size
        column_piece = (column_block * TOK + column_token) // size
        linked = taken(row_piece, slices) == taken(column_piece, slices) + 1
        crossings = [
            product(beside(jnp.where(linked, taken(lower, slices), 0.0)), factor(result))
            for lower, result in zip(lowers, results)
        ]
        changes = [
            product(beside(taken(result, slices)), factor(put(zero, crossing, slices)))
            for crossing, result in zip(crossings, results)
        ]
        results = [put(result, -change, slices) for change, result in zip(changes, results)]
        size *= 2
    return results


def read_rows(value):
    return jnp.concatenate(
        [
            value[(NH - 1) * TOK : NH * TOK],
            value[(2 * NH - 1) * TOK : 2 * NH * TOK],
        ],
        0,
    )


def call(kernel, outs, *args, scratch=(), flops=0, far=0, name=None):
    specs = [pl.BlockSpec(memory_space=pltpu.HBM)] * far
    specs += [pl.BlockSpec(memory_space=pltpu.VMEM)] * (len(args) - far)
    return pl.pallas_call(
        kernel,
        out_shape=outs,
        in_specs=specs,
        scratch_shapes=scratch,
        compiler_params=pltpu.CompilerParams(vmem_limit_bytes=24 * 2**20),
        cost_estimate=pl.CostEstimate(flops=flops, bytes_accessed=0, transcendentals=0),
        name=name,
    )(*args)


def shape(*sizes, dtype=BF16):
    return jax.ShapeDtypeStruct(sizes, dtype)


def axis_index(axis):
    return lax.axis_index(axis).astype(jnp.int32)


class Sizes:
    def __init__(self, groups, group_heads, chips):
        self.groups = groups
        self.group_heads = group_heads
        self.heads = group_heads // 2
        self.chips = chips
        self.units = self.heads * groups
        self.swapped = chips == self.heads and chips & (chips - 1) == 0

    def unit(self, number):
        return number // self.groups, number % self.groups


def shifted(index, by, size):
    moved = index + by
    return jnp.where(moved >= size, moved - size, moved)


def block_columns(source, first, count):
    return [
        source[:, pl.ds(pl.multiple_of(first + number * DK, DK), DK)] for number in range(count)
    ]


def pack_keys(sizes, keys, betas, log_gates, starts):
    rows = sizes.heads * KEY_ROWS
    count = sizes.heads * NH

    def kernel(far_keys, far_betas, far_gates, far_starts, *refs):
        outs = refs[: sizes.groups]
        keys, betas, log_gates, starts, done = refs[sizes.groups :]
        width = sizes.group_heads * NH * DK
        pairs = [(far_betas, betas), (far_gates, log_gates), (far_starts, starts)]
        for group in range(sizes.groups):
            part = slice(group * width, (group + 1) * width)
            pairs.append((far_keys.at[:, part], keys.at[:, part]))
        copies = [
            pltpu.make_async_copy(far, near, done.at[number])
            for number, (far, near) in enumerate(pairs)
        ]
        for copy in copies:
            copy.start()
        for copy in copies:
            copy.wait()
        z = axis_index("head")
        core = axis_index("core")
        heads = log_gates.shape[1]
        pieces = []
        for step in range(NH):
            extent = (heads, heads * NH)
            pick = iota(extent, 1) == iota(extent, 0) * NH + step
            pieces.append(dot_nt(pick.astype(BF16), betas[...]))
        same = iota((heads, heads), 0) == iota((heads, heads), 1)
        pieces.append(dot_nt(same.astype(BF16), log_gates[...]))
        length = sizes.groups * TOK
        own = iota((length, TOK), 0) == z * TOK + iota((length, TOK), 1)
        own_starts = jnp.broadcast_to(starts[...].astype(F32), (heads, length)).astype(BF16)
        pieces.append(dot(own_starts, own.astype(BF16)))
        scales = jnp.concatenate(pieces, 1).astype(BF16)
        for ahead, out in enumerate(outs):
            target = shifted(z, ahead, sizes.groups)
            for side in range(2):
                owner = jnp.bitwise_xor(core, side)
                first = ((target * 2 + owner) * sizes.heads) * NH * DK
                for number, piece in enumerate(block_columns(keys, first, count)):
                    at = side * rows + number * TOK
                    out[at : at + TOK, :] = piece
            extent = (SCALE_ROWS, heads)
            pick = (iota(extent, 1) == target * sizes.group_heads + iota(extent, 0)) & (
                iota(extent, 0) < sizes.group_heads
            )
            out[2 * rows :, :] = dot(pick.astype(BF16), scales).astype(BF16)

    outs = [shape(2 * rows + SCALE_ROWS, DK)] * sizes.groups
    loaded = (keys, betas, log_gates, starts)
    scratch = [pltpu.VMEM(each.shape, each.dtype) for each in loaded]
    return call(
        kernel,
        outs,
        *[pltpu.with_memory_space_constraint(each, pltpu.HBM) for each in loaded],
        scratch=scratch + [pltpu.SemaphoreType.DMA((3 + sizes.groups,))],
        far=4,
        name="pack_keys",
    )


def swap_keys(sizes, arrived):
    rows = sizes.heads * KEY_ROWS

    def kernel(*refs):
        out = refs[-1]
        z = axis_index("head")
        for behind, piece in enumerate(refs[:-1]):
            source = shifted(z, sizes.groups - behind, sizes.groups) if behind else z
            out[source] = piece[rows:, :]

    return call(kernel, shape(sizes.groups, rows + SCALE_ROWS, DK), *arrived, name="swap_keys")


def pack_reads(sizes, values, queries):
    value_rows = sizes.heads * KEY_ROWS
    rows = value_rows + sizes.heads * TOK

    def kernel(values, queries, kept, sent):
        z = axis_index("head")
        core = axis_index("core")
        for ahead in range(sizes.groups):
            target = shifted(z, ahead, sizes.groups)
            for side, out in enumerate((kept, sent)):
                first = (target * 2 + jnp.bitwise_xor(core, side)) * sizes.heads * DK
                pieces = block_columns(values, first * NH, sizes.heads * NH)
                pieces += block_columns(queries, first, sizes.heads)
                for number, piece in enumerate(pieces):
                    out[ahead, number * TOK : (number + 1) * TOK, :] = piece

    return call(
        kernel, [shape(sizes.groups, rows, DK)] * 2, values, queries, name="pack_reads"
    )


def merge_reads(sizes, kept, swapped):
    value_rows = sizes.heads * KEY_ROWS
    query_rows = sizes.heads * TOK

    def kernel(kept, swapped, *outs):
        for ahead in range(sizes.groups):
            for side, source in enumerate((kept, swapped)):
                outs[ahead][side] = source[ahead, :value_rows, :]
                outs[sizes.groups + ahead][side] = source[ahead, value_rows:, :]

    outs = [shape(2, value_rows, DK)] * sizes.groups + [shape(2, query_rows, DK)] * sizes.groups
    merged = call(kernel, outs, kept, swapped, name="merge_reads")
    return merged[: sizes.groups], merged[sizes.groups :]


def gather(sizes, pieces, scratch):
    z = axis_index("head")
    core = axis_index("core")
    for behind, piece in enumerate(pieces):
        source = shifted(z, sizes.groups - behind, sizes.groups) if behind else z
        for side in range(2):
            scratch[jnp.bitwise_xor(core, side) * sizes.groups + source] = piece[side]


def unit_rows(scratch, head, chunk, count):
    first = head * count
    return jnp.concatenate(
        [
            scratch[2 * chunk, first : first + count, :],
            scratch[2 * chunk + 1, first : first + count, :],
        ],
        0,
    )


def key_stage(sizes, arrived, swapped):
    rows = sizes.heads * KEY_ROWS
    units = sizes.units
    groups = sizes.groups

    def kernel(*refs):
        pieces = refs[:groups]
        swapped = refs[groups]
        keys_out, inverse_out, end_out, ratio_out, row_out, step_out, prefix_out = refs[
            groups + 1 : groups + 8
        ]
        totals = refs[groups + 8 : groups + 8 + sizes.heads]
        blocks, scales, every = refs[groups + 8 + sizes.heads :]
        z = axis_index("head")
        core = axis_index("core")
        for behind, piece in enumerate(pieces):
            source = shifted(z, groups - behind, groups) if behind else z
            blocks[core * groups + source] = piece[:rows, :]
            scales[core * groups + source] = piece[2 * rows :, :]
        other = (1 - core) * groups
        for source in range(groups):
            blocks[other + source] = swapped[source, :rows, :]
            scales[other + source] = swapped[source, rows:, :]
        flat = scales[...].reshape(2 * groups * SCALE_ROWS, 4 * TOK)
        picks = []
        for block in range(2):
            extent = (units, 2 * groups * SCALE_ROWS)
            unit = iota(extent, 0)
            row = (unit % groups * 2 + block) * SCALE_ROWS + unit // groups
            pick = iota(extent, 1) == row + core * sizes.heads
            picks.append(dot(pick.astype(BF16), flat))
        by_unit = jnp.concatenate(picks, 1).astype(BF16)
        maps = scale_maps()
        as_rows = dot_nt(by_unit, maps)
        as_columns = dot_nt(maps, by_unit)
        decay_row, segment_row, beta_row = (
            as_rows[:, number * REFL : (number + 1) * REFL] for number in range(3)
        )
        decay_column, segment_column, beta_column = (
            as_columns[number * REFL : (number + 1) * REFL] for number in range(3)
        )
        carried_row = jnp.exp(decay_row) * (segment_row == 0).astype(F32)
        last = REFL - 1
        end_row = jnp.exp(decay_row[:, last:] - decay_row)
        end_row = end_row * (segment_row[:, last:] == segment_row).astype(F32)
        square = (REFL, REFL)
        _, _, _, row_time = place(iota(square, 0))
        _, _, _, column_time = place(iota(square, 1))
        causal = row_time >= column_time
        strict = row_time > column_time
        diagonal = row_time == column_time
        same = (iota((DK, DK), 0) == iota((DK, DK), 1)).astype(F32)
        row_out[0] = beta_row
        row_out[2] = carried_row
        for base in range(0, units, GROUP):
            members = range(base, min(base + GROUP, units))
            keys = [unit_rows(blocks, *sizes.unit(unit), KEY_ROWS) for unit in members]
            grams = [dot_nt(key, key) for key in keys]
            squares = [jnp.where(diagonal, gram, 0.0) for gram in grams]
            norm_rows = [lax.rsqrt(jnp.sum(each, 0, keepdims=True) + EPSILON) for each in squares]
            norm_columns = [
                lax.rsqrt(jnp.sum(each, 1, keepdims=True) + EPSILON) for each in squares
            ]
            lowers = []
            for number, unit in enumerate(members):
                keys_out[unit] = keys[number]
                one = slice(unit, unit + 1)
                linked = causal & (segment_column[:, one] == segment_row[one])
                gap = decay_column[:, one] - decay_row[one]
                ratio = jnp.where(linked, jnp.exp(jnp.minimum(gap, 0.0)), 0.0) * norm_rows[number]
                ratio_out[unit] = read_rows(ratio)
                strengths = beta_column[:, one] * norm_columns[number]
                lowers.append(jnp.where(strict, strengths * ratio * grams[number], 0.0))
            solved = inverses(lowers)
            pairs = [split(each) for each in solved]
            kept_rows = [
                beta_row[unit : unit + 1] * carried_row[unit : unit + 1] * norm
                for unit, norm in zip(members, norm_rows)
            ]
            turned_keys = [key.T for key in keys]
            ends = []
            for number, unit in enumerate(members):
                high, low = pairs[number]
                inverse_out[unit] = jnp.concatenate([high, low], 1)
                row_out[1, unit : unit + 1, :] = kept_rows[number]
                weights = end_row[unit : unit + 1] * norm_rows[number]
                ends.append(
                    product(
                        beside(turned_keys[number].astype(F32) * weights), factor_of(high, low)
                    )
                )
            for number, unit in enumerate(members):
                turned = turned_keys[number]
                end_out[unit] = beside(ends[number] * beta_row[unit : unit + 1])
                every[unit] = carried_row[unit : unit + 1, last:] * same - dot_nt(
                    jnp.concatenate([turned, turned], 1), beside(ends[number] * kept_rows[number])
                )
        prefixes = [same] * sizes.heads
        for chunk in range(groups):
            for head in range(sizes.heads):
                unit = head * groups + chunk
                step = every[unit]
                high, low = split(step)
                step_out[unit] = jnp.concatenate([high, low], 1)
                prefix_out[unit] = prefixes[head]
                if chunk == 0:
                    prefixes[head] = step
                else:
                    prefixes[head] = product(beside(prefixes[head]), factor_of(high, low))
        if sizes.swapped:
            for head in range(sizes.heads):
                every[head] = prefixes[head]
            chip = axis_index("chip")
            for number in range(sizes.heads):
                totals[number][...] = every[jnp.bitwise_xor(chip, number)]
        else:
            for head in range(sizes.heads):
                totals[head][...] = prefixes[head]

    outs = [
        shape(units, REFL, DK),
        shape(units, REFL, 2 * REFL),
        shape(units, DK, 2 * REFL),
        shape(units, CHUNK, REFL, dtype=F32),
        shape(3, units, REFL, dtype=F32),
        shape(units, DK, 2 * DK),
        shape(units, DK, DK, dtype=F32),
    ] + [shape(DK, DK, dtype=F32)] * sizes.heads
    scratch = [
        pltpu.VMEM((2 * groups, rows, DK), BF16),
        pltpu.VMEM((2 * groups, SCALE_ROWS, DK), BF16),
        pltpu.VMEM((units, DK, DK), F32),
    ]
    results = call(
        kernel, outs, *arrived, swapped, scratch=scratch, flops=6_000_000_000, name="key_stage"
    )
    return results[:7], results[7:]


def value_stage(sizes, pieces, ends, steps):
    groups = sizes.groups

    def kernel(*refs):
        pieces = refs[:groups]
        ends, steps, values_out, before_out = refs[groups : groups + 4]
        totals = refs[groups + 4 : groups + 4 + sizes.heads]
        blocks, every = refs[groups + 4 + sizes.heads :]
        gather(sizes, pieces, blocks)
        injects = []
        for unit in range(sizes.units):
            value = unit_rows(blocks, *sizes.unit(unit), KEY_ROWS)
            values_out[unit] = value
            turned = value.T
            injects.append(dot_nt(jnp.concatenate([turned, turned], 1), ends[unit]))
        sums = [jnp.zeros((DV, DK), F32)] * sizes.heads
        for chunk in range(groups):
            for head in range(sizes.heads):
                unit = head * groups + chunk
                before_out[unit] = sums[head]
                if chunk == 0:
                    sums[head] = injects[unit]
                else:
                    step = steps[unit]
                    sums[head] = injects[unit] + product(
                        beside(sums[head]), factor_of(step[:, :DK], step[:, DK:])
                    )
        if sizes.swapped:
            for head in range(sizes.heads):
                every[head] = sums[head]
            chip = axis_index("chip")
            for number in range(sizes.heads):
                totals[number][...] = every[jnp.bitwise_xor(chip, number)]
        else:
            for head in range(sizes.heads):
                totals[head][...] = sums[head]

    outs = [shape(sizes.units, REFL, DV), shape(sizes.units, DV, DK, dtype=F32)]
    outs += [shape(DV, DK, dtype=F32)] * sizes.heads
    scratch = [
        pltpu.VMEM((2 * groups, sizes.heads * KEY_ROWS, DV), BF16),
        pltpu.VMEM((sizes.heads, DV, DK), F32),
    ]
    results = call(
        kernel, outs, *pieces, ends, steps, scratch=scratch, flops=2_000_000_000, name="value_stage"
    )
    return results[0], results[1], results[2:]


def scan_states(sizes, transitions, injects):
    chips = sizes.chips

    def kernel(*refs):
        transitions = refs[:chips]
        injects = refs[chips : 2 * chips]
        outs = refs[2 * chips : 3 * chips]
        step, inject, entry = refs[3 * chips :]
        chip = axis_index("chip")
        for number in range(chips):
            source = jnp.bitwise_xor(chip, number)
            step[source] = transitions[number][...]
            inject[source] = injects[number][...]
        state = jnp.zeros((DV, DK), F32)
        for index in range(chips):
            entry[index] = state
            if index == 0:
                state = inject[index]
            elif index < chips - 1:
                state = product(beside(state), factor(step[index])) + inject[index]
        for number in range(chips):
            outs[number][...] = entry[jnp.bitwise_xor(chip, number)]

    scratch = [pltpu.VMEM((chips, DV, DK), F32)] * 3
    return call(
        kernel,
        [shape(DV, DK, dtype=F32)] * chips,
        *transitions,
        *injects,
        scratch=scratch,
        name="scan_states",
    )


def exchanged(sizes, parts):
    return [parts[0]] + [
        lax.ppermute(part, "chip", [(chip, chip ^ number) for chip in range(sizes.chips)])
        for number, part in enumerate(parts)
        if number
    ]


def entry_states(sizes, transitions, injects):
    if sizes.swapped:
        arrived = exchanged(sizes, transitions), exchanged(sizes, injects)
        return exchanged(sizes, scan_states(sizes, *arrived))
    transition = jnp.stack(transitions)
    inject = jnp.stack(injects)
    forward = [(chip, chip + 1) for chip in range(sizes.chips - 1)]

    def advance(_, entry):
        left = jnp.einsum("hvd,hde->hve", entry, transition, precision=lax.Precision.HIGHEST)
        return lax.ppermute(left + inject, "chip", forward)

    entry = lax.fori_loop(0, sizes.chips - 1, advance, jnp.zeros_like(inject))
    return [entry[head] for head in range(sizes.heads)]


def query_stage(sizes, pieces, values, before, keys, inverses_, ratios, rows, prefixes):
    groups = sizes.groups

    def kernel(*refs):
        pieces = refs[:groups]
        values, before, keys, inverse, ratio, rows, prefix, reader_out, inner_out, blocks = refs[
            groups:
        ]
        gather(sizes, pieces, blocks)
        for base in range(0, sizes.units, GROUP):
            members = range(base, min(base + GROUP, sizes.units))
            queries = [unit_rows(blocks, *sizes.unit(unit), TOK) for unit in members]
            scores = []
            for number, unit in enumerate(members):
                pair = inverse[unit]
                score = dot_nt(queries[number], keys[unit]) * ratio[unit]
                scores.append(product(beside(score), factor_of(pair[:, :REFL], pair[:, REFL:])))
            for number, unit in enumerate(members):
                one = slice(unit, unit + 1)
                inner = dot(beside(scores[number] * rows[0, one, :]), twice(values[unit]))
                carried = read_rows(jnp.broadcast_to(rows[2, one, :], (DK, REFL)).T)
                reader = carried * queries[number].astype(F32) - dot(
                    beside(scores[number] * rows[1, one, :]), twice(keys[unit])
                )
                high, low = split(jnp.concatenate([prefix[unit], before[unit]], 0))
                pair = beside(reader)
                both = dot_nt(pair, jnp.concatenate([high, high], 1)) + dot_nt(pair[:, :DK], low)
                reader_out[unit] = beside(both[:, :DK])
                inner_out[unit] = inner + both[:, DK:]

    outs = [
        shape(sizes.units, CHUNK, 2 * DK),
        shape(sizes.units, CHUNK, DV, dtype=F32),
    ]
    scratch = [pltpu.VMEM((2 * groups, sizes.heads * TOK, DK), BF16)]
    return call(
        kernel,
        outs,
        *pieces,
        values,
        before,
        keys,
        inverses_,
        ratios,
        rows,
        prefixes,
        scratch=scratch,
        flops=3_000_000_000,
        name="query_stage",
    )


def read_states(sizes, states, readers, inners):
    groups = sizes.groups
    half = groups // 2

    def kernel(*refs):
        states = refs[: sizes.heads]
        readers, inners, own, other, entry = refs[sizes.heads :]
        core = axis_index("core")
        chip = axis_index("chip") if sizes.swapped else 0
        for number in range(sizes.heads):
            place_ = jnp.bitwise_xor(chip, number) if sizes.swapped else number
            entry[place_] = states[number][...]
        for head in range(sizes.heads):
            high, low = split(entry[head])
            stack = jnp.concatenate(
                [
                    jnp.concatenate([high, high], 1),
                    jnp.concatenate([low, jnp.zeros_like(low)], 1),
                ],
                0,
            )
            for side, out in enumerate((own, other)):
                first = head * groups + jnp.bitwise_xor(core, side) * half
                pair = readers[pl.ds(first, half)].reshape(half * CHUNK, 2 * DK)
                both = dot_nt(pair, stack)
                inner = inners[pl.ds(first, half)].reshape(half * CHUNK, DV)
                result = inner + both[:, :DV] + both[:, DV:]
                out[:, head * DV : (head + 1) * DV] = result.astype(BF16)

    outs = [shape(half * CHUNK, sizes.heads * DV)] * 2
    scratch = [pltpu.VMEM((sizes.heads, DV, DK), F32)]
    return call(kernel, outs, *states, readers, inners, scratch=scratch, name="read_states")


def join(sizes, own, other):
    width = sizes.heads * DV

    def kernel(own, other, out):
        first = axis_index("core") * width
        out[:, pl.ds(pl.multiple_of(first, width), width)] = own[...]
        out[:, pl.ds(pl.multiple_of(width - first, width), width)] = other[...]

    return call(kernel, shape(own.shape[0], 2 * width), own, other, name="join")


def local(queries, keys, values, betas, log_gates, starts):
    groups = lax.axis_size("head")
    sizes = Sizes(groups, log_gates.shape[1] // groups, lax.axis_size("chip"))

    def spread(parts):
        return [parts[0]] + [
            lax.ppermute(part, "head", [(z, (z + ahead) % groups) for z in range(groups)])
            for ahead, part in enumerate(parts)
            if ahead
        ]

    def swapped(part):
        return lax.ppermute(part, "core", [(0, 1), (1, 0)])

    arrived = spread(pack_keys(sizes, keys, betas, log_gates, starts.reshape(1, -1)))
    kept, sent = pack_reads(sizes, values, queries)
    value_parts, query_parts = merge_reads(sizes, kept, swapped(sent))
    value_parts = spread(value_parts)
    query_parts = spread(query_parts)
    other_keys = swapped(swap_keys(sizes, arrived))
    (unit_keys, inverse, ends, ratios, rows, steps, prefixes), transitions = key_stage(
        sizes, arrived, other_keys
    )
    unit_values, before, injects = value_stage(sizes, value_parts, ends, steps)
    states = entry_states(sizes, transitions, injects)
    readers, inners = query_stage(
        sizes, query_parts, unit_values, before, unit_keys, inverse, ratios, rows, prefixes
    )
    own, other = read_states(sizes, states, readers, inners)
    return join(sizes, own, swapped(other))


def solution(mesh):
    devices = mesh.devices
    rows = P(("chip", "core", "head"), None)
    return jax.shard_map(
        local,
        mesh=Mesh(
            devices.reshape(devices.shape[0] // 2, 2, devices.shape[1]), ("chip", "core", "head")
        ),
        in_specs=(rows, rows, rows, rows, rows, P(("chip", "core"))),
        out_specs=P(("chip", "core"), "head"),
        check_vma=False,
    )
```

```python
import jax
import jax.numpy as jnp
from jax import lax
from jax.experimental import pallas as pl
from jax.experimental.pallas import tpu as pltpu
from jax.sharding import Mesh
from jax.sharding import PartitionSpec as P

DK = 128
DV = 128
NH = 2
TOK = 32
CHUNK = 2 * TOK
REFL = CHUNK * NH
GROUP = 8
EPSILON = 1e-06

KEY_ROWS = NH * TOK
SCALE_ROWS = 16

BF16 = jnp.bfloat16
F32 = jnp.float32
NT = (((1,), (1,)), ((), ()))


def iota(shape, axis):
    return lax.broadcasted_iota(jnp.int32, shape, axis)


def dot(left, right):
    return jnp.dot(left, right, preferred_element_type=F32)


def dot_nt(left, right):
    return lax.dot_general(left, right, NT, preferred_element_type=F32)


def split(value):
    high = value.astype(BF16)
    low = (value - high.astype(F32)).astype(BF16)
    return high, low


def beside(value):
    return jnp.concatenate(split(value), 1)


def twice(value):
    return jnp.concatenate([value, value], 0)


def factor(value):
    return factor_of(*split(value))


def factor_of(high, low):
    return jnp.concatenate(
        [jnp.concatenate([high, low], 1), jnp.concatenate([high, jnp.zeros_like(low)], 1)], 0
    )


def product(left_pair, right_factor):
    both = dot(left_pair, right_factor)
    half = both.shape[1] // 2
    return both[:, :half] + both[:, half:]


def place(index):
    block = index // (NH * TOK)
    step = (index // TOK) % NH
    token = index % TOK
    return block, step, token, (block * TOK + token) * NH + step


def scale_maps():
    shape = (REFL, 8 * TOK)
    block, step, token, _ = place(iota(shape, 0))
    column = iota(shape, 1)
    source_block = column // (4 * TOK)
    kind = (column // TOK) % 4
    source = source_block * TOK + column % TOK
    now = block * TOK + token
    decay = (kind == NH) & (source <= now)
    segment = (kind == NH + 1) & (source <= now)
    beta = (kind == step) & (source == now)
    return jnp.concatenate([part.astype(F32) for part in (decay, segment, beta)], 0).astype(BF16)


def piece_rows(size):
    if size == TOK:
        return [slice(NH * TOK, 2 * NH * TOK)]
    return [
        slice(start, start + size)
        for part in range(2 * NH)
        for start in range(part * TOK + size, (part + 1) * TOK, 2 * size)
    ]


def taken(value, slices):
    return jnp.concatenate([value[each] for each in slices], 0) if len(slices) > 1 else value[slices[0]]


def put(base, rows, slices):
    pieces = []
    at = 0
    done = 0
    for each in slices:
        if each.start > at:
            pieces.append(base[at : each.start])
        size = each.stop - each.start
        pieces.append(base[each] + rows[done : done + size])
        done += size
        at = each.stop
    if at < REFL:
        pieces.append(base[at:])
    return jnp.concatenate(pieces, 0)


def inverses(lowers):
    small = 8
    count = len(lowers)
    lane = iota((small, REFL), 1)
    group_of = (lane // (NH * TOK)) * (TOK // small) + (lane % TOK) // small
    groups = [(block, piece) for block in range(2) for piece in range(TOK // small)]

    def start_row(block, step, piece):
        return block * NH * TOK + step * TOK + piece * small

    folded = []
    for lower in lowers:
        for step in range(NH):
            rows = jnp.zeros((small, REFL), F32)
            for number, (block, piece) in enumerate(groups):
                first = start_row(block, step, piece)
                rows = jnp.where(group_of == number, lower[first : first + small], rows)
            folded.append(rows)
    height = NH * small
    lower_fold = jnp.concatenate(folded, 0)
    wide = iota((count * height, REFL), 1)
    high = iota((count * height, REFL), 0) % height
    inverse = ((wide // TOK) % NH == high // small) & (wide % small == high % small)
    inverse = inverse.astype(F32).reshape(count, height, REFL)
    for token in range(small):
        for step in range(NH):
            if token == small - 1 and step == NH - 1:
                continue
            source = (wide // (NH * TOK)) * (NH * TOK) + step * TOK + (wide % TOK) // small * small + token
            column = jnp.take_along_axis(lower_fold, source, axis=1, mode="promise_in_bounds")
            row = step * small + token
            inverse = inverse - column.reshape(count, height, REFL) * inverse[:, row : row + 1, :]
    results = []
    for number in range(count):
        pieces = []
        for block in range(2):
            for step in range(NH):
                rows = inverse[number, step * small : (step + 1) * small]
                for piece in range(TOK // small):
                    mine = group_of == block * (TOK // small) + piece
                    pieces.append(jnp.where(mine, rows, 0.0))
        results.append(jnp.concatenate(pieces, 0))
    size = small
    zero = jnp.zeros((REFL, REFL), F32)
    while size < CHUNK:
        slices = piece_rows(size)
        row_block, _, row_token, _ = place(iota((REFL, REFL), 0))
        column_block, _, column_token, _ = place(iota((REFL, REFL), 1))
        row_piece = (row_block * TOK + row_token) // size
        column_piece = (column_block * TOK + column_token) // size
        linked = taken(row_piece, slices) == taken(column_piece, slices) + 1
        crossings = [
            product(beside(jnp.where(linked, taken(lower, slices), 0.0)), factor(result))
            for lower, result in zip(lowers, results)
        ]
        changes = [
            product(beside(taken(result, slices)), factor(put(zero, crossing, slices)))
            for crossing, result in zip(crossings, results)
        ]
        results = [put(result, -change, slices) for change, result in zip(changes, results)]
        size *= 2
    return results


def read_rows(value):
    return jnp.concatenate(
        [
            value[(NH - 1) * TOK : NH * TOK],
            value[(2 * NH - 1) * TOK : 2 * NH * TOK],
        ],
        0,
    )


def call(kernel, outs, *args, scratch=(), flops=0, far=0, after=(), name=None):
    count = len(args)

    def body(*refs):
        kernel(*refs[:count], *refs[count + len(after) :])

    specs = [pl.BlockSpec(memory_space=pltpu.HBM)] * far
    specs += [pl.BlockSpec(memory_space=pltpu.VMEM)] * (count - far)
    specs += [pl.BlockSpec(memory_space=pl.ANY)] * len(after)
    return pl.pallas_call(
        body,
        out_shape=outs,
        in_specs=specs,
        scratch_shapes=scratch,
        compiler_params=pltpu.CompilerParams(vmem_limit_bytes=24 * 2**20),
        cost_estimate=pl.CostEstimate(flops=flops, bytes_accessed=0, transcendentals=0),
        name=name,
    )(*args, *after)


def shape(*sizes, dtype=BF16):
    return jax.ShapeDtypeStruct(sizes, dtype)


def axis_index(axis):
    return lax.axis_index(axis).astype(jnp.int32)


def held(value, after):
    return pl.pallas_call(
        lambda *refs: None,
        out_shape=shape(*value.shape, dtype=value.dtype),
        in_specs=[pl.BlockSpec(memory_space=pl.ANY)] * (1 + len(after)),
        out_specs=pl.BlockSpec(memory_space=pl.ANY),
        input_output_aliases={0: 0},
        compiler_params=pltpu.CompilerParams(vmem_limit_bytes=2**20),
        name="held",
    )(value, *after)


class Sizes:
    def __init__(self, groups, group_heads, chips):
        self.groups = groups
        self.group_heads = group_heads
        self.heads = group_heads // 2
        self.chips = chips
        self.units = self.heads * groups
        self.swapped = chips == self.heads and chips & (chips - 1) == 0

    def unit(self, number):
        return number // self.groups, number % self.groups


def shifted(index, by, size):
    moved = index + by
    return jnp.where(moved >= size, moved - size, moved)


def block_columns(source, first, count):
    return [
        source[:, pl.ds(pl.multiple_of(first + number * DK, DK), DK)] for number in range(count)
    ]


def pack_keys(sizes, keys, betas, log_gates, starts):
    rows = sizes.heads * KEY_ROWS
    count = sizes.heads * NH

    def kernel(far_keys, far_betas, far_gates, far_starts, *refs):
        outs = refs[: sizes.groups]
        keys, betas, log_gates, starts, done = refs[sizes.groups :]
        width = sizes.group_heads * NH * DK
        pairs = [(far_betas, betas), (far_gates, log_gates), (far_starts, starts)]
        for group in range(sizes.groups):
            part = slice(group * width, (group + 1) * width)
            pairs.append((far_keys.at[:, part], keys.at[:, part]))
        copies = [
            pltpu.make_async_copy(far, near, done.at[number])
            for number, (far, near) in enumerate(pairs)
        ]
        for copy in copies:
            copy.start()
        for copy in copies:
            copy.wait()
        z = axis_index("head")
        core = axis_index("core")
        heads = log_gates.shape[1]
        pieces = []
        for step in range(NH):
            extent = (heads, heads * NH)
            pick = iota(extent, 1) == iota(extent, 0) * NH + step
            pieces.append(dot_nt(pick.astype(BF16), betas[...]))
        same = iota((heads, heads), 0) == iota((heads, heads), 1)
        pieces.append(dot_nt(same.astype(BF16), log_gates[...]))
        length = sizes.groups * TOK
        own = iota((length, TOK), 0) == z * TOK + iota((length, TOK), 1)
        own_starts = jnp.broadcast_to(starts[...].astype(F32), (heads, length)).astype(BF16)
        pieces.append(dot(own_starts, own.astype(BF16)))
        scales = jnp.concatenate(pieces, 1).astype(BF16)
        for ahead, out in enumerate(outs):
            target = shifted(z, ahead, sizes.groups)
            for side in range(2):
                owner = jnp.bitwise_xor(core, side)
                first = ((target * 2 + owner) * sizes.heads) * NH * DK
                for number, piece in enumerate(block_columns(keys, first, count)):
                    at = side * rows + number * TOK
                    out[at : at + TOK, :] = piece
            extent = (SCALE_ROWS, heads)
            pick = (iota(extent, 1) == target * sizes.group_heads + iota(extent, 0)) & (
                iota(extent, 0) < sizes.group_heads
            )
            out[2 * rows :, :] = dot(pick.astype(BF16), scales).astype(BF16)

    outs = [shape(2 * rows + SCALE_ROWS, DK)] * sizes.groups
    loaded = (keys, betas, log_gates, starts)
    scratch = [pltpu.VMEM(each.shape, each.dtype) for each in loaded]
    return call(
        kernel,
        outs,
        *[pltpu.with_memory_space_constraint(each, pltpu.HBM) for each in loaded],
        scratch=scratch + [pltpu.SemaphoreType.DMA((3 + sizes.groups,))],
        far=4,
        name="pack_keys",
    )


def swap_keys(sizes, arrived):
    rows = sizes.heads * KEY_ROWS

    def kernel(*refs):
        out = refs[-1]
        z = axis_index("head")
        for behind, piece in enumerate(refs[:-1]):
            source = shifted(z, sizes.groups - behind, sizes.groups) if behind else z
            out[source] = piece[rows:, :]

    return call(kernel, shape(sizes.groups, rows + SCALE_ROWS, DK), *arrived, name="swap_keys")


def pack_reads(sizes, values, queries):
    value_rows = sizes.heads * KEY_ROWS
    rows = value_rows + sizes.heads * TOK

    def kernel(values, queries, kept, sent):
        z = axis_index("head")
        core = axis_index("core")
        for ahead in range(sizes.groups):
            target = shifted(z, ahead, sizes.groups)
            for side, out in enumerate((kept, sent)):
                first = (target * 2 + jnp.bitwise_xor(core, side)) * sizes.heads * DK
                pieces = block_columns(values, first * NH, sizes.heads * NH)
                pieces += block_columns(queries, first, sizes.heads)
                for number, piece in enumerate(pieces):
                    out[ahead, number * TOK : (number + 1) * TOK, :] = piece

    return call(
        kernel,
        [shape(sizes.groups, rows, DK)] * 2,
        values,
        queries,
        name="pack_reads",
    )


def merge_reads(sizes, kept, swapped):
    value_rows = sizes.heads * KEY_ROWS
    query_rows = sizes.heads * TOK

    def kernel(kept, swapped, *outs):
        for ahead in range(sizes.groups):
            for side, source in enumerate((kept, swapped)):
                outs[ahead][side] = source[ahead, :value_rows, :]
                outs[sizes.groups + ahead][side] = source[ahead, value_rows:, :]

    outs = [shape(2, value_rows, DK)] * sizes.groups + [shape(2, query_rows, DK)] * sizes.groups
    merged = call(kernel, outs, kept, swapped, name="merge_reads")
    return merged[: sizes.groups], merged[sizes.groups :]


def gather(sizes, pieces, scratch):
    z = axis_index("head")
    core = axis_index("core")
    for behind, piece in enumerate(pieces):
        source = shifted(z, sizes.groups - behind, sizes.groups) if behind else z
        for side in range(2):
            scratch[jnp.bitwise_xor(core, side) * sizes.groups + source] = piece[side]


def unit_rows(scratch, head, chunk, count):
    first = head * count
    return jnp.concatenate(
        [
            scratch[2 * chunk, first : first + count, :],
            scratch[2 * chunk + 1, first : first + count, :],
        ],
        0,
    )


def key_stage(sizes, arrived, swapped):
    rows = sizes.heads * KEY_ROWS
    units = sizes.units
    groups = sizes.groups

    def kernel(*refs):
        pieces = refs[:groups]
        swapped = refs[groups]
        keys_out, inverse_out, end_out, ratio_out, row_out, step_out, prefix_out = refs[
            groups + 1 : groups + 8
        ]
        totals = refs[groups + 8 : groups + 8 + sizes.heads]
        blocks, scales, every = refs[groups + 8 + sizes.heads :]
        z = axis_index("head")
        core = axis_index("core")
        for behind, piece in enumerate(pieces):
            source = shifted(z, groups - behind, groups) if behind else z
            blocks[core * groups + source] = piece[:rows, :]
            scales[core * groups + source] = piece[2 * rows :, :]
        other = (1 - core) * groups
        for source in range(groups):
            blocks[other + source] = swapped[source, :rows, :]
            scales[other + source] = swapped[source, rows:, :]
        flat = scales[...].reshape(2 * groups * SCALE_ROWS, 4 * TOK)
        picks = []
        for block in range(2):
            extent = (units, 2 * groups * SCALE_ROWS)
            unit = iota(extent, 0)
            row = (unit % groups * 2 + block) * SCALE_ROWS + unit // groups
            pick = iota(extent, 1) == row + core * sizes.heads
            picks.append(dot(pick.astype(BF16), flat))
        by_unit = jnp.concatenate(picks, 1).astype(BF16)
        maps = scale_maps()
        as_rows = dot_nt(by_unit, maps)
        as_columns = dot_nt(maps, by_unit)
        decay_row, segment_row, beta_row = (
            as_rows[:, number * REFL : (number + 1) * REFL] for number in range(3)
        )
        decay_column, segment_column, beta_column = (
            as_columns[number * REFL : (number + 1) * REFL] for number in range(3)
        )
        carried_row = jnp.exp(decay_row) * (segment_row == 0).astype(F32)
        last = REFL - 1
        end_row = jnp.exp(decay_row[:, last:] - decay_row)
        end_row = end_row * (segment_row[:, last:] == segment_row).astype(F32)
        square = (REFL, REFL)
        _, _, _, row_time = place(iota(square, 0))
        _, _, _, column_time = place(iota(square, 1))
        causal = row_time >= column_time
        strict = row_time > column_time
        diagonal = row_time == column_time
        same = (iota((DK, DK), 0) == iota((DK, DK), 1)).astype(F32)
        row_out[0] = beta_row
        row_out[2] = carried_row
        for base in range(0, units, GROUP):
            members = range(base, min(base + GROUP, units))
            keys = [unit_rows(blocks, *sizes.unit(unit), KEY_ROWS) for unit in members]
            grams = [dot_nt(key, key) for key in keys]
            squares = [jnp.where(diagonal, gram, 0.0) for gram in grams]
            norm_rows = [lax.rsqrt(jnp.sum(each, 0, keepdims=True) + EPSILON) for each in squares]
            norm_columns = [
                lax.rsqrt(jnp.sum(each, 1, keepdims=True) + EPSILON) for each in squares
            ]
            lowers = []
            for number, unit in enumerate(members):
                keys_out[unit] = keys[number]
                one = slice(unit, unit + 1)
                linked = causal & (segment_column[:, one] == segment_row[one])
                gap = decay_column[:, one] - decay_row[one]
                ratio = jnp.where(linked, jnp.exp(jnp.minimum(gap, 0.0)), 0.0) * norm_rows[number]
                ratio_out[unit] = read_rows(ratio)
                strengths = beta_column[:, one] * norm_columns[number]
                lowers.append(jnp.where(strict, strengths * ratio * grams[number], 0.0))
            solved = inverses(lowers)
            pairs = [split(each) for each in solved]
            kept_rows = [
                beta_row[unit : unit + 1] * carried_row[unit : unit + 1] * norm
                for unit, norm in zip(members, norm_rows)
            ]
            turned_keys = [key.T for key in keys]
            ends = []
            for number, unit in enumerate(members):
                high, low = pairs[number]
                inverse_out[unit] = jnp.concatenate([high, low], 1)
                row_out[1, unit : unit + 1, :] = kept_rows[number]
                weights = end_row[unit : unit + 1] * norm_rows[number]
                ends.append(
                    product(
                        beside(turned_keys[number].astype(F32) * weights), factor_of(high, low)
                    )
                )
            for number, unit in enumerate(members):
                turned = turned_keys[number]
                end_out[unit] = beside(ends[number] * beta_row[unit : unit + 1])
                every[unit] = carried_row[unit : unit + 1, last:] * same - dot_nt(
                    jnp.concatenate([turned, turned], 1), beside(ends[number] * kept_rows[number])
                )
        prefixes = [same] * sizes.heads
        for chunk in range(groups):
            for head in range(sizes.heads):
                unit = head * groups + chunk
                step = every[unit]
                high, low = split(step)
                step_out[unit] = jnp.concatenate([high, low], 1)
                prefix_out[unit] = prefixes[head]
                if chunk == 0:
                    prefixes[head] = step
                else:
                    prefixes[head] = product(beside(prefixes[head]), factor_of(high, low))
        if sizes.swapped:
            for head in range(sizes.heads):
                every[head] = prefixes[head]
            chip = axis_index("chip")
            for number in range(sizes.heads):
                totals[number][...] = every[jnp.bitwise_xor(chip, number)]
        else:
            for head in range(sizes.heads):
                totals[head][...] = prefixes[head]

    outs = [
        shape(units, REFL, DK),
        shape(units, REFL, 2 * REFL),
        shape(units, DK, 2 * REFL),
        shape(units, CHUNK, REFL, dtype=F32),
        shape(3, units, REFL, dtype=F32),
        shape(units, DK, 2 * DK),
        shape(units, DK, DK, dtype=F32),
    ] + [shape(DK, DK, dtype=F32)] * sizes.heads
    scratch = [
        pltpu.VMEM((2 * groups, rows, DK), BF16),
        pltpu.VMEM((2 * groups, SCALE_ROWS, DK), BF16),
        pltpu.VMEM((units, DK, DK), F32),
    ]
    results = call(
        kernel, outs, *arrived, swapped, scratch=scratch, flops=6_000_000_000, name="key_stage"
    )
    return results[:7], results[7:]


def value_stage(sizes, pieces, ends, steps):
    groups = sizes.groups

    def kernel(*refs):
        pieces = refs[:groups]
        ends, steps, values_out, before_out = refs[groups : groups + 4]
        totals = refs[groups + 4 : groups + 4 + sizes.heads]
        blocks, every = refs[groups + 4 + sizes.heads :]
        gather(sizes, pieces, blocks)
        injects = []
        for unit in range(sizes.units):
            value = unit_rows(blocks, *sizes.unit(unit), KEY_ROWS)
            values_out[unit] = value
            turned = value.T
            injects.append(dot_nt(jnp.concatenate([turned, turned], 1), ends[unit]))
        sums = [jnp.zeros((DV, DK), F32)] * sizes.heads
        for chunk in range(groups):
            for head in range(sizes.heads):
                unit = head * groups + chunk
                before_out[unit] = sums[head]
                if chunk == 0:
                    sums[head] = injects[unit]
                else:
                    step = steps[unit]
                    sums[head] = injects[unit] + product(
                        beside(sums[head]), factor_of(step[:, :DK], step[:, DK:])
                    )
        if sizes.swapped:
            for head in range(sizes.heads):
                every[head] = sums[head]
            chip = axis_index("chip")
            for number in range(sizes.heads):
                totals[number][...] = every[jnp.bitwise_xor(chip, number)]
        else:
            for head in range(sizes.heads):
                totals[head][...] = sums[head]

    outs = [shape(sizes.units, REFL, DV), shape(sizes.units, DV, DK, dtype=F32)]
    outs += [shape(DV, DK, dtype=F32)] * sizes.heads
    scratch = [
        pltpu.VMEM((2 * groups, sizes.heads * KEY_ROWS, DV), BF16),
        pltpu.VMEM((sizes.heads, DV, DK), F32),
    ]
    results = call(
        kernel, outs, *pieces, ends, steps, scratch=scratch, flops=2_000_000_000, name="value_stage"
    )
    return results[0], results[1], results[2:]


def scan_states(sizes, transitions, injects):
    chips = sizes.chips

    def kernel(*refs):
        transitions = refs[:chips]
        injects = refs[chips : 2 * chips]
        outs = refs[2 * chips : 3 * chips]
        step, inject, entry = refs[3 * chips :]
        chip = axis_index("chip")
        for number in range(chips):
            source = jnp.bitwise_xor(chip, number)
            step[source] = transitions[number][...]
            inject[source] = injects[number][...]
        state = jnp.zeros((DV, DK), F32)
        for index in range(chips):
            entry[index] = state
            if index == 0:
                state = inject[index]
            elif index < chips - 1:
                state = product(beside(state), factor(step[index])) + inject[index]
        for number in range(chips):
            outs[number][...] = entry[jnp.bitwise_xor(chip, number)]

    scratch = [pltpu.VMEM((chips, DV, DK), F32)] * 3
    return call(
        kernel,
        [shape(DV, DK, dtype=F32)] * chips,
        *transitions,
        *injects,
        scratch=scratch,
        name="scan_states",
    )


def exchanged(sizes, parts):
    return [parts[0]] + [
        lax.ppermute(part, "chip", [(chip, chip ^ number) for chip in range(sizes.chips)])
        for number, part in enumerate(parts)
        if number
    ]


def entry_states(sizes, transitions, injects):
    if sizes.swapped:
        arrived = exchanged(sizes, transitions), exchanged(sizes, injects)
        return exchanged(sizes, scan_states(sizes, *arrived))
    transition = jnp.stack(transitions)
    inject = jnp.stack(injects)
    forward = [(chip, chip + 1) for chip in range(sizes.chips - 1)]

    def advance(_, entry):
        left = jnp.einsum("hvd,hde->hve", entry, transition, precision=lax.Precision.HIGHEST)
        return lax.ppermute(left + inject, "chip", forward)

    entry = lax.fori_loop(0, sizes.chips - 1, advance, jnp.zeros_like(inject))
    return [entry[head] for head in range(sizes.heads)]


def query_stage(sizes, pieces, values, before, keys, inverses_, ratios, rows, prefixes):
    groups = sizes.groups

    def kernel(*refs):
        pieces = refs[:groups]
        values, before, keys, inverse, ratio, rows, prefix, reader_out, inner_out, blocks = refs[
            groups:
        ]
        gather(sizes, pieces, blocks)
        for base in range(0, sizes.units, GROUP):
            members = range(base, min(base + GROUP, sizes.units))
            queries = [unit_rows(blocks, *sizes.unit(unit), TOK) for unit in members]
            scores = []
            for number, unit in enumerate(members):
                pair = inverse[unit]
                score = dot_nt(queries[number], keys[unit]) * ratio[unit]
                scores.append(product(beside(score), factor_of(pair[:, :REFL], pair[:, REFL:])))
            for number, unit in enumerate(members):
                one = slice(unit, unit + 1)
                inner = dot(beside(scores[number] * rows[0, one, :]), twice(values[unit]))
                carried = read_rows(jnp.broadcast_to(rows[2, one, :], (DK, REFL)).T)
                reader = carried * queries[number].astype(F32) - dot(
                    beside(scores[number] * rows[1, one, :]), twice(keys[unit])
                )
                high, low = split(jnp.concatenate([prefix[unit], before[unit]], 0))
                pair = beside(reader)
                both = dot_nt(pair, jnp.concatenate([high, high], 1)) + dot_nt(pair[:, :DK], low)
                reader_out[unit] = beside(both[:, :DK])
                inner_out[unit] = inner + both[:, DK:]

    outs = [
        shape(sizes.units, CHUNK, 2 * DK),
        shape(sizes.units, CHUNK, DV, dtype=F32),
    ]
    scratch = [pltpu.VMEM((2 * groups, sizes.heads * TOK, DK), BF16)]
    return call(
        kernel,
        outs,
        *pieces,
        values,
        before,
        keys,
        inverses_,
        ratios,
        rows,
        prefixes,
        scratch=scratch,
        flops=3_000_000_000,
        name="query_stage",
    )


def read_states(sizes, states, readers, inners):
    groups = sizes.groups
    half = groups // 2

    def kernel(*refs):
        states = refs[: sizes.heads]
        readers, inners, own, other, entry = refs[sizes.heads :]
        core = axis_index("core")
        chip = axis_index("chip") if sizes.swapped else 0
        for number in range(sizes.heads):
            place_ = jnp.bitwise_xor(chip, number) if sizes.swapped else number
            entry[place_] = states[number][...]
        for head in range(sizes.heads):
            high, low = split(entry[head])
            stack = jnp.concatenate(
                [
                    jnp.concatenate([high, high], 1),
                    jnp.concatenate([low, jnp.zeros_like(low)], 1),
                ],
                0,
            )
            for side, out in enumerate((own, other)):
                first = head * groups + jnp.bitwise_xor(core, side) * half
                pair = readers[pl.ds(first, half)].reshape(half * CHUNK, 2 * DK)
                both = dot_nt(pair, stack)
                inner = inners[pl.ds(first, half)].reshape(half * CHUNK, DV)
                result = inner + both[:, :DV] + both[:, DV:]
                out[:, head * DV : (head + 1) * DV] = result.astype(BF16)

    outs = [shape(half * CHUNK, sizes.heads * DV)] * 2
    scratch = [pltpu.VMEM((sizes.heads, DV, DK), F32)]
    return call(kernel, outs, *states, readers, inners, scratch=scratch, name="read_states")


def join(sizes, own, other):
    width = sizes.heads * DV

    def kernel(own, other, out):
        first = axis_index("core") * width
        out[:, pl.ds(pl.multiple_of(first, width), width)] = own[...]
        out[:, pl.ds(pl.multiple_of(width - first, width), width)] = other[...]

    return call(kernel, shape(own.shape[0], 2 * width), own, other, name="join")


def local(queries, keys, values, betas, log_gates, starts):
    groups = lax.axis_size("head")
    sizes = Sizes(groups, log_gates.shape[1] // groups, lax.axis_size("chip"))

    def spread(parts):
        return [parts[0]] + [
            lax.ppermute(part, "head", [(z, (z + ahead) % groups) for z in range(groups)])
            for ahead, part in enumerate(parts)
            if ahead
        ]

    def swapped(part):
        return lax.ppermute(part, "core", [(0, 1), (1, 0)])

    arrived = spread(pack_keys(sizes, keys, betas, log_gates, starts.reshape(1, -1)))
    kept, sent = pack_reads(sizes, values, queries)
    sent = held(sent, after=arrived[1:])
    value_parts, query_parts = merge_reads(sizes, kept, swapped(sent))
    value_parts = spread(value_parts)
    query_parts = spread(query_parts)
    other_keys = swapped(swap_keys(sizes, arrived))
    (unit_keys, inverse, ends, ratios, rows, steps, prefixes), transitions = key_stage(
        sizes, arrived, other_keys
    )
    unit_values, before, injects = value_stage(sizes, value_parts, ends, steps)
    states = entry_states(sizes, transitions, injects)
    readers, inners = query_stage(
        sizes, query_parts, unit_values, before, unit_keys, inverse, ratios, rows, prefixes
    )
    own, other = read_states(sizes, states, readers, inners)
    return join(sizes, own, swapped(other))


def solution(mesh):
    devices = mesh.devices
    rows = P(("chip", "core", "head"), None)
    return jax.shard_map(
        local,
        mesh=Mesh(
            devices.reshape(devices.shape[0] // 2, 2, devices.shape[1]), ("chip", "core", "head")
        ),
        in_specs=(rows, rows, rows, rows, rows, P(("chip", "core"))),
        out_specs=P(("chip", "core"), "head"),
        check_vma=False,
    )
```

```python
import jax
import jax.numpy as jnp
from jax import lax
from jax.experimental import pallas as pl
from jax.experimental.pallas import tpu as pltpu
from jax.sharding import Mesh
from jax.sharding import PartitionSpec as P

DK = 128
DV = 128
NH = 2
TOK = 32
CHUNK = 2 * TOK
REFL = CHUNK * NH
GROUP = 8
EPSILON = 1e-06

KEY_ROWS = NH * TOK
SCALE_ROWS = 16

BF16 = jnp.bfloat16
F32 = jnp.float32
NT = (((1,), (1,)), ((), ()))


def iota(shape, axis):
    return lax.broadcasted_iota(jnp.int32, shape, axis)


def dot(left, right):
    return jnp.dot(left, right, preferred_element_type=F32)


def dot_nt(left, right):
    return lax.dot_general(left, right, NT, preferred_element_type=F32)


def split(value):
    high = value.astype(BF16)
    low = (value - high.astype(F32)).astype(BF16)
    return high, low


def beside(value):
    return jnp.concatenate(split(value), 1)


def twice(value):
    return jnp.concatenate([value, value], 0)


def factor(value):
    return factor_of(*split(value))


def factor_of(high, low):
    return jnp.concatenate(
        [jnp.concatenate([high, low], 1), jnp.concatenate([high, jnp.zeros_like(low)], 1)], 0
    )


def product(left_pair, right_factor):
    both = dot(left_pair, right_factor)
    half = both.shape[1] // 2
    return both[:, :half] + both[:, half:]


def place(index):
    block = index // (NH * TOK)
    step = (index // TOK) % NH
    token = index % TOK
    return block, step, token, (block * TOK + token) * NH + step


def scale_maps():
    shape = (REFL, 8 * TOK)
    block, step, token, _ = place(iota(shape, 0))
    column = iota(shape, 1)
    source_block = column // (4 * TOK)
    kind = (column // TOK) % 4
    source = source_block * TOK + column % TOK
    now = block * TOK + token
    decay = (kind == NH) & (source <= now)
    segment = (kind == NH + 1) & (source <= now)
    beta = (kind == step) & (source == now)
    return jnp.concatenate([part.astype(F32) for part in (decay, segment, beta)], 0).astype(BF16)


def piece_rows(size):
    if size == TOK:
        return [slice(NH * TOK, 2 * NH * TOK)]
    return [
        slice(start, start + size)
        for part in range(2 * NH)
        for start in range(part * TOK + size, (part + 1) * TOK, 2 * size)
    ]


def taken(value, slices):
    return jnp.concatenate([value[each] for each in slices], 0) if len(slices) > 1 else value[slices[0]]


def put(base, rows, slices):
    pieces = []
    at = 0
    done = 0
    for each in slices:
        if each.start > at:
            pieces.append(base[at : each.start])
        size = each.stop - each.start
        pieces.append(base[each] + rows[done : done + size])
        done += size
        at = each.stop
    if at < REFL:
        pieces.append(base[at:])
    return jnp.concatenate(pieces, 0)


def inverses(lowers):
    small = 8
    count = len(lowers)
    lane = iota((small, REFL), 1)
    group_of = (lane // (NH * TOK)) * (TOK // small) + (lane % TOK) // small
    groups = [(block, piece) for block in range(2) for piece in range(TOK // small)]

    def start_row(block, step, piece):
        return block * NH * TOK + step * TOK + piece * small

    folded = []
    for lower in lowers:
        for step in range(NH):
            rows = jnp.zeros((small, REFL), F32)
            for number, (block, piece) in enumerate(groups):
                first = start_row(block, step, piece)
                rows = jnp.where(group_of == number, lower[first : first + small], rows)
            folded.append(rows)
    height = NH * small
    lower_fold = jnp.concatenate(folded, 0)
    wide = iota((count * height, REFL), 1)
    high = iota((count * height, REFL), 0) % height
    inverse = ((wide // TOK) % NH == high // small) & (wide % small == high % small)
    inverse = inverse.astype(F32).reshape(count, height, REFL)
    for token in range(small):
        for step in range(NH):
            if token == small - 1 and step == NH - 1:
                continue
            source = (wide // (NH * TOK)) * (NH * TOK) + step * TOK + (wide % TOK) // small * small + token
            column = jnp.take_along_axis(lower_fold, source, axis=1, mode="promise_in_bounds")
            row = step * small + token
            inverse = inverse - column.reshape(count, height, REFL) * inverse[:, row : row + 1, :]
    results = []
    for number in range(count):
        pieces = []
        for block in range(2):
            for step in range(NH):
                rows = inverse[number, step * small : (step + 1) * small]
                for piece in range(TOK // small):
                    mine = group_of == block * (TOK // small) + piece
                    pieces.append(jnp.where(mine, rows, 0.0))
        results.append(jnp.concatenate(pieces, 0))
    size = small
    zero = jnp.zeros((REFL, REFL), F32)
    while size < CHUNK:
        slices = piece_rows(size)
        row_block, _, row_token, _ = place(iota((REFL, REFL), 0))
        column_block, _, column_token, _ = place(iota((REFL, REFL), 1))
        row_piece = (row_block * TOK + row_token) // size
        column_piece = (column_block * TOK + column_token) // size
        linked = taken(row_piece, slices) == taken(column_piece, slices) + 1
        crossings = [
            product(beside(jnp.where(linked, taken(lower, slices), 0.0)), factor(result))
            for lower, result in zip(lowers, results)
        ]
        changes = [
            product(beside(taken(result, slices)), factor(put(zero, crossing, slices)))
            for crossing, result in zip(crossings, results)
        ]
        results = [put(result, -change, slices) for change, result in zip(changes, results)]
        size *= 2
    return results


def read_rows(value):
    return jnp.concatenate(
        [
            value[(NH - 1) * TOK : NH * TOK],
            value[(2 * NH - 1) * TOK : 2 * NH * TOK],
        ],
        0,
    )


def call(kernel, outs, *args, scratch=(), flops=0, far=0, name=None):
    specs = [pl.BlockSpec(memory_space=pltpu.HBM)] * far
    specs += [pl.BlockSpec(memory_space=pltpu.VMEM)] * (len(args) - far)
    return pl.pallas_call(
        kernel,
        out_shape=outs,
        in_specs=specs,
        scratch_shapes=scratch,
        compiler_params=pltpu.CompilerParams(vmem_limit_bytes=24 * 2**20),
        cost_estimate=pl.CostEstimate(flops=flops, bytes_accessed=0, transcendentals=0),
        name=name,
    )(*args)


def shape(*sizes, dtype=BF16):
    return jax.ShapeDtypeStruct(sizes, dtype)


def axis_index(axis):
    return lax.axis_index(axis).astype(jnp.int32)


class Sizes:
    def __init__(self, groups, group_heads, chips):
        self.groups = groups
        self.group_heads = group_heads
        self.heads = group_heads // 2
        self.chips = chips
        self.units = self.heads * groups
        self.distances = [0] + sorted(range(1, groups), key=lambda ahead: abs(2 * ahead - groups))
        self.swapped = chips == self.heads and chips & (chips - 1) == 0

    def unit(self, number):
        return number // self.groups, number % self.groups


def shifted(index, by, size):
    moved = index + by
    return jnp.where(moved >= size, moved - size, moved)


def block_columns(source, first, count):
    return [
        source[:, pl.ds(pl.multiple_of(first + number * DK, DK), DK)] for number in range(count)
    ]


def pack_keys(sizes, keys, betas, log_gates, starts):
    rows = sizes.heads * KEY_ROWS
    count = sizes.heads * NH

    def kernel(far_keys, far_betas, far_gates, far_starts, *refs):
        outs = refs[: sizes.groups]
        keys, betas, log_gates, starts, done = refs[sizes.groups :]
        width = sizes.group_heads * NH * DK
        pairs = [(far_betas, betas), (far_gates, log_gates), (far_starts, starts)]
        for group in range(sizes.groups):
            part = slice(group * width, (group + 1) * width)
            pairs.append((far_keys.at[:, part], keys.at[:, part]))
        copies = [
            pltpu.make_async_copy(far, near, done.at[number])
            for number, (far, near) in enumerate(pairs)
        ]
        for copy in copies:
            copy.start()
        for copy in copies:
            copy.wait()
        z = axis_index("head")
        core = axis_index("core")
        heads = log_gates.shape[1]
        pieces = []
        for step in range(NH):
            extent = (heads, heads * NH)
            pick = iota(extent, 1) == iota(extent, 0) * NH + step
            pieces.append(dot_nt(pick.astype(BF16), betas[...]))
        same = iota((heads, heads), 0) == iota((heads, heads), 1)
        pieces.append(dot_nt(same.astype(BF16), log_gates[...]))
        length = sizes.groups * TOK
        own = iota((length, TOK), 0) == z * TOK + iota((length, TOK), 1)
        own_starts = jnp.broadcast_to(starts[...].astype(F32), (heads, length)).astype(BF16)
        pieces.append(dot(own_starts, own.astype(BF16)))
        scales = jnp.concatenate(pieces, 1).astype(BF16)
        for ahead, out in zip(sizes.distances, outs):
            target = shifted(z, ahead, sizes.groups)
            for side in range(2):
                owner = jnp.bitwise_xor(core, side)
                first = ((target * 2 + owner) * sizes.heads) * NH * DK
                for number, piece in enumerate(block_columns(keys, first, count)):
                    at = side * rows + number * TOK
                    out[at : at + TOK, :] = piece
            extent = (SCALE_ROWS, heads)
            pick = (iota(extent, 1) == target * sizes.group_heads + iota(extent, 0)) & (
                iota(extent, 0) < sizes.group_heads
            )
            out[2 * rows :, :] = dot(pick.astype(BF16), scales).astype(BF16)

    outs = [shape(2 * rows + SCALE_ROWS, DK)] * sizes.groups
    loaded = (keys, betas, log_gates, starts)
    scratch = [pltpu.VMEM(each.shape, each.dtype) for each in loaded]
    return call(
        kernel,
        outs,
        *[pltpu.with_memory_space_constraint(each, pltpu.HBM) for each in loaded],
        scratch=scratch + [pltpu.SemaphoreType.DMA((3 + sizes.groups,))],
        far=4,
        name="pack_keys",
    )


def swap_keys(sizes, arrived):
    rows = sizes.heads * KEY_ROWS

    def kernel(*refs):
        out = refs[-1]
        z = axis_index("head")
        for behind, piece in zip(sizes.distances, refs[:-1]):
            source = shifted(z, sizes.groups - behind, sizes.groups) if behind else z
            out[source] = piece[rows:, :]

    return call(kernel, shape(sizes.groups, rows + SCALE_ROWS, DK), *arrived, name="swap_keys")


def pack_reads(sizes, values, queries):
    value_rows = sizes.heads * KEY_ROWS
    rows = value_rows + sizes.heads * TOK

    def kernel(values, queries, kept, sent):
        z = axis_index("head")
        core = axis_index("core")
        for ahead in range(sizes.groups):
            target = shifted(z, ahead, sizes.groups)
            for side, out in enumerate((kept, sent)):
                first = (target * 2 + jnp.bitwise_xor(core, side)) * sizes.heads * DK
                pieces = block_columns(values, first * NH, sizes.heads * NH)
                pieces += block_columns(queries, first, sizes.heads)
                for number, piece in enumerate(pieces):
                    out[ahead, number * TOK : (number + 1) * TOK, :] = piece

    return call(
        kernel, [shape(sizes.groups, rows, DK)] * 2, values, queries, name="pack_reads"
    )


def merge_reads(sizes, kept, swapped):
    value_rows = sizes.heads * KEY_ROWS
    query_rows = sizes.heads * TOK

    def kernel(kept, swapped, *outs):
        for number, ahead in enumerate(sizes.distances):
            for side, source in enumerate((kept, swapped)):
                outs[number][side] = source[ahead, :value_rows, :]
                outs[sizes.groups + number][side] = source[ahead, value_rows:, :]

    outs = [shape(2, value_rows, DK)] * sizes.groups + [shape(2, query_rows, DK)] * sizes.groups
    merged = call(kernel, outs, kept, swapped, name="merge_reads")
    return merged[: sizes.groups], merged[sizes.groups :]


def gather(sizes, pieces, scratch):
    z = axis_index("head")
    core = axis_index("core")
    for behind, piece in zip(sizes.distances, pieces):
        source = shifted(z, sizes.groups - behind, sizes.groups) if behind else z
        for side in range(2):
            scratch[jnp.bitwise_xor(core, side) * sizes.groups + source] = piece[side]


def unit_rows(scratch, head, chunk, count):
    first = head * count
    return jnp.concatenate(
        [
            scratch[2 * chunk, first : first + count, :],
            scratch[2 * chunk + 1, first : first + count, :],
        ],
        0,
    )


def key_stage(sizes, arrived, swapped):
    rows = sizes.heads * KEY_ROWS
    units = sizes.units
    groups = sizes.groups

    def kernel(*refs):
        pieces = refs[:groups]
        swapped = refs[groups]
        keys_out, inverse_out, end_out, ratio_out, row_out, step_out, prefix_out = refs[
            groups + 1 : groups + 8
        ]
        totals = refs[groups + 8 : groups + 8 + sizes.heads]
        blocks, scales, every = refs[groups + 8 + sizes.heads :]
        z = axis_index("head")
        core = axis_index("core")
        for behind, piece in zip(sizes.distances, pieces):
            source = shifted(z, groups - behind, groups) if behind else z
            blocks[core * groups + source] = piece[:rows, :]
            scales[core * groups + source] = piece[2 * rows :, :]
        other = (1 - core) * groups
        for source in range(groups):
            blocks[other + source] = swapped[source, :rows, :]
            scales[other + source] = swapped[source, rows:, :]
        flat = scales[...].reshape(2 * groups * SCALE_ROWS, 4 * TOK)
        picks = []
        for block in range(2):
            extent = (units, 2 * groups * SCALE_ROWS)
            unit = iota(extent, 0)
            row = (unit % groups * 2 + block) * SCALE_ROWS + unit // groups
            pick = iota(extent, 1) == row + core * sizes.heads
            picks.append(dot(pick.astype(BF16), flat))
        by_unit = jnp.concatenate(picks, 1).astype(BF16)
        maps = scale_maps()
        as_rows = dot_nt(by_unit, maps)
        as_columns = dot_nt(maps, by_unit)
        decay_row, segment_row, beta_row = (
            as_rows[:, number * REFL : (number + 1) * REFL] for number in range(3)
        )
        decay_column, segment_column, beta_column = (
            as_columns[number * REFL : (number + 1) * REFL] for number in range(3)
        )
        carried_row = jnp.exp(decay_row) * (segment_row == 0).astype(F32)
        last = REFL - 1
        end_row = jnp.exp(decay_row[:, last:] - decay_row)
        end_row = end_row * (segment_row[:, last:] == segment_row).astype(F32)
        square = (REFL, REFL)
        _, _, _, row_time = place(iota(square, 0))
        _, _, _, column_time = place(iota(square, 1))
        causal = row_time >= column_time
        strict = row_time > column_time
        diagonal = row_time == column_time
        same = (iota((DK, DK), 0) == iota((DK, DK), 1)).astype(F32)
        row_out[0] = beta_row
        row_out[2] = carried_row
        for base in range(0, units, GROUP):
            members = range(base, min(base + GROUP, units))
            keys = [unit_rows(blocks, *sizes.unit(unit), KEY_ROWS) for unit in members]
            grams = [dot_nt(key, key) for key in keys]
            squares = [jnp.where(diagonal, gram, 0.0) for gram in grams]
            norm_rows = [lax.rsqrt(jnp.sum(each, 0, keepdims=True) + EPSILON) for each in squares]
            norm_columns = [
                lax.rsqrt(jnp.sum(each, 1, keepdims=True) + EPSILON) for each in squares
            ]
            lowers = []
            for number, unit in enumerate(members):
                keys_out[unit] = keys[number]
                one = slice(unit, unit + 1)
                linked = causal & (segment_column[:, one] == segment_row[one])
                gap = decay_column[:, one] - decay_row[one]
                ratio = jnp.where(linked, jnp.exp(jnp.minimum(gap, 0.0)), 0.0) * norm_rows[number]
                ratio_out[unit] = read_rows(ratio)
                strengths = beta_column[:, one] * norm_columns[number]
                lowers.append(jnp.where(strict, strengths * ratio * grams[number], 0.0))
            solved = inverses(lowers)
            pairs = [split(each) for each in solved]
            kept_rows = [
                beta_row[unit : unit + 1] * carried_row[unit : unit + 1] * norm
                for unit, norm in zip(members, norm_rows)
            ]
            turned_keys = [key.T for key in keys]
            ends = []
            for number, unit in enumerate(members):
                high, low = pairs[number]
                inverse_out[unit] = jnp.concatenate([high, low], 1)
                row_out[1, unit : unit + 1, :] = kept_rows[number]
                weights = end_row[unit : unit + 1] * norm_rows[number]
                ends.append(
                    product(
                        beside(turned_keys[number].astype(F32) * weights), factor_of(high, low)
                    )
                )
            for number, unit in enumerate(members):
                turned = turned_keys[number]
                end_out[unit] = beside(ends[number] * beta_row[unit : unit + 1])
                every[unit] = carried_row[unit : unit + 1, last:] * same - dot_nt(
                    jnp.concatenate([turned, turned], 1), beside(ends[number] * kept_rows[number])
                )
        prefixes = [same] * sizes.heads
        for chunk in range(groups):
            for head in range(sizes.heads):
                unit = head * groups + chunk
                step = every[unit]
                high, low = split(step)
                step_out[unit] = jnp.concatenate([high, low], 1)
                prefix_out[unit] = prefixes[head]
                if chunk == 0:
                    prefixes[head] = step
                else:
                    prefixes[head] = product(beside(prefixes[head]), factor_of(high, low))
        if sizes.swapped:
            for head in range(sizes.heads):
                every[head] = prefixes[head]
            chip = axis_index("chip")
            for number in range(sizes.heads):
                totals[number][...] = every[jnp.bitwise_xor(chip, number)]
        else:
            for head in range(sizes.heads):
                totals[head][...] = prefixes[head]

    outs = [
        shape(units, REFL, DK),
        shape(units, REFL, 2 * REFL),
        shape(units, DK, 2 * REFL),
        shape(units, CHUNK, REFL, dtype=F32),
        shape(3, units, REFL, dtype=F32),
        shape(units, DK, 2 * DK),
        shape(units, DK, DK, dtype=F32),
    ] + [shape(DK, DK, dtype=F32)] * sizes.heads
    scratch = [
        pltpu.VMEM((2 * groups, rows, DK), BF16),
        pltpu.VMEM((2 * groups, SCALE_ROWS, DK), BF16),
        pltpu.VMEM((units, DK, DK), F32),
    ]
    results = call(
        kernel, outs, *arrived, swapped, scratch=scratch, flops=6_000_000_000, name="key_stage"
    )
    return results[:7], results[7:]


def value_stage(sizes, pieces, ends, steps):
    groups = sizes.groups

    def kernel(*refs):
        pieces = refs[:groups]
        ends, steps, values_out, before_out = refs[groups : groups + 4]
        totals = refs[groups + 4 : groups + 4 + sizes.heads]
        blocks, every = refs[groups + 4 + sizes.heads :]
        gather(sizes, pieces, blocks)
        injects = []
        for unit in range(sizes.units):
            value = unit_rows(blocks, *sizes.unit(unit), KEY_ROWS)
            values_out[unit] = value
            turned = value.T
            injects.append(dot_nt(jnp.concatenate([turned, turned], 1), ends[unit]))
        sums = [jnp.zeros((DV, DK), F32)] * sizes.heads
        for chunk in range(groups):
            for head in range(sizes.heads):
                unit = head * groups + chunk
                before_out[unit] = sums[head]
                if chunk == 0:
                    sums[head] = injects[unit]
                else:
                    step = steps[unit]
                    sums[head] = injects[unit] + product(
                        beside(sums[head]), factor_of(step[:, :DK], step[:, DK:])
                    )
        if sizes.swapped:
            for head in range(sizes.heads):
                every[head] = sums[head]
            chip = axis_index("chip")
            for number in range(sizes.heads):
                totals[number][...] = every[jnp.bitwise_xor(chip, number)]
        else:
            for head in range(sizes.heads):
                totals[head][...] = sums[head]

    outs = [shape(sizes.units, REFL, DV), shape(sizes.units, DV, DK, dtype=F32)]
    outs += [shape(DV, DK, dtype=F32)] * sizes.heads
    scratch = [
        pltpu.VMEM((2 * groups, sizes.heads * KEY_ROWS, DV), BF16),
        pltpu.VMEM((sizes.heads, DV, DK), F32),
    ]
    results = call(
        kernel, outs, *pieces, ends, steps, scratch=scratch, flops=2_000_000_000, name="value_stage"
    )
    return results[0], results[1], results[2:]


def scan_states(sizes, transitions, injects):
    chips = sizes.chips

    def kernel(*refs):
        transitions = refs[:chips]
        injects = refs[chips : 2 * chips]
        outs = refs[2 * chips : 3 * chips]
        step, inject, entry = refs[3 * chips :]
        chip = axis_index("chip")
        for number in range(chips):
            source = jnp.bitwise_xor(chip, number)
            step[source] = transitions[number][...]
            inject[source] = injects[number][...]
        state = jnp.zeros((DV, DK), F32)
        for index in range(chips):
            entry[index] = state
            if index == 0:
                state = inject[index]
            elif index < chips - 1:
                state = product(beside(state), factor(step[index])) + inject[index]
        for number in range(chips):
            outs[number][...] = entry[jnp.bitwise_xor(chip, number)]

    scratch = [pltpu.VMEM((chips, DV, DK), F32)] * 3
    return call(
        kernel,
        [shape(DV, DK, dtype=F32)] * chips,
        *transitions,
        *injects,
        scratch=scratch,
        name="scan_states",
    )


def exchanged(sizes, parts):
    return [parts[0]] + [
        lax.ppermute(part, "chip", [(chip, chip ^ number) for chip in range(sizes.chips)])
        for number, part in enumerate(parts)
        if number
    ]


def entry_states(sizes, transitions, injects):
    if sizes.swapped:
        arrived = exchanged(sizes, transitions), exchanged(sizes, injects)
        return exchanged(sizes, scan_states(sizes, *arrived))
    transition = jnp.stack(transitions)
    inject = jnp.stack(injects)
    forward = [(chip, chip + 1) for chip in range(sizes.chips - 1)]

    def advance(_, entry):
        left = jnp.einsum("hvd,hde->hve", entry, transition, precision=lax.Precision.HIGHEST)
        return lax.ppermute(left + inject, "chip", forward)

    entry = lax.fori_loop(0, sizes.chips - 1, advance, jnp.zeros_like(inject))
    return [entry[head] for head in range(sizes.heads)]


def query_stage(sizes, pieces, values, before, keys, inverses_, ratios, rows, prefixes):
    groups = sizes.groups

    def kernel(*refs):
        pieces = refs[:groups]
        values, before, keys, inverse, ratio, rows, prefix, reader_out, inner_out, blocks = refs[
            groups:
        ]
        gather(sizes, pieces, blocks)
        for base in range(0, sizes.units, GROUP):
            members = range(base, min(base + GROUP, sizes.units))
            queries = [unit_rows(blocks, *sizes.unit(unit), TOK) for unit in members]
            scores = []
            for number, unit in enumerate(members):
                pair = inverse[unit]
                score = dot_nt(queries[number], keys[unit]) * ratio[unit]
                scores.append(product(beside(score), factor_of(pair[:, :REFL], pair[:, REFL:])))
            for number, unit in enumerate(members):
                one = slice(unit, unit + 1)
                inner = dot(beside(scores[number] * rows[0, one, :]), twice(values[unit]))
                carried = read_rows(jnp.broadcast_to(rows[2, one, :], (DK, REFL)).T)
                reader = carried * queries[number].astype(F32) - dot(
                    beside(scores[number] * rows[1, one, :]), twice(keys[unit])
                )
                high, low = split(jnp.concatenate([prefix[unit], before[unit]], 0))
                pair = beside(reader)
                both = dot_nt(pair, jnp.concatenate([high, high], 1)) + dot_nt(pair[:, :DK], low)
                reader_out[unit] = beside(both[:, :DK])
                inner_out[unit] = inner + both[:, DK:]

    outs = [
        shape(sizes.units, CHUNK, 2 * DK),
        shape(sizes.units, CHUNK, DV, dtype=F32),
    ]
    scratch = [pltpu.VMEM((2 * groups, sizes.heads * TOK, DK), BF16)]
    return call(
        kernel,
        outs,
        *pieces,
        values,
        before,
        keys,
        inverses_,
        ratios,
        rows,
        prefixes,
        scratch=scratch,
        flops=3_000_000_000,
        name="query_stage",
    )


def read_states(sizes, states, readers, inners):
    groups = sizes.groups
    half = groups // 2

    def kernel(*refs):
        states = refs[: sizes.heads]
        readers, inners, own, other, entry = refs[sizes.heads :]
        core = axis_index("core")
        chip = axis_index("chip") if sizes.swapped else 0
        for number in range(sizes.heads):
            place_ = jnp.bitwise_xor(chip, number) if sizes.swapped else number
            entry[place_] = states[number][...]
        for head in range(sizes.heads):
            high, low = split(entry[head])
            stack = jnp.concatenate(
                [
                    jnp.concatenate([high, high], 1),
                    jnp.concatenate([low, jnp.zeros_like(low)], 1),
                ],
                0,
            )
            for side, out in enumerate((own, other)):
                first = head * groups + jnp.bitwise_xor(core, side) * half
                pair = readers[pl.ds(first, half)].reshape(half * CHUNK, 2 * DK)
                both = dot_nt(pair, stack)
                inner = inners[pl.ds(first, half)].reshape(half * CHUNK, DV)
                result = inner + both[:, :DV] + both[:, DV:]
                out[:, head * DV : (head + 1) * DV] = result.astype(BF16)

    outs = [shape(half * CHUNK, sizes.heads * DV)] * 2
    scratch = [pltpu.VMEM((sizes.heads, DV, DK), F32)]
    return call(kernel, outs, *states, readers, inners, scratch=scratch, name="read_states")


def join(sizes, own, other):
    width = sizes.heads * DV

    def kernel(own, other, out):
        first = axis_index("core") * width
        out[:, pl.ds(pl.multiple_of(first, width), width)] = own[...]
        out[:, pl.ds(pl.multiple_of(width - first, width), width)] = other[...]

    return call(kernel, shape(own.shape[0], 2 * width), own, other, name="join")


def local(queries, keys, values, betas, log_gates, starts):
    groups = lax.axis_size("head")
    sizes = Sizes(groups, log_gates.shape[1] // groups, lax.axis_size("chip"))

    def spread(parts):
        return [parts[0]] + [
            lax.ppermute(part, "head", [(z, (z + ahead) % groups) for z in range(groups)])
            for ahead, part in zip(sizes.distances[1:], parts[1:])
        ]

    def swapped(part):
        return lax.ppermute(part, "core", [(0, 1), (1, 0)])

    arrived = spread(pack_keys(sizes, keys, betas, log_gates, starts.reshape(1, -1)))
    kept, sent = pack_reads(sizes, values, queries)
    value_parts, query_parts = merge_reads(sizes, kept, swapped(sent))
    value_parts = spread(value_parts)
    query_parts = spread(query_parts)
    other_keys = swapped(swap_keys(sizes, arrived))
    (unit_keys, inverse, ends, ratios, rows, steps, prefixes), transitions = key_stage(
        sizes, arrived, other_keys
    )
    unit_values, before, injects = value_stage(sizes, value_parts, ends, steps)
    states = entry_states(sizes, transitions, injects)
    readers, inners = query_stage(
        sizes, query_parts, unit_values, before, unit_keys, inverse, ratios, rows, prefixes
    )
    own, other = read_states(sizes, states, readers, inners)
    return join(sizes, own, swapped(other))


def solution(mesh):
    devices = mesh.devices
    rows = P(("chip", "core", "head"), None)
    return jax.shard_map(
        local,
        mesh=Mesh(
            devices.reshape(devices.shape[0] // 2, 2, devices.shape[1]), ("chip", "core", "head")
        ),
        in_specs=(rows, rows, rows, rows, rows, P(("chip", "core"))),
        out_specs=P(("chip", "core"), "head"),
        check_vma=False,
    )
```

```python
import jax
import jax.numpy as jnp
from jax import lax
from jax.experimental import pallas as pl
from jax.experimental.pallas import tpu as pltpu
from jax.sharding import Mesh
from jax.sharding import PartitionSpec as P

DK = 128
DV = 128
NH = 2
TOK = 32
CHUNK = 2 * TOK
REFL = CHUNK * NH
GROUP = 8
EPSILON = 1e-06

KEY_ROWS = NH * TOK
SCALE_ROWS = 16

BF16 = jnp.bfloat16
F32 = jnp.float32
NT = (((1,), (1,)), ((), ()))


def iota(shape, axis):
    return lax.broadcasted_iota(jnp.int32, shape, axis)


def dot(left, right):
    return jnp.dot(left, right, preferred_element_type=F32)


def dot_nt(left, right):
    return lax.dot_general(left, right, NT, preferred_element_type=F32)


def split(value):
    high = value.astype(BF16)
    low = (value - high.astype(F32)).astype(BF16)
    return high, low


def beside(value):
    return jnp.concatenate(split(value), 1)


def twice(value):
    return jnp.concatenate([value, value], 0)


def factor(value):
    return factor_of(*split(value))


def factor_of(high, low):
    return jnp.concatenate(
        [jnp.concatenate([high, low], 1), jnp.concatenate([high, jnp.zeros_like(low)], 1)], 0
    )


def product(left_pair, right_factor):
    both = dot(left_pair, right_factor)
    half = both.shape[1] // 2
    return both[:, :half] + both[:, half:]


def place(index):
    block = index // (NH * TOK)
    step = (index // TOK) % NH
    token = index % TOK
    return block, step, token, (block * TOK + token) * NH + step


def scale_maps():
    shape = (REFL, 8 * TOK)
    block, step, token, _ = place(iota(shape, 0))
    column = iota(shape, 1)
    source_block = column // (4 * TOK)
    kind = (column // TOK) % 4
    source = source_block * TOK + column % TOK
    now = block * TOK + token
    decay = (kind == NH) & (source <= now)
    segment = (kind == NH + 1) & (source <= now)
    beta = (kind == step) & (source == now)
    return jnp.concatenate([part.astype(F32) for part in (decay, segment, beta)], 0).astype(BF16)


def piece_rows(size):
    if size == TOK:
        return [slice(NH * TOK, 2 * NH * TOK)]
    return [
        slice(start, start + size)
        for part in range(2 * NH)
        for start in range(part * TOK + size, (part + 1) * TOK, 2 * size)
    ]


def taken(value, slices):
    return jnp.concatenate([value[each] for each in slices], 0) if len(slices) > 1 else value[slices[0]]


def put(base, rows, slices):
    pieces = []
    at = 0
    done = 0
    for each in slices:
        if each.start > at:
            pieces.append(base[at : each.start])
        size = each.stop - each.start
        pieces.append(base[each] + rows[done : done + size])
        done += size
        at = each.stop
    if at < REFL:
        pieces.append(base[at:])
    return jnp.concatenate(pieces, 0)


def inverses(lowers):
    small = 8
    count = len(lowers)
    lane = iota((small, REFL), 1)
    group_of = (lane // (NH * TOK)) * (TOK // small) + (lane % TOK) // small
    groups = [(block, piece) for block in range(2) for piece in range(TOK // small)]

    def start_row(block, step, piece):
        return block * NH * TOK + step * TOK + piece * small

    folded = []
    for lower in lowers:
        for step in range(NH):
            rows = jnp.zeros((small, REFL), F32)
            for number, (block, piece) in enumerate(groups):
                first = start_row(block, step, piece)
                rows = jnp.where(group_of == number, lower[first : first + small], rows)
            folded.append(rows)
    height = NH * small
    lower_fold = jnp.concatenate(folded, 0)
    wide = iota((count * height, REFL), 1)
    high = iota((count * height, REFL), 0) % height
    inverse = ((wide // TOK) % NH == high // small) & (wide % small == high % small)
    inverse = inverse.astype(F32).reshape(count, height, REFL)
    for token in range(small):
        for step in range(NH):
            if token == small - 1 and step == NH - 1:
                continue
            source = (wide // (NH * TOK)) * (NH * TOK) + step * TOK + (wide % TOK) // small * small + token
            column = jnp.take_along_axis(lower_fold, source, axis=1, mode="promise_in_bounds")
            row = step * small + token
            inverse = inverse - column.reshape(count, height, REFL) * inverse[:, row : row + 1, :]
    results = []
    for number in range(count):
        pieces = []
        for block in range(2):
            for step in range(NH):
                rows = inverse[number, step * small : (step + 1) * small]
                for piece in range(TOK // small):
                    mine = group_of == block * (TOK // small) + piece
                    pieces.append(jnp.where(mine, rows, 0.0))
        results.append(jnp.concatenate(pieces, 0))
    size = small
    zero = jnp.zeros((REFL, REFL), F32)
    while size < CHUNK:
        slices = piece_rows(size)
        row_block, _, row_token, _ = place(iota((REFL, REFL), 0))
        column_block, _, column_token, _ = place(iota((REFL, REFL), 1))
        row_piece = (row_block * TOK + row_token) // size
        column_piece = (column_block * TOK + column_token) // size
        linked = taken(row_piece, slices) == taken(column_piece, slices) + 1
        crossings = [
            product(beside(jnp.where(linked, taken(lower, slices), 0.0)), factor(result))
            for lower, result in zip(lowers, results)
        ]
        changes = [
            product(beside(taken(result, slices)), factor(put(zero, crossing, slices)))
            for crossing, result in zip(crossings, results)
        ]
        results = [put(result, -change, slices) for change, result in zip(changes, results)]
        size *= 2
    return results


def read_rows(value):
    return jnp.concatenate(
        [
            value[(NH - 1) * TOK : NH * TOK],
            value[(2 * NH - 1) * TOK : 2 * NH * TOK],
        ],
        0,
    )


def call(kernel, outs, *args, scratch=(), flops=0, far=0, after=(), name=None):
    count = len(args)

    def body(*refs):
        kernel(*refs[:count], *refs[count + len(after) :])

    specs = [pl.BlockSpec(memory_space=pltpu.HBM)] * far
    specs += [pl.BlockSpec(memory_space=pltpu.VMEM)] * (count - far)
    specs += [pl.BlockSpec(memory_space=pl.ANY)] * len(after)
    return pl.pallas_call(
        body,
        out_shape=outs,
        in_specs=specs,
        scratch_shapes=scratch,
        compiler_params=pltpu.CompilerParams(vmem_limit_bytes=24 * 2**20),
        cost_estimate=pl.CostEstimate(flops=flops, bytes_accessed=0, transcendentals=0),
        name=name,
    )(*args, *after)


def shape(*sizes, dtype=BF16):
    return jax.ShapeDtypeStruct(sizes, dtype)


def axis_index(axis):
    return lax.axis_index(axis).astype(jnp.int32)


class Sizes:
    def __init__(self, groups, group_heads, chips):
        self.groups = groups
        self.group_heads = group_heads
        self.heads = group_heads // 2
        self.chips = chips
        self.units = self.heads * groups
        self.swapped = chips == self.heads and chips & (chips - 1) == 0

    def unit(self, number):
        return number // self.groups, number % self.groups


def shifted(index, by, size):
    moved = index + by
    return jnp.where(moved >= size, moved - size, moved)


def block_columns(source, first, count):
    return [
        source[:, pl.ds(pl.multiple_of(first + number * DK, DK), DK)] for number in range(count)
    ]


def pack_keys(sizes, keys, betas, log_gates, starts):
    rows = sizes.heads * KEY_ROWS
    count = sizes.heads * NH

    def kernel(far_keys, far_betas, far_gates, far_starts, *refs):
        outs = refs[: sizes.groups]
        keys, betas, log_gates, starts, done = refs[sizes.groups :]
        width = sizes.group_heads * NH * DK
        pairs = [(far_betas, betas), (far_gates, log_gates), (far_starts, starts)]
        for group in range(sizes.groups):
            part = slice(group * width, (group + 1) * width)
            pairs.append((far_keys.at[:, part], keys.at[:, part]))
        copies = [
            pltpu.make_async_copy(far, near, done.at[number])
            for number, (far, near) in enumerate(pairs)
        ]
        for copy in copies:
            copy.start()
        for copy in copies:
            copy.wait()
        z = axis_index("head")
        core = axis_index("core")
        heads = log_gates.shape[1]
        pieces = []
        for step in range(NH):
            extent = (heads, heads * NH)
            pick = iota(extent, 1) == iota(extent, 0) * NH + step
            pieces.append(dot_nt(pick.astype(BF16), betas[...]))
        same = iota((heads, heads), 0) == iota((heads, heads), 1)
        pieces.append(dot_nt(same.astype(BF16), log_gates[...]))
        length = sizes.groups * TOK
        own = iota((length, TOK), 0) == z * TOK + iota((length, TOK), 1)
        own_starts = jnp.broadcast_to(starts[...].astype(F32), (heads, length)).astype(BF16)
        pieces.append(dot(own_starts, own.astype(BF16)))
        scales = jnp.concatenate(pieces, 1).astype(BF16)
        for ahead, out in enumerate(outs):
            target = shifted(z, ahead, sizes.groups)
            for side in range(2):
                owner = jnp.bitwise_xor(core, side)
                first = ((target * 2 + owner) * sizes.heads) * NH * DK
                for number, piece in enumerate(block_columns(keys, first, count)):
                    at = side * rows + number * TOK
                    out[at : at + TOK, :] = piece
            extent = (SCALE_ROWS, heads)
            pick = (iota(extent, 1) == target * sizes.group_heads + iota(extent, 0)) & (
                iota(extent, 0) < sizes.group_heads
            )
            out[2 * rows :, :] = dot(pick.astype(BF16), scales).astype(BF16)

    outs = [shape(2 * rows + SCALE_ROWS, DK)] * sizes.groups
    loaded = (keys, betas, log_gates, starts)
    scratch = [pltpu.VMEM(each.shape, each.dtype) for each in loaded]
    return call(
        kernel,
        outs,
        *[pltpu.with_memory_space_constraint(each, pltpu.HBM) for each in loaded],
        scratch=scratch + [pltpu.SemaphoreType.DMA((3 + sizes.groups,))],
        far=4,
        name="pack_keys",
    )


def swap_keys(sizes, arrived):
    rows = sizes.heads * KEY_ROWS

    def kernel(*refs):
        out = refs[-1]
        z = axis_index("head")
        for behind, piece in enumerate(refs[:-1]):
            source = shifted(z, sizes.groups - behind, sizes.groups) if behind else z
            out[source] = piece[rows:, :]

    return call(kernel, shape(sizes.groups, rows + SCALE_ROWS, DK), *arrived, name="swap_keys")


def pack_reads(sizes, values, queries):
    value_rows = sizes.heads * KEY_ROWS
    rows = value_rows + sizes.heads * TOK

    def kernel(values, queries, kept, sent):
        z = axis_index("head")
        core = axis_index("core")
        for ahead in range(sizes.groups):
            target = shifted(z, ahead, sizes.groups)
            for side, out in enumerate((kept, sent)):
                first = (target * 2 + jnp.bitwise_xor(core, side)) * sizes.heads * DK
                pieces = block_columns(values, first * NH, sizes.heads * NH)
                pieces += block_columns(queries, first, sizes.heads)
                for number, piece in enumerate(pieces):
                    out[ahead, number * TOK : (number + 1) * TOK, :] = piece

    return call(
        kernel, [shape(sizes.groups, rows, DK)] * 2, values, queries, name="pack_reads"
    )


def merge_reads(sizes, kept, swapped):
    value_rows = sizes.heads * KEY_ROWS
    query_rows = sizes.heads * TOK

    def kernel(kept, swapped, *outs):
        for ahead in range(sizes.groups):
            for side, source in enumerate((kept, swapped)):
                outs[ahead][side] = source[ahead, :value_rows, :]
                outs[sizes.groups + ahead][side] = source[ahead, value_rows:, :]

    outs = [shape(2, value_rows, DK)] * sizes.groups + [shape(2, query_rows, DK)] * sizes.groups
    merged = call(kernel, outs, kept, swapped, name="merge_reads")
    return merged[: sizes.groups], merged[sizes.groups :]


def gather(sizes, pieces, scratch):
    z = axis_index("head")
    core = axis_index("core")
    for behind, piece in enumerate(pieces):
        source = shifted(z, sizes.groups - behind, sizes.groups) if behind else z
        for side in range(2):
            scratch[jnp.bitwise_xor(core, side) * sizes.groups + source] = piece[side]


def unit_rows(scratch, head, chunk, count):
    first = head * count
    return jnp.concatenate(
        [
            scratch[2 * chunk, first : first + count, :],
            scratch[2 * chunk + 1, first : first + count, :],
        ],
        0,
    )


def key_stage(sizes, arrived, swapped):
    rows = sizes.heads * KEY_ROWS
    units = sizes.units
    groups = sizes.groups

    def kernel(*refs):
        pieces = refs[:groups]
        swapped = refs[groups]
        keys_out, inverse_out, end_out, ratio_out, row_out, step_out, prefix_out = refs[
            groups + 1 : groups + 8
        ]
        totals = refs[groups + 8 : groups + 8 + sizes.heads]
        blocks, scales, every = refs[groups + 8 + sizes.heads :]
        z = axis_index("head")
        core = axis_index("core")
        for behind, piece in enumerate(pieces):
            source = shifted(z, groups - behind, groups) if behind else z
            blocks[core * groups + source] = piece[:rows, :]
            scales[core * groups + source] = piece[2 * rows :, :]
        other = (1 - core) * groups
        for source in range(groups):
            blocks[other + source] = swapped[source, :rows, :]
            scales[other + source] = swapped[source, rows:, :]
        flat = scales[...].reshape(2 * groups * SCALE_ROWS, 4 * TOK)
        picks = []
        for block in range(2):
            extent = (units, 2 * groups * SCALE_ROWS)
            unit = iota(extent, 0)
            row = (unit % groups * 2 + block) * SCALE_ROWS + unit // groups
            pick = iota(extent, 1) == row + core * sizes.heads
            picks.append(dot(pick.astype(BF16), flat))
        by_unit = jnp.concatenate(picks, 1).astype(BF16)
        maps = scale_maps()
        as_rows = dot_nt(by_unit, maps)
        as_columns = dot_nt(maps, by_unit)
        decay_row, segment_row, beta_row = (
            as_rows[:, number * REFL : (number + 1) * REFL] for number in range(3)
        )
        decay_column, segment_column, beta_column = (
            as_columns[number * REFL : (number + 1) * REFL] for number in range(3)
        )
        carried_row = jnp.exp(decay_row) * (segment_row == 0).astype(F32)
        last = REFL - 1
        end_row = jnp.exp(decay_row[:, last:] - decay_row)
        end_row = end_row * (segment_row[:, last:] == segment_row).astype(F32)
        square = (REFL, REFL)
        _, _, _, row_time = place(iota(square, 0))
        _, _, _, column_time = place(iota(square, 1))
        causal = row_time >= column_time
        strict = row_time > column_time
        diagonal = row_time == column_time
        same = (iota((DK, DK), 0) == iota((DK, DK), 1)).astype(F32)
        row_out[0] = beta_row
        row_out[2] = carried_row
        for base in range(0, units, GROUP):
            members = range(base, min(base + GROUP, units))
            keys = [unit_rows(blocks, *sizes.unit(unit), KEY_ROWS) for unit in members]
            grams = [dot_nt(key, key) for key in keys]
            squares = [jnp.where(diagonal, gram, 0.0) for gram in grams]
            norm_rows = [lax.rsqrt(jnp.sum(each, 0, keepdims=True) + EPSILON) for each in squares]
            norm_columns = [
                lax.rsqrt(jnp.sum(each, 1, keepdims=True) + EPSILON) for each in squares
            ]
            lowers = []
            for number, unit in enumerate(members):
                keys_out[unit] = keys[number]
                one = slice(unit, unit + 1)
                linked = causal & (segment_column[:, one] == segment_row[one])
                gap = decay_column[:, one] - decay_row[one]
                ratio = jnp.where(linked, jnp.exp(jnp.minimum(gap, 0.0)), 0.0) * norm_rows[number]
                ratio_out[unit] = read_rows(ratio)
                strengths = beta_column[:, one] * norm_columns[number]
                lowers.append(jnp.where(strict, strengths * ratio * grams[number], 0.0))
            solved = inverses(lowers)
            pairs = [split(each) for each in solved]
            kept_rows = [
                beta_row[unit : unit + 1] * carried_row[unit : unit + 1] * norm
                for unit, norm in zip(members, norm_rows)
            ]
            turned_keys = [key.T for key in keys]
            ends = []
            for number, unit in enumerate(members):
                high, low = pairs[number]
                inverse_out[unit] = jnp.concatenate([high, low], 1)
                row_out[1, unit : unit + 1, :] = kept_rows[number]
                weights = end_row[unit : unit + 1] * norm_rows[number]
                ends.append(
                    product(
                        beside(turned_keys[number].astype(F32) * weights), factor_of(high, low)
                    )
                )
            for number, unit in enumerate(members):
                turned = turned_keys[number]
                end_out[unit] = beside(ends[number] * beta_row[unit : unit + 1])
                every[unit] = carried_row[unit : unit + 1, last:] * same - dot_nt(
                    jnp.concatenate([turned, turned], 1), beside(ends[number] * kept_rows[number])
                )
        prefixes = [same] * sizes.heads
        for chunk in range(groups):
            for head in range(sizes.heads):
                unit = head * groups + chunk
                step = every[unit]
                high, low = split(step)
                step_out[unit] = jnp.concatenate([high, low], 1)
                prefix_out[unit] = prefixes[head]
                if chunk == 0:
                    prefixes[head] = step
                else:
                    prefixes[head] = product(beside(prefixes[head]), factor_of(high, low))
        if sizes.swapped:
            for head in range(sizes.heads):
                every[head] = prefixes[head]
            chip = axis_index("chip")
            for number in range(sizes.heads):
                totals[number][...] = every[jnp.bitwise_xor(chip, number)]
        else:
            for head in range(sizes.heads):
                totals[head][...] = prefixes[head]

    outs = [
        shape(units, REFL, DK),
        shape(units, REFL, 2 * REFL),
        shape(units, DK, 2 * REFL),
        shape(units, CHUNK, REFL, dtype=F32),
        shape(3, units, REFL, dtype=F32),
        shape(units, DK, 2 * DK),
        shape(units, DK, DK, dtype=F32),
    ] + [shape(DK, DK, dtype=F32)] * sizes.heads
    scratch = [
        pltpu.VMEM((2 * groups, rows, DK), BF16),
        pltpu.VMEM((2 * groups, SCALE_ROWS, DK), BF16),
        pltpu.VMEM((units, DK, DK), F32),
    ]
    results = call(
        kernel, outs, *arrived, swapped, scratch=scratch, flops=6_000_000_000, name="key_stage"
    )
    return results[:7], results[7:]


def value_stage(sizes, pieces, ends, steps, transitions):
    groups = sizes.groups

    def kernel(*refs):
        pieces = refs[:groups]
        ends, steps = refs[groups : groups + 2]
        transitions = refs[groups + 2 : groups + 2 + sizes.heads]
        values_out, before_out, *totals, blocks, every = refs[groups + 2 + sizes.heads :]
        gather(sizes, pieces, blocks)
        injects = []
        for unit in range(sizes.units):
            value = unit_rows(blocks, *sizes.unit(unit), KEY_ROWS)
            values_out[unit] = value
            turned = value.T
            injects.append(dot_nt(jnp.concatenate([turned, turned], 1), ends[unit]))
        sums = [jnp.zeros((DV, DK), F32)] * sizes.heads
        for chunk in range(groups):
            for head in range(sizes.heads):
                unit = head * groups + chunk
                before_out[unit] = sums[head]
                if chunk == 0:
                    sums[head] = injects[unit]
                else:
                    step = steps[unit]
                    sums[head] = injects[unit] + product(
                        beside(sums[head]), factor_of(step[:, :DK], step[:, DK:])
                    )
        if sizes.swapped:
            for head in range(sizes.heads):
                every[head] = sums[head]
            chip = axis_index("chip")
            for number in range(sizes.heads):
                totals[number][0] = transitions[number][...]
                totals[number][1] = every[jnp.bitwise_xor(chip, number)]
        else:
            for head in range(sizes.heads):
                totals[head][0] = transitions[head][...]
                totals[head][1] = sums[head]

    outs = [shape(sizes.units, REFL, DV), shape(sizes.units, DV, DK, dtype=F32)]
    outs += [shape(2, DV, DK, dtype=F32)] * sizes.heads
    scratch = [
        pltpu.VMEM((2 * groups, sizes.heads * KEY_ROWS, DV), BF16),
        pltpu.VMEM((sizes.heads, DV, DK), F32),
    ]
    results = call(
        kernel, outs, *pieces, ends, steps, *transitions, scratch=scratch, name="value_stage"
    )
    return results[0], results[1], results[2:]


def scan_states(sizes, changes):
    chips = sizes.chips

    def kernel(*refs):
        changes = refs[:chips]
        outs = refs[chips : 2 * chips]
        step, inject, entry = refs[2 * chips :]
        chip = axis_index("chip")
        for number in range(chips):
            source = jnp.bitwise_xor(chip, number)
            step[source] = changes[number][0]
            inject[source] = changes[number][1]
        state = jnp.zeros((DV, DK), F32)
        for index in range(chips):
            entry[index] = state
            if index == 0:
                state = inject[index]
            elif index < chips - 1:
                state = product(beside(state), factor(step[index])) + inject[index]
        for number in range(chips):
            outs[number][...] = entry[jnp.bitwise_xor(chip, number)]

    scratch = [pltpu.VMEM((chips, DV, DK), F32)] * 3
    return call(
        kernel,
        [shape(DV, DK, dtype=F32)] * chips,
        *changes,
        scratch=scratch,
        name="scan_states",
    )


def exchanged(sizes, parts):
    return [parts[0]] + [
        lax.ppermute(part, "chip", [(chip, chip ^ number) for chip in range(sizes.chips)])
        for number, part in enumerate(parts)
        if number
    ]


def entry_states(sizes, changes):
    if sizes.swapped:
        return exchanged(sizes, scan_states(sizes, exchanged(sizes, changes)))
    transition = jnp.stack([change[0] for change in changes])
    inject = jnp.stack([change[1] for change in changes])
    forward = [(chip, chip + 1) for chip in range(sizes.chips - 1)]

    def advance(_, entry):
        left = jnp.einsum("hvd,hde->hve", entry, transition, precision=lax.Precision.HIGHEST)
        return lax.ppermute(left + inject, "chip", forward)

    entry = lax.fori_loop(0, sizes.chips - 1, advance, jnp.zeros_like(inject))
    return [entry[head] for head in range(sizes.heads)]


def query_stage(sizes, pieces, values, before, keys, inverses_, ratios, rows, prefixes):
    groups = sizes.groups

    def kernel(*refs):
        pieces = refs[:groups]
        values, before, keys, inverse, ratio, rows, prefix, reader_out, inner_out, blocks = refs[
            groups:
        ]
        gather(sizes, pieces, blocks)
        for base in range(0, sizes.units, GROUP):
            members = range(base, min(base + GROUP, sizes.units))
            queries = [unit_rows(blocks, *sizes.unit(unit), TOK) for unit in members]
            scores = []
            for number, unit in enumerate(members):
                pair = inverse[unit]
                score = dot_nt(queries[number], keys[unit]) * ratio[unit]
                scores.append(product(beside(score), factor_of(pair[:, :REFL], pair[:, REFL:])))
            for number, unit in enumerate(members):
                one = slice(unit, unit + 1)
                inner = dot(beside(scores[number] * rows[0, one, :]), twice(values[unit]))
                carried = read_rows(jnp.broadcast_to(rows[2, one, :], (DK, REFL)).T)
                reader = carried * queries[number].astype(F32) - dot(
                    beside(scores[number] * rows[1, one, :]), twice(keys[unit])
                )
                high, low = split(jnp.concatenate([prefix[unit], before[unit]], 0))
                pair = beside(reader)
                both = dot_nt(pair, jnp.concatenate([high, high], 1)) + dot_nt(pair[:, :DK], low)
                reader_out[unit] = beside(both[:, :DK])
                inner_out[unit] = inner + both[:, DK:]

    outs = [
        shape(sizes.units, CHUNK, 2 * DK),
        shape(sizes.units, CHUNK, DV, dtype=F32),
    ]
    scratch = [pltpu.VMEM((2 * groups, sizes.heads * TOK, DK), BF16)]
    return call(
        kernel,
        outs,
        *pieces,
        values,
        before,
        keys,
        inverses_,
        ratios,
        rows,
        prefixes,
        scratch=scratch,
        flops=3_000_000_000,
        name="query_stage",
    )


def read_states(sizes, states, readers, inners):
    groups = sizes.groups
    half = groups // 2

    def kernel(*refs):
        states = refs[: sizes.heads]
        readers, inners, own, other, entry = refs[sizes.heads :]
        core = axis_index("core")
        chip = axis_index("chip") if sizes.swapped else 0
        for number in range(sizes.heads):
            place_ = jnp.bitwise_xor(chip, number) if sizes.swapped else number
            entry[place_] = states[number][...]
        for head in range(sizes.heads):
            high, low = split(entry[head])
            stack = jnp.concatenate(
                [
                    jnp.concatenate([high, high], 1),
                    jnp.concatenate([low, jnp.zeros_like(low)], 1),
                ],
                0,
            )
            for side, out in enumerate((own, other)):
                first = head * groups + jnp.bitwise_xor(core, side) * half
                pair = readers[pl.ds(first, half)].reshape(half * CHUNK, 2 * DK)
                both = dot_nt(pair, stack)
                inner = inners[pl.ds(first, half)].reshape(half * CHUNK, DV)
                result = inner + both[:, :DV] + both[:, DV:]
                out[:, head * DV : (head + 1) * DV] = result.astype(BF16)

    outs = [shape(half * CHUNK, sizes.heads * DV)] * 2
    scratch = [pltpu.VMEM((sizes.heads, DV, DK), F32)]
    return call(kernel, outs, *states, readers, inners, scratch=scratch, name="read_states")


def join(sizes, own, other):
    width = sizes.heads * DV

    def kernel(own, other, out):
        first = axis_index("core") * width
        out[:, pl.ds(pl.multiple_of(first, width), width)] = own[...]
        out[:, pl.ds(pl.multiple_of(width - first, width), width)] = other[...]

    return call(kernel, shape(own.shape[0], 2 * width), own, other, name="join")


def local(queries, keys, values, betas, log_gates, starts):
    groups = lax.axis_size("head")
    sizes = Sizes(groups, log_gates.shape[1] // groups, lax.axis_size("chip"))

    def spread(parts):
        return [parts[0]] + [
            lax.ppermute(part, "head", [(z, (z + ahead) % groups) for z in range(groups)])
            for ahead, part in enumerate(parts)
            if ahead
        ]

    def swapped(part):
        return lax.ppermute(part, "core", [(0, 1), (1, 0)])

    arrived = spread(pack_keys(sizes, keys, betas, log_gates, starts.reshape(1, -1)))
    kept, sent = pack_reads(sizes, values, queries)
    value_parts, query_parts = merge_reads(sizes, kept, swapped(sent))
    value_parts = spread(value_parts)
    query_parts = spread(query_parts)
    other_keys = swapped(swap_keys(sizes, arrived))
    (unit_keys, inverse, ends, ratios, rows, steps, prefixes), transitions = key_stage(
        sizes, arrived, other_keys
    )
    unit_values, before, changes = value_stage(sizes, value_parts, ends, steps, transitions)
    readers, inners = query_stage(
        sizes, query_parts, unit_values, before, unit_keys, inverse, ratios, rows, prefixes
    )
    states = entry_states(sizes, changes)
    own, other = read_states(sizes, states, readers, inners)
    return join(sizes, own, swapped(other))


def solution(mesh):
    devices = mesh.devices
    rows = P(("chip", "core", "head"), None)
    return jax.shard_map(
        local,
        mesh=Mesh(
            devices.reshape(devices.shape[0] // 2, 2, devices.shape[1]), ("chip", "core", "head")
        ),
        in_specs=(rows, rows, rows, rows, rows, P(("chip", "core"))),
        out_specs=P(("chip", "core"), "head"),
        check_vma=False,
    )
```

```python
import jax
import jax.numpy as jnp
from jax import lax
from jax.experimental import pallas as pl
from jax.experimental.pallas import tpu as pltpu
from jax.sharding import Mesh
from jax.sharding import PartitionSpec as P

DK = 128
DV = 128
NH = 2
TOK = 32
CHUNK = 2 * TOK
REFL = CHUNK * NH
GROUP = 8
EPSILON = 1e-06

KEY_ROWS = NH * TOK
SCALE_ROWS = 16

BF16 = jnp.bfloat16
F32 = jnp.float32
NT = (((1,), (1,)), ((), ()))


def iota(shape, axis):
    return lax.broadcasted_iota(jnp.int32, shape, axis)


def dot(left, right):
    return jnp.dot(left, right, preferred_element_type=F32)


def dot_nt(left, right):
    return lax.dot_general(left, right, NT, preferred_element_type=F32)


def split(value):
    high = value.astype(BF16)
    low = (value - high.astype(F32)).astype(BF16)
    return high, low


def beside(value):
    return jnp.concatenate(split(value), 1)


def twice(value):
    return jnp.concatenate([value, value], 0)


def factor(value):
    return factor_of(*split(value))


def factor_of(high, low):
    return jnp.concatenate(
        [jnp.concatenate([high, low], 1), jnp.concatenate([high, jnp.zeros_like(low)], 1)], 0
    )


def product(left_pair, right_factor):
    both = dot(left_pair, right_factor)
    half = both.shape[1] // 2
    return both[:, :half] + both[:, half:]


def place(index):
    block = index // (NH * TOK)
    step = (index // TOK) % NH
    token = index % TOK
    return block, step, token, (block * TOK + token) * NH + step


def scale_maps():
    shape = (REFL, 8 * TOK)
    block, step, token, _ = place(iota(shape, 0))
    column = iota(shape, 1)
    source_block = column // (4 * TOK)
    kind = (column // TOK) % 4
    source = source_block * TOK + column % TOK
    now = block * TOK + token
    decay = (kind == NH) & (source <= now)
    segment = (kind == NH + 1) & (source <= now)
    beta = (kind == step) & (source == now)
    return jnp.concatenate([part.astype(F32) for part in (decay, segment, beta)], 0).astype(BF16)


def piece_rows(size):
    if size == TOK:
        return [slice(NH * TOK, 2 * NH * TOK)]
    return [
        slice(start, start + size)
        for part in range(2 * NH)
        for start in range(part * TOK + size, (part + 1) * TOK, 2 * size)
    ]


def taken(value, slices):
    return jnp.concatenate([value[each] for each in slices], 0) if len(slices) > 1 else value[slices[0]]


def put(base, rows, slices):
    pieces = []
    at = 0
    done = 0
    for each in slices:
        if each.start > at:
            pieces.append(base[at : each.start])
        size = each.stop - each.start
        pieces.append(base[each] + rows[done : done + size])
        done += size
        at = each.stop
    if at < REFL:
        pieces.append(base[at:])
    return jnp.concatenate(pieces, 0)


def inverses(lowers):
    small = 8
    count = len(lowers)
    lane = iota((small, REFL), 1)
    group_of = (lane // (NH * TOK)) * (TOK // small) + (lane % TOK) // small
    groups = [(block, piece) for block in range(2) for piece in range(TOK // small)]

    def start_row(block, step, piece):
        return block * NH * TOK + step * TOK + piece * small

    folded = []
    for lower in lowers:
        for step in range(NH):
            rows = jnp.zeros((small, REFL), F32)
            for number, (block, piece) in enumerate(groups):
                first = start_row(block, step, piece)
                rows = jnp.where(group_of == number, lower[first : first + small], rows)
            folded.append(rows)
    height = NH * small
    lower_fold = jnp.concatenate(folded, 0)
    wide = iota((count * height, REFL), 1)
    high = iota((count * height, REFL), 0) % height
    inverse = ((wide // TOK) % NH == high // small) & (wide % small == high % small)
    inverse = inverse.astype(F32).reshape(count, height, REFL)
    for token in range(small):
        for step in range(NH):
            if token == small - 1 and step == NH - 1:
                continue
            source = (wide // (NH * TOK)) * (NH * TOK) + step * TOK + (wide % TOK) // small * small + token
            column = jnp.take_along_axis(lower_fold, source, axis=1, mode="promise_in_bounds")
            row = step * small + token
            inverse = inverse - column.reshape(count, height, REFL) * inverse[:, row : row + 1, :]
    results = []
    for number in range(count):
        pieces = []
        for block in range(2):
            for step in range(NH):
                rows = inverse[number, step * small : (step + 1) * small]
                for piece in range(TOK // small):
                    mine = group_of == block * (TOK // small) + piece
                    pieces.append(jnp.where(mine, rows, 0.0))
        results.append(jnp.concatenate(pieces, 0))
    size = small
    zero = jnp.zeros((REFL, REFL), F32)
    while size < CHUNK:
        slices = piece_rows(size)
        row_block, _, row_token, _ = place(iota((REFL, REFL), 0))
        column_block, _, column_token, _ = place(iota((REFL, REFL), 1))
        row_piece = (row_block * TOK + row_token) // size
        column_piece = (column_block * TOK + column_token) // size
        linked = taken(row_piece, slices) == taken(column_piece, slices) + 1
        crossings = [
            product(beside(jnp.where(linked, taken(lower, slices), 0.0)), factor(result))
            for lower, result in zip(lowers, results)
        ]
        changes = [
            product(beside(taken(result, slices)), factor(put(zero, crossing, slices)))
            for crossing, result in zip(crossings, results)
        ]
        results = [put(result, -change, slices) for change, result in zip(changes, results)]
        size *= 2
    return results


def read_rows(value):
    return jnp.concatenate(
        [
            value[(NH - 1) * TOK : NH * TOK],
            value[(2 * NH - 1) * TOK : 2 * NH * TOK],
        ],
        0,
    )


def call(kernel, outs, *args, scratch=(), flops=0, far=0, name=None):
    specs = [pl.BlockSpec(memory_space=pltpu.HBM)] * far
    specs += [pl.BlockSpec(memory_space=pltpu.VMEM)] * (len(args) - far)
    return pl.pallas_call(
        kernel,
        out_shape=outs,
        in_specs=specs,
        scratch_shapes=scratch,
        compiler_params=pltpu.CompilerParams(vmem_limit_bytes=24 * 2**20),
        cost_estimate=pl.CostEstimate(flops=flops, bytes_accessed=0, transcendentals=0),
        name=name,
    )(*args)


def shape(*sizes, dtype=BF16):
    return jax.ShapeDtypeStruct(sizes, dtype)


def axis_index(axis):
    return lax.axis_index(axis).astype(jnp.int32)


class Sizes:
    def __init__(self, groups, group_heads, chips):
        self.groups = groups
        self.group_heads = group_heads
        self.heads = group_heads // 2
        self.chips = chips
        self.units = self.heads * groups
        self.swapped = chips == self.heads == 4

    def unit(self, number):
        return number // self.groups, number % self.groups


def shifted(index, by, size):
    moved = index + by
    return jnp.where(moved >= size, moved - size, moved)


def head_distance(core, number, groups):
    return number if number == 0 else number + (groups - 2 * number) * core


def chip_distance(core, number):
    return number + (3 - 2 * number) * core if number in (1, 2) else number


def block_columns(source, first, count):
    return [
        source[:, pl.ds(pl.multiple_of(first + number * DK, DK), DK)] for number in range(count)
    ]


def pack_keys(sizes, keys, betas, log_gates, starts):
    rows = sizes.heads * KEY_ROWS
    count = sizes.heads * NH

    def kernel(far_keys, far_betas, far_gates, far_starts, *refs):
        outs = refs[: sizes.groups]
        keys, betas, log_gates, starts, done = refs[sizes.groups :]
        width = sizes.group_heads * NH * DK
        pairs = [(far_betas, betas), (far_gates, log_gates), (far_starts, starts)]
        for group in range(sizes.groups):
            part = slice(group * width, (group + 1) * width)
            pairs.append((far_keys.at[:, part], keys.at[:, part]))
        copies = [
            pltpu.make_async_copy(far, near, done.at[number])
            for number, (far, near) in enumerate(pairs)
        ]
        for copy in copies:
            copy.start()
        for copy in copies:
            copy.wait()
        z = axis_index("head")
        core = axis_index("core")
        heads = log_gates.shape[1]
        pieces = []
        for step in range(NH):
            extent = (heads, heads * NH)
            pick = iota(extent, 1) == iota(extent, 0) * NH + step
            pieces.append(dot_nt(pick.astype(BF16), betas[...]))
        same = iota((heads, heads), 0) == iota((heads, heads), 1)
        pieces.append(dot_nt(same.astype(BF16), log_gates[...]))
        length = sizes.groups * TOK
        own = iota((length, TOK), 0) == z * TOK + iota((length, TOK), 1)
        own_starts = jnp.broadcast_to(starts[...].astype(F32), (heads, length)).astype(BF16)
        pieces.append(dot(own_starts, own.astype(BF16)))
        scales = jnp.concatenate(pieces, 1).astype(BF16)
        for number, out in enumerate(outs):
            target = shifted(z, head_distance(core, number, sizes.groups), sizes.groups)
            for side in range(2):
                owner = jnp.bitwise_xor(core, side)
                first = ((target * 2 + owner) * sizes.heads) * NH * DK
                for part, piece in enumerate(block_columns(keys, first, count)):
                    at = side * rows + part * TOK
                    out[at : at + TOK, :] = piece
            extent = (SCALE_ROWS, heads)
            pick = (iota(extent, 1) == target * sizes.group_heads + iota(extent, 0)) & (
                iota(extent, 0) < sizes.group_heads
            )
            out[2 * rows :, :] = dot(pick.astype(BF16), scales).astype(BF16)

    outs = [shape(2 * rows + SCALE_ROWS, DK)] * sizes.groups
    loaded = (keys, betas, log_gates, starts)
    scratch = [pltpu.VMEM(each.shape, each.dtype) for each in loaded]
    return call(
        kernel,
        outs,
        *[pltpu.with_memory_space_constraint(each, pltpu.HBM) for each in loaded],
        scratch=scratch + [pltpu.SemaphoreType.DMA((3 + sizes.groups,))],
        far=4,
        name="pack_keys",
    )


def swap_keys(sizes, arrived):
    rows = sizes.heads * KEY_ROWS

    def kernel(*refs):
        out = refs[-1]
        z = axis_index("head")
        core = axis_index("core")
        for number, piece in enumerate(refs[:-1]):
            behind = head_distance(core, number, sizes.groups)
            source = shifted(z, sizes.groups - behind, sizes.groups)
            out[source] = piece[rows:, :]

    return call(kernel, shape(sizes.groups, rows + SCALE_ROWS, DK), *arrived, name="swap_keys")


def pack_reads(sizes, values, queries):
    value_rows = sizes.heads * KEY_ROWS
    rows = value_rows + sizes.heads * TOK

    def kernel(values, queries, kept, sent):
        z = axis_index("head")
        core = axis_index("core")
        for ahead in range(sizes.groups):
            for side, out in enumerate((kept, sent)):
                owner = jnp.bitwise_xor(core, side)
                target = shifted(z, head_distance(owner, ahead, sizes.groups), sizes.groups)
                first = (target * 2 + owner) * sizes.heads * DK
                pieces = block_columns(values, first * NH, sizes.heads * NH)
                pieces += block_columns(queries, first, sizes.heads)
                for number, piece in enumerate(pieces):
                    out[ahead, number * TOK : (number + 1) * TOK, :] = piece

    return call(
        kernel, [shape(sizes.groups, rows, DK)] * 2, values, queries, name="pack_reads"
    )


def merge_reads(sizes, kept, swapped):
    value_rows = sizes.heads * KEY_ROWS
    query_rows = sizes.heads * TOK

    def kernel(kept, swapped, *outs):
        for ahead in range(sizes.groups):
            for side, source in enumerate((kept, swapped)):
                outs[ahead][side] = source[ahead, :value_rows, :]
                outs[sizes.groups + ahead][side] = source[ahead, value_rows:, :]

    outs = [shape(2, value_rows, DK)] * sizes.groups + [shape(2, query_rows, DK)] * sizes.groups
    merged = call(kernel, outs, kept, swapped, name="merge_reads")
    return merged[: sizes.groups], merged[sizes.groups :]


def gather(sizes, pieces, scratch):
    z = axis_index("head")
    core = axis_index("core")
    for number, piece in enumerate(pieces):
        behind = head_distance(core, number, sizes.groups)
        source = shifted(z, sizes.groups - behind, sizes.groups)
        for side in range(2):
            scratch[jnp.bitwise_xor(core, side) * sizes.groups + source] = piece[side]


def unit_rows(scratch, head, chunk, count):
    first = head * count
    return jnp.concatenate(
        [
            scratch[2 * chunk, first : first + count, :],
            scratch[2 * chunk + 1, first : first + count, :],
        ],
        0,
    )


def key_stage(sizes, arrived, swapped):
    rows = sizes.heads * KEY_ROWS
    units = sizes.units
    groups = sizes.groups

    def kernel(*refs):
        pieces = refs[:groups]
        swapped = refs[groups]
        keys_out, inverse_out, end_out, ratio_out, row_out, step_out, prefix_out = refs[
            groups + 1 : groups + 8
        ]
        totals = refs[groups + 8 : groups + 8 + sizes.heads]
        blocks, scales, every = refs[groups + 8 + sizes.heads :]
        z = axis_index("head")
        core = axis_index("core")
        for number, piece in enumerate(pieces):
            source = shifted(z, groups - head_distance(core, number, groups), groups)
            blocks[core * groups + source] = piece[:rows, :]
            scales[core * groups + source] = piece[2 * rows :, :]
        other = (1 - core) * groups
        for source in range(groups):
            blocks[other + source] = swapped[source, :rows, :]
            scales[other + source] = swapped[source, rows:, :]
        flat = scales[...].reshape(2 * groups * SCALE_ROWS, 4 * TOK)
        picks = []
        for block in range(2):
            extent = (units, 2 * groups * SCALE_ROWS)
            unit = iota(extent, 0)
            row = (unit % groups * 2 + block) * SCALE_ROWS + unit // groups
            pick = iota(extent, 1) == row + core * sizes.heads
            picks.append(dot(pick.astype(BF16), flat))
        by_unit = jnp.concatenate(picks, 1).astype(BF16)
        maps = scale_maps()
        as_rows = dot_nt(by_unit, maps)
        as_columns = dot_nt(maps, by_unit)
        decay_row, segment_row, beta_row = (
            as_rows[:, number * REFL : (number + 1) * REFL] for number in range(3)
        )
        decay_column, segment_column, beta_column = (
            as_columns[number * REFL : (number + 1) * REFL] for number in range(3)
        )
        carried_row = jnp.exp(decay_row) * (segment_row == 0).astype(F32)
        last = REFL - 1
        end_row = jnp.exp(decay_row[:, last:] - decay_row)
        end_row = end_row * (segment_row[:, last:] == segment_row).astype(F32)
        square = (REFL, REFL)
        _, _, _, row_time = place(iota(square, 0))
        _, _, _, column_time = place(iota(square, 1))
        causal = row_time >= column_time
        strict = row_time > column_time
        diagonal = row_time == column_time
        same = (iota((DK, DK), 0) == iota((DK, DK), 1)).astype(F32)
        row_out[0] = beta_row
        row_out[2] = carried_row
        for base in range(0, units, GROUP):
            members = range(base, min(base + GROUP, units))
            keys = [unit_rows(blocks, *sizes.unit(unit), KEY_ROWS) for unit in members]
            grams = [dot_nt(key, key) for key in keys]
            squares = [jnp.where(diagonal, gram, 0.0) for gram in grams]
            norm_rows = [lax.rsqrt(jnp.sum(each, 0, keepdims=True) + EPSILON) for each in squares]
            norm_columns = [
                lax.rsqrt(jnp.sum(each, 1, keepdims=True) + EPSILON) for each in squares
            ]
            lowers = []
            for number, unit in enumerate(members):
                keys_out[unit] = keys[number]
                one = slice(unit, unit + 1)
                linked = causal & (segment_column[:, one] == segment_row[one])
                gap = decay_column[:, one] - decay_row[one]
                ratio = jnp.where(linked, jnp.exp(jnp.minimum(gap, 0.0)), 0.0) * norm_rows[number]
                ratio_out[unit] = read_rows(ratio)
                strengths = beta_column[:, one] * norm_columns[number]
                lowers.append(jnp.where(strict, strengths * ratio * grams[number], 0.0))
            solved = inverses(lowers)
            pairs = [split(each) for each in solved]
            kept_rows = [
                beta_row[unit : unit + 1] * carried_row[unit : unit + 1] * norm
                for unit, norm in zip(members, norm_rows)
            ]
            turned_keys = [key.T for key in keys]
            ends = []
            for number, unit in enumerate(members):
                high, low = pairs[number]
                inverse_out[unit] = jnp.concatenate([high, low], 1)
                row_out[1, unit : unit + 1, :] = kept_rows[number]
                weights = end_row[unit : unit + 1] * norm_rows[number]
                ends.append(
                    product(
                        beside(turned_keys[number].astype(F32) * weights), factor_of(high, low)
                    )
                )
            for number, unit in enumerate(members):
                turned = turned_keys[number]
                end_out[unit] = beside(ends[number] * beta_row[unit : unit + 1])
                every[unit] = carried_row[unit : unit + 1, last:] * same - dot_nt(
                    jnp.concatenate([turned, turned], 1), beside(ends[number] * kept_rows[number])
                )
        prefixes = [same] * sizes.heads
        for chunk in range(groups):
            for head in range(sizes.heads):
                unit = head * groups + chunk
                step = every[unit]
                high, low = split(step)
                step_out[unit] = jnp.concatenate([high, low], 1)
                prefix_out[unit] = prefixes[head]
                if chunk == 0:
                    prefixes[head] = step
                else:
                    prefixes[head] = product(beside(prefixes[head]), factor_of(high, low))
        if sizes.swapped:
            for head in range(sizes.heads):
                every[head] = prefixes[head]
            chip = axis_index("chip")
            core = axis_index("core")
            for number in range(sizes.heads):
                totals[number][...] = every[jnp.bitwise_xor(chip, chip_distance(core, number))]
        else:
            for head in range(sizes.heads):
                totals[head][...] = prefixes[head]

    outs = [
        shape(units, REFL, DK),
        shape(units, REFL, 2 * REFL),
        shape(units, DK, 2 * REFL),
        shape(units, CHUNK, REFL, dtype=F32),
        shape(3, units, REFL, dtype=F32),
        shape(units, DK, 2 * DK),
        shape(units, DK, DK, dtype=F32),
    ] + [shape(DK, DK, dtype=F32)] * sizes.heads
    scratch = [
        pltpu.VMEM((2 * groups, rows, DK), BF16),
        pltpu.VMEM((2 * groups, SCALE_ROWS, DK), BF16),
        pltpu.VMEM((units, DK, DK), F32),
    ]
    results = call(
        kernel, outs, *arrived, swapped, scratch=scratch, flops=6_000_000_000, name="key_stage"
    )
    return results[:7], results[7:]


def value_stage(sizes, pieces, ends, steps):
    groups = sizes.groups

    def kernel(*refs):
        pieces = refs[:groups]
        ends, steps, values_out, before_out = refs[groups : groups + 4]
        totals = refs[groups + 4 : groups + 4 + sizes.heads]
        blocks, every = refs[groups + 4 + sizes.heads :]
        gather(sizes, pieces, blocks)
        injects = []
        for unit in range(sizes.units):
            value = unit_rows(blocks, *sizes.unit(unit), KEY_ROWS)
            values_out[unit] = value
            turned = value.T
            injects.append(dot_nt(jnp.concatenate([turned, turned], 1), ends[unit]))
        sums = [jnp.zeros((DV, DK), F32)] * sizes.heads
        for chunk in range(groups):
            for head in range(sizes.heads):
                unit = head * groups + chunk
                before_out[unit] = sums[head]
                if chunk == 0:
                    sums[head] = injects[unit]
                else:
                    step = steps[unit]
                    sums[head] = injects[unit] + product(
                        beside(sums[head]), factor_of(step[:, :DK], step[:, DK:])
                    )
        if sizes.swapped:
            for head in range(sizes.heads):
                every[head] = sums[head]
            chip = axis_index("chip")
            core = axis_index("core")
            for number in range(sizes.heads):
                totals[number][...] = every[jnp.bitwise_xor(chip, chip_distance(core, number))]
        else:
            for head in range(sizes.heads):
                totals[head][...] = sums[head]

    outs = [shape(sizes.units, REFL, DV), shape(sizes.units, DV, DK, dtype=F32)]
    outs += [shape(DV, DK, dtype=F32)] * sizes.heads
    scratch = [
        pltpu.VMEM((2 * groups, sizes.heads * KEY_ROWS, DV), BF16),
        pltpu.VMEM((sizes.heads, DV, DK), F32),
    ]
    results = call(
        kernel, outs, *pieces, ends, steps, scratch=scratch, flops=2_000_000_000, name="value_stage"
    )
    return results[0], results[1], results[2:]


def scan_states(sizes, transitions, injects):
    chips = sizes.chips

    def kernel(*refs):
        transitions = refs[:chips]
        injects = refs[chips : 2 * chips]
        outs = refs[2 * chips : 3 * chips]
        step, inject, entry = refs[3 * chips :]
        chip = axis_index("chip")
        core = axis_index("core")
        for number in range(chips):
            source = jnp.bitwise_xor(chip, chip_distance(core, number))
            step[source] = transitions[number][...]
            inject[source] = injects[number][...]
        state = jnp.zeros((DV, DK), F32)
        for index in range(chips):
            entry[index] = state
            if index == 0:
                state = inject[index]
            elif index < chips - 1:
                state = product(beside(state), factor(step[index])) + inject[index]
        for number in range(chips):
            outs[number][...] = entry[jnp.bitwise_xor(chip, chip_distance(core, number))]

    scratch = [pltpu.VMEM((chips, DV, DK), F32)] * 3
    return call(
        kernel,
        [shape(DV, DK, dtype=F32)] * chips,
        *transitions,
        *injects,
        scratch=scratch,
        name="scan_states",
    )


def exchanged(sizes, parts):
    def moved(number, part):
        pairs = [
            (chip * 2 + core, (chip ^ chip_distance(core, number)) * 2 + core)
            for chip in range(sizes.chips)
            for core in range(2)
        ]
        return lax.ppermute(part, ("chip", "core"), pairs)

    return [parts[0]] + [moved(number, part) for number, part in enumerate(parts) if number]


def entry_states(sizes, transitions, injects):
    if sizes.swapped:
        arrived = exchanged(sizes, transitions), exchanged(sizes, injects)
        return exchanged(sizes, scan_states(sizes, *arrived))
    transition = jnp.stack(transitions)
    inject = jnp.stack(injects)
    forward = [(chip, chip + 1) for chip in range(sizes.chips - 1)]

    def advance(_, entry):
        left = jnp.einsum("hvd,hde->hve", entry, transition, precision=lax.Precision.HIGHEST)
        return lax.ppermute(left + inject, "chip", forward)

    entry = lax.fori_loop(0, sizes.chips - 1, advance, jnp.zeros_like(inject))
    return [entry[head] for head in range(sizes.heads)]


def query_stage(sizes, pieces, values, before, keys, inverses_, ratios, rows, prefixes):
    groups = sizes.groups

    def kernel(*refs):
        pieces = refs[:groups]
        values, before, keys, inverse, ratio, rows, prefix, reader_out, inner_out, blocks = refs[
            groups:
        ]
        gather(sizes, pieces, blocks)
        for base in range(0, sizes.units, GROUP):
            members = range(base, min(base + GROUP, sizes.units))
            queries = [unit_rows(blocks, *sizes.unit(unit), TOK) for unit in members]
            scores = []
            for number, unit in enumerate(members):
                pair = inverse[unit]
                score = dot_nt(queries[number], keys[unit]) * ratio[unit]
                scores.append(product(beside(score), factor_of(pair[:, :REFL], pair[:, REFL:])))
            for number, unit in enumerate(members):
                one = slice(unit, unit + 1)
                inner = dot(beside(scores[number] * rows[0, one, :]), twice(values[unit]))
                carried = read_rows(jnp.broadcast_to(rows[2, one, :], (DK, REFL)).T)
                reader = carried * queries[number].astype(F32) - dot(
                    beside(scores[number] * rows[1, one, :]), twice(keys[unit])
                )
                high, low = split(jnp.concatenate([prefix[unit], before[unit]], 0))
                pair = beside(reader)
                both = dot_nt(pair, jnp.concatenate([high, high], 1)) + dot_nt(pair[:, :DK], low)
                reader_out[unit] = beside(both[:, :DK])
                inner_out[unit] = inner + both[:, DK:]

    outs = [
        shape(sizes.units, CHUNK, 2 * DK),
        shape(sizes.units, CHUNK, DV, dtype=F32),
    ]
    scratch = [pltpu.VMEM((2 * groups, sizes.heads * TOK, DK), BF16)]
    return call(
        kernel,
        outs,
        *pieces,
        values,
        before,
        keys,
        inverses_,
        ratios,
        rows,
        prefixes,
        scratch=scratch,
        flops=3_000_000_000,
        name="query_stage",
    )


def read_states(sizes, states, readers, inners):
    groups = sizes.groups
    half = groups // 2

    def kernel(*refs):
        states = refs[: sizes.heads]
        readers, inners, own, other, entry = refs[sizes.heads :]
        core = axis_index("core")
        chip = axis_index("chip") if sizes.swapped else 0
        for number in range(sizes.heads):
            place_ = jnp.bitwise_xor(chip, chip_distance(core, number)) if sizes.swapped else number
            entry[place_] = states[number][...]
        for head in range(sizes.heads):
            high, low = split(entry[head])
            stack = jnp.concatenate(
                [
                    jnp.concatenate([high, high], 1),
                    jnp.concatenate([low, jnp.zeros_like(low)], 1),
                ],
                0,
            )
            for side, out in enumerate((own, other)):
                first = head * groups + jnp.bitwise_xor(core, side) * half
                pair = readers[pl.ds(first, half)].reshape(half * CHUNK, 2 * DK)
                both = dot_nt(pair, stack)
                inner = inners[pl.ds(first, half)].reshape(half * CHUNK, DV)
                result = inner + both[:, :DV] + both[:, DV:]
                out[:, head * DV : (head + 1) * DV] = result.astype(BF16)

    outs = [shape(half * CHUNK, sizes.heads * DV)] * 2
    scratch = [pltpu.VMEM((sizes.heads, DV, DK), F32)]
    return call(kernel, outs, *states, readers, inners, scratch=scratch, name="read_states")


def join(sizes, own, other):
    width = sizes.heads * DV

    def kernel(own, other, out):
        first = axis_index("core") * width
        out[:, pl.ds(pl.multiple_of(first, width), width)] = own[...]
        out[:, pl.ds(pl.multiple_of(width - first, width), width)] = other[...]

    return call(kernel, shape(own.shape[0], 2 * width), own, other, name="join")


def local(queries, keys, values, betas, log_gates, starts):
    groups = lax.axis_size("head")
    sizes = Sizes(groups, log_gates.shape[1] // groups, lax.axis_size("chip"))

    def moved(number, part):
        pairs = [
            (core * groups + z, core * groups + (z + head_distance(core, number, groups)) % groups)
            for core in range(2)
            for z in range(groups)
        ]
        return lax.ppermute(part, ("core", "head"), pairs)

    def spread(parts):
        return [parts[0]] + [moved(number, part) for number, part in enumerate(parts) if number]

    def swapped(part):
        return lax.ppermute(part, "core", [(0, 1), (1, 0)])

    arrived = spread(pack_keys(sizes, keys, betas, log_gates, starts.reshape(1, -1)))
    kept, sent = pack_reads(sizes, values, queries)
    value_parts, query_parts = merge_reads(sizes, kept, swapped(sent))
    value_parts = spread(value_parts)
    query_parts = spread(query_parts)
    other_keys = swapped(swap_keys(sizes, arrived))
    (unit_keys, inverse, ends, ratios, rows, steps, prefixes), transitions = key_stage(
        sizes, arrived, other_keys
    )
    unit_values, before, injects = value_stage(sizes, value_parts, ends, steps)
    states = entry_states(sizes, transitions, injects)
    readers, inners = query_stage(
        sizes, query_parts, unit_values, before, unit_keys, inverse, ratios, rows, prefixes
    )
    own, other = read_states(sizes, states, readers, inners)
    return join(sizes, own, swapped(other))


def solution(mesh):
    devices = mesh.devices
    rows = P(("chip", "core", "head"), None)
    return jax.shard_map(
        local,
        mesh=Mesh(
            devices.reshape(devices.shape[0] // 2, 2, devices.shape[1]), ("chip", "core", "head")
        ),
        in_specs=(rows, rows, rows, rows, rows, P(("chip", "core"))),
        out_specs=P(("chip", "core"), "head"),
        check_vma=False,
    )
```

```python
import jax
import jax.numpy as jnp
from jax import lax
from jax.experimental import pallas as pl
from jax.experimental.pallas import tpu as pltpu
from jax.sharding import Mesh
from jax.sharding import PartitionSpec as P

DK = 128
DV = 128
NH = 2
TOK = 32
CHUNK = 2 * TOK
REFL = CHUNK * NH
GROUP = 8
EPSILON = 1e-06

KEY_ROWS = NH * TOK
SCALE_ROWS = 16

BF16 = jnp.bfloat16
F32 = jnp.float32
NT = (((1,), (1,)), ((), ()))


def iota(shape, axis):
    return lax.broadcasted_iota(jnp.int32, shape, axis)


def dot(left, right):
    return jnp.dot(left, right, preferred_element_type=F32)


def dot_nt(left, right):
    return lax.dot_general(left, right, NT, preferred_element_type=F32)


def split(value):
    high = value.astype(BF16)
    low = (value - high.astype(F32)).astype(BF16)
    return high, low


def beside(value):
    return jnp.concatenate(split(value), 1)


def twice(value):
    return jnp.concatenate([value, value], 0)


def factor(value):
    return factor_of(*split(value))


def factor_of(high, low):
    return jnp.concatenate(
        [jnp.concatenate([high, low], 1), jnp.concatenate([high, jnp.zeros_like(low)], 1)], 0
    )


def product(left_pair, right_factor):
    both = dot(left_pair, right_factor)
    half = both.shape[1] // 2
    return both[:, :half] + both[:, half:]


def place(index):
    block = index // (NH * TOK)
    step = (index // TOK) % NH
    token = index % TOK
    return block, step, token, (block * TOK + token) * NH + step


def scale_maps():
    shape = (REFL, 8 * TOK)
    block, step, token, _ = place(iota(shape, 0))
    column = iota(shape, 1)
    source_block = column // (4 * TOK)
    kind = (column // TOK) % 4
    source = source_block * TOK + column % TOK
    now = block * TOK + token
    decay = (kind == NH) & (source <= now)
    segment = (kind == NH + 1) & (source <= now)
    beta = (kind == step) & (source == now)
    return jnp.concatenate([part.astype(F32) for part in (decay, segment, beta)], 0).astype(BF16)


def piece_rows(size):
    if size == TOK:
        return [slice(NH * TOK, 2 * NH * TOK)]
    return [
        slice(start, start + size)
        for part in range(2 * NH)
        for start in range(part * TOK + size, (part + 1) * TOK, 2 * size)
    ]


def taken(value, slices):
    return jnp.concatenate([value[each] for each in slices], 0) if len(slices) > 1 else value[slices[0]]


def put(base, rows, slices):
    pieces = []
    at = 0
    done = 0
    for each in slices:
        if each.start > at:
            pieces.append(base[at : each.start])
        size = each.stop - each.start
        pieces.append(base[each] + rows[done : done + size])
        done += size
        at = each.stop
    if at < REFL:
        pieces.append(base[at:])
    return jnp.concatenate(pieces, 0)


def inverses(lowers):
    small = 8
    count = len(lowers)
    lane = iota((small, REFL), 1)
    group_of = (lane // (NH * TOK)) * (TOK // small) + (lane % TOK) // small
    groups = [(block, piece) for block in range(2) for piece in range(TOK // small)]

    def start_row(block, step, piece):
        return block * NH * TOK + step * TOK + piece * small

    folded = []
    for lower in lowers:
        for step in range(NH):
            rows = jnp.zeros((small, REFL), F32)
            for number, (block, piece) in enumerate(groups):
                first = start_row(block, step, piece)
                rows = jnp.where(group_of == number, lower[first : first + small], rows)
            folded.append(rows)
    height = NH * small
    lower_fold = jnp.concatenate(folded, 0)
    wide = iota((count * height, REFL), 1)
    high = iota((count * height, REFL), 0) % height
    inverse = ((wide // TOK) % NH == high // small) & (wide % small == high % small)
    inverse = inverse.astype(F32).reshape(count, height, REFL)
    for token in range(small):
        for step in range(NH):
            if token == small - 1 and step == NH - 1:
                continue
            source = (wide // (NH * TOK)) * (NH * TOK) + step * TOK + (wide % TOK) // small * small + token
            column = jnp.take_along_axis(lower_fold, source, axis=1, mode="promise_in_bounds")
            row = step * small + token
            inverse = inverse - column.reshape(count, height, REFL) * inverse[:, row : row + 1, :]
    results = []
    for number in range(count):
        pieces = []
        for block in range(2):
            for step in range(NH):
                rows = inverse[number, step * small : (step + 1) * small]
                for piece in range(TOK // small):
                    mine = group_of == block * (TOK // small) + piece
                    pieces.append(jnp.where(mine, rows, 0.0))
        results.append(jnp.concatenate(pieces, 0))
    size = small
    zero = jnp.zeros((REFL, REFL), F32)
    while size < CHUNK:
        slices = piece_rows(size)
        row_block, _, row_token, _ = place(iota((REFL, REFL), 0))
        column_block, _, column_token, _ = place(iota((REFL, REFL), 1))
        row_piece = (row_block * TOK + row_token) // size
        column_piece = (column_block * TOK + column_token) // size
        linked = taken(row_piece, slices) == taken(column_piece, slices) + 1
        crossings = [
            product(beside(jnp.where(linked, taken(lower, slices), 0.0)), factor(result))
            for lower, result in zip(lowers, results)
        ]
        changes = [
            product(beside(taken(result, slices)), factor(put(zero, crossing, slices)))
            for crossing, result in zip(crossings, results)
        ]
        results = [put(result, -change, slices) for change, result in zip(changes, results)]
        size *= 2
    return results


def read_rows(value):
    return jnp.concatenate(
        [
            value[(NH - 1) * TOK : NH * TOK],
            value[(2 * NH - 1) * TOK : 2 * NH * TOK],
        ],
        0,
    )


def call(kernel, outs, *args, scratch=(), flops=0, far=0, name=None):
    specs = [pl.BlockSpec(memory_space=pltpu.HBM)] * far
    specs += [pl.BlockSpec(memory_space=pltpu.VMEM)] * (len(args) - far)
    return pl.pallas_call(
        kernel,
        out_shape=outs,
        in_specs=specs,
        scratch_shapes=scratch,
        compiler_params=pltpu.CompilerParams(vmem_limit_bytes=24 * 2**20),
        cost_estimate=pl.CostEstimate(flops=flops, bytes_accessed=0, transcendentals=0),
        name=name,
    )(*args)


def shape(*sizes, dtype=BF16):
    return jax.ShapeDtypeStruct(sizes, dtype)


def axis_index(axis):
    return lax.axis_index(axis).astype(jnp.int32)


class Sizes:
    def __init__(self, groups, group_heads, chips):
        self.groups = groups
        self.group_heads = group_heads
        self.heads = group_heads // 2
        self.chips = chips
        self.units = self.heads * groups
        self.swapped = chips == self.heads and chips & (chips - 1) == 0

    def unit(self, number):
        return number // self.groups, number % self.groups


def shifted(index, by, size):
    moved = index + by
    return jnp.where(moved >= size, moved - size, moved)


def block_columns(source, first, count):
    return [
        source[:, pl.ds(pl.multiple_of(first + number * DK, DK), DK)] for number in range(count)
    ]


def pack_keys(sizes, keys, betas, log_gates, starts):
    rows = sizes.heads * KEY_ROWS
    count = sizes.heads * NH

    def kernel(far_keys, far_betas, far_gates, far_starts, *refs):
        outs = refs[: sizes.groups]
        keys, betas, log_gates, starts, done = refs[sizes.groups :]
        width = sizes.group_heads * NH * DK
        pairs = [(far_betas, betas), (far_gates, log_gates), (far_starts, starts)]
        for group in range(sizes.groups):
            part = slice(group * width, (group + 1) * width)
            pairs.append((far_keys.at[:, part], keys.at[:, part]))
        copies = [
            pltpu.make_async_copy(far, near, done.at[number])
            for number, (far, near) in enumerate(pairs)
        ]
        for copy in copies:
            copy.start()
        for copy in copies:
            copy.wait()
        z = axis_index("head")
        core = axis_index("core")
        heads = log_gates.shape[1]
        pieces = []
        for step in range(NH):
            extent = (heads, heads * NH)
            pick = iota(extent, 1) == iota(extent, 0) * NH + step
            pieces.append(dot_nt(pick.astype(BF16), betas[...]))
        same = iota((heads, heads), 0) == iota((heads, heads), 1)
        pieces.append(dot_nt(same.astype(BF16), log_gates[...]))
        length = sizes.groups * TOK
        own = iota((length, TOK), 0) == z * TOK + iota((length, TOK), 1)
        own_starts = jnp.broadcast_to(starts[...].astype(F32), (heads, length)).astype(BF16)
        pieces.append(dot(own_starts, own.astype(BF16)))
        scales = jnp.concatenate(pieces, 1).astype(BF16)
        for ahead, out in enumerate(outs):
            target = shifted(z, ahead, sizes.groups)
            for side in range(2):
                owner = jnp.bitwise_xor(core, side)
                first = ((target * 2 + owner) * sizes.heads) * NH * DK
                for number, piece in enumerate(block_columns(keys, first, count)):
                    at = side * rows + number * TOK
                    out[at : at + TOK, :] = piece
            extent = (SCALE_ROWS, heads)
            pick = (iota(extent, 1) == target * sizes.group_heads + iota(extent, 0)) & (
                iota(extent, 0) < sizes.group_heads
            )
            out[2 * rows :, :] = dot(pick.astype(BF16), scales).astype(BF16)

    outs = [shape(2 * rows + SCALE_ROWS, DK)] * sizes.groups
    loaded = (keys, betas, log_gates, starts)
    scratch = [pltpu.VMEM(each.shape, each.dtype) for each in loaded]
    return call(
        kernel,
        outs,
        *[pltpu.with_memory_space_constraint(each, pltpu.HBM) for each in loaded],
        scratch=scratch + [pltpu.SemaphoreType.DMA((3 + sizes.groups,))],
        far=4,
        name="pack_keys",
    )


def swap_keys(sizes, arrived):
    rows = sizes.heads * KEY_ROWS

    def kernel(*refs):
        out = refs[-1]
        z = axis_index("head")
        for behind, piece in enumerate(refs[:-1]):
            source = shifted(z, sizes.groups - behind, sizes.groups) if behind else z
            out[source] = piece[rows:, :]

    return call(kernel, shape(sizes.groups, rows + SCALE_ROWS, DK), *arrived, name="swap_keys")


def pack_reads(sizes, values, queries):
    value_rows = sizes.heads * KEY_ROWS
    rows = value_rows + sizes.heads * TOK

    def kernel(values, queries, kept, sent):
        z = axis_index("head")
        core = axis_index("core")
        for ahead in range(sizes.groups):
            target = shifted(z, ahead, sizes.groups)
            for side, out in enumerate((kept, sent)):
                first = (target * 2 + jnp.bitwise_xor(core, side)) * sizes.heads * DK
                pieces = block_columns(values, first * NH, sizes.heads * NH)
                pieces += block_columns(queries, first, sizes.heads)
                for number, piece in enumerate(pieces):
                    out[ahead, number * TOK : (number + 1) * TOK, :] = piece

    return call(
        kernel, [shape(sizes.groups, rows, DK)] * 2, values, queries, name="pack_reads"
    )


def merge_reads(sizes, kept, swapped):
    value_rows = sizes.heads * KEY_ROWS
    query_rows = sizes.heads * TOK

    def kernel(kept, swapped, *outs):
        for ahead in range(sizes.groups):
            for side, source in enumerate((kept, swapped)):
                outs[ahead][side] = source[ahead, :value_rows, :]
                outs[sizes.groups + ahead][side] = source[ahead, value_rows:, :]

    outs = [shape(2, value_rows, DK)] * sizes.groups + [shape(2, query_rows, DK)] * sizes.groups
    merged = call(kernel, outs, kept, swapped, name="merge_reads")
    return merged[: sizes.groups], merged[sizes.groups :]


def gather(sizes, pieces, scratch):
    z = axis_index("head")
    core = axis_index("core")
    for behind, piece in enumerate(pieces):
        source = shifted(z, sizes.groups - behind, sizes.groups) if behind else z
        for side in range(2):
            scratch[jnp.bitwise_xor(core, side) * sizes.groups + source] = piece[side]


def unit_rows(scratch, head, chunk, count):
    first = head * count
    return jnp.concatenate(
        [
            scratch[2 * chunk, first : first + count, :],
            scratch[2 * chunk + 1, first : first + count, :],
        ],
        0,
    )


def key_stage(sizes, arrived, swapped):
    rows = sizes.heads * KEY_ROWS
    units = sizes.units
    groups = sizes.groups

    def kernel(*refs):
        pieces = refs[:groups]
        swapped = refs[groups]
        keys_out, inverse_out, end_out, ratio_out, row_out, step_out, prefix_out = refs[
            groups + 1 : groups + 8
        ]
        totals = refs[groups + 8 : groups + 8 + sizes.heads]
        blocks, scales, every = refs[groups + 8 + sizes.heads :]
        z = axis_index("head")
        core = axis_index("core")
        for behind, piece in enumerate(pieces):
            source = shifted(z, groups - behind, groups) if behind else z
            blocks[core * groups + source] = piece[:rows, :]
            scales[core * groups + source] = piece[2 * rows :, :]
        other = (1 - core) * groups
        for source in range(groups):
            blocks[other + source] = swapped[source, :rows, :]
            scales[other + source] = swapped[source, rows:, :]
        flat = scales[...].reshape(2 * groups * SCALE_ROWS, 4 * TOK)
        picks = []
        for block in range(2):
            extent = (units, 2 * groups * SCALE_ROWS)
            unit = iota(extent, 0)
            row = (unit % groups * 2 + block) * SCALE_ROWS + unit // groups
            pick = iota(extent, 1) == row + core * sizes.heads
            picks.append(dot(pick.astype(BF16), flat))
        by_unit = jnp.concatenate(picks, 1).astype(BF16)
        maps = scale_maps()
        as_rows = dot_nt(by_unit, maps)
        as_columns = dot_nt(maps, by_unit)
        decay_row, segment_row, beta_row = (
            as_rows[:, number * REFL : (number + 1) * REFL] for number in range(3)
        )
        decay_column, segment_column, beta_column = (
            as_columns[number * REFL : (number + 1) * REFL] for number in range(3)
        )
        carried_row = jnp.exp(decay_row) * (segment_row == 0).astype(F32)
        last = REFL - 1
        end_row = jnp.exp(decay_row[:, last:] - decay_row)
        end_row = end_row * (segment_row[:, last:] == segment_row).astype(F32)
        square = (REFL, REFL)
        _, _, _, row_time = place(iota(square, 0))
        _, _, _, column_time = place(iota(square, 1))
        causal = row_time >= column_time
        strict = row_time > column_time
        diagonal = row_time == column_time
        same = (iota((DK, DK), 0) == iota((DK, DK), 1)).astype(F32)
        row_out[0] = beta_row
        row_out[2] = carried_row
        for base in range(0, units, GROUP):
            members = range(base, min(base + GROUP, units))
            keys = [unit_rows(blocks, *sizes.unit(unit), KEY_ROWS) for unit in members]
            grams = [dot_nt(key, key) for key in keys]
            squares = [jnp.where(diagonal, gram, 0.0) for gram in grams]
            norm_rows = [lax.rsqrt(jnp.sum(each, 0, keepdims=True) + EPSILON) for each in squares]
            norm_columns = [
                lax.rsqrt(jnp.sum(each, 1, keepdims=True) + EPSILON) for each in squares
            ]
            lowers = []
            for number, unit in enumerate(members):
                keys_out[unit] = keys[number]
                one = slice(unit, unit + 1)
                linked = causal & (segment_column[:, one] == segment_row[one])
                gap = decay_column[:, one] - decay_row[one]
                ratio = jnp.where(linked, jnp.exp(jnp.minimum(gap, 0.0)), 0.0) * norm_rows[number]
                ratio_out[unit] = read_rows(ratio)
                strengths = beta_column[:, one] * norm_columns[number]
                lowers.append(jnp.where(strict, strengths * ratio * grams[number], 0.0))
            solved = inverses(lowers)
            pairs = [split(each) for each in solved]
            kept_rows = [
                beta_row[unit : unit + 1] * carried_row[unit : unit + 1] * norm
                for unit, norm in zip(members, norm_rows)
            ]
            turned_keys = [key.T for key in keys]
            ends = []
            for number, unit in enumerate(members):
                high, low = pairs[number]
                inverse_out[unit] = jnp.concatenate([high, low], 1)
                row_out[1, unit : unit + 1, :] = kept_rows[number]
                weights = end_row[unit : unit + 1] * norm_rows[number]
                ends.append(
                    product(
                        beside(turned_keys[number].astype(F32) * weights), factor_of(high, low)
                    )
                )
            for number, unit in enumerate(members):
                turned = turned_keys[number]
                end_out[unit] = beside(ends[number] * beta_row[unit : unit + 1])
                every[unit] = carried_row[unit : unit + 1, last:] * same - dot_nt(
                    jnp.concatenate([turned, turned], 1), beside(ends[number] * kept_rows[number])
                )
        prefixes = [same] * sizes.heads
        for chunk in range(groups):
            for head in range(sizes.heads):
                unit = head * groups + chunk
                step = every[unit]
                high, low = split(step)
                step_out[unit] = jnp.concatenate([high, low], 1)
                prefix_out[unit] = prefixes[head]
                if chunk == 0:
                    prefixes[head] = step
                else:
                    prefixes[head] = product(beside(prefixes[head]), factor_of(high, low))
        if sizes.swapped:
            for head in range(sizes.heads):
                every[head] = prefixes[head]
            chip = axis_index("chip")
            for number in range(sizes.heads):
                totals[number][...] = every[jnp.bitwise_xor(chip, number)]
        else:
            for head in range(sizes.heads):
                totals[head][...] = prefixes[head]

    outs = [
        shape(units, REFL, DK),
        shape(units, REFL, 2 * REFL),
        shape(units, DK, 2 * REFL),
        shape(units, CHUNK, REFL, dtype=F32),
        shape(3, units, REFL, dtype=F32),
        shape(units, DK, 2 * DK),
        shape(units, DK, DK, dtype=F32),
    ] + [shape(DK, DK, dtype=F32)] * sizes.heads
    scratch = [
        pltpu.VMEM((2 * groups, rows, DK), BF16),
        pltpu.VMEM((2 * groups, SCALE_ROWS, DK), BF16),
        pltpu.VMEM((units, DK, DK), F32),
    ]
    results = call(
        kernel, outs, *arrived, swapped, scratch=scratch, flops=6_000_000_000, name="key_stage"
    )
    return results[:7], results[7:]


def value_stage(sizes, pieces, ends, steps):
    groups = sizes.groups

    def kernel(*refs):
        pieces = refs[:groups]
        ends, steps, values_out, before_out = refs[groups : groups + 4]
        totals = refs[groups + 4 : groups + 4 + sizes.heads]
        blocks, every = refs[groups + 4 + sizes.heads :]
        gather(sizes, pieces, blocks)
        injects = []
        for unit in range(sizes.units):
            value = unit_rows(blocks, *sizes.unit(unit), KEY_ROWS)
            values_out[unit] = value
            turned = value.T
            injects.append(dot_nt(jnp.concatenate([turned, turned], 1), ends[unit]))
        sums = [jnp.zeros((DV, DK), F32)] * sizes.heads
        for chunk in range(groups):
            for head in range(sizes.heads):
                unit = head * groups + chunk
                before_out[unit] = sums[head]
                if chunk == 0:
                    sums[head] = injects[unit]
                else:
                    step = steps[unit]
                    sums[head] = injects[unit] + product(
                        beside(sums[head]), factor_of(step[:, :DK], step[:, DK:])
                    )
        if sizes.swapped:
            for head in range(sizes.heads):
                every[head] = sums[head]
            chip = axis_index("chip")
            for number in range(sizes.heads):
                totals[number][...] = every[jnp.bitwise_xor(chip, number)]
        else:
            for head in range(sizes.heads):
                totals[head][...] = sums[head]

    outs = [shape(sizes.units, REFL, DV), shape(sizes.units, DV, DK, dtype=F32)]
    outs += [shape(DV, DK, dtype=F32)] * sizes.heads
    scratch = [
        pltpu.VMEM((2 * groups, sizes.heads * KEY_ROWS, DV), BF16),
        pltpu.VMEM((sizes.heads, DV, DK), F32),
    ]
    results = call(
        kernel, outs, *pieces, ends, steps, scratch=scratch, flops=2_000_000_000, name="value_stage"
    )
    return results[0], results[1], results[2:]


def scan_states(sizes, transitions, injects):
    chips = sizes.chips

    def kernel(*refs):
        transitions = refs[:chips]
        injects = refs[chips : 2 * chips]
        outs = refs[2 * chips : 3 * chips]
        step, inject, entry = refs[3 * chips :]
        chip = axis_index("chip")
        for number in range(chips):
            source = jnp.bitwise_xor(chip, number)
            step[source] = transitions[number][...]
            inject[source] = injects[number][...]
        state = jnp.zeros((DV, DK), F32)
        for index in range(chips):
            entry[index] = state
            if index == 0:
                state = inject[index]
            elif index < chips - 1:
                state = product(beside(state), factor(step[index])) + inject[index]
        for number in range(chips):
            outs[number][...] = entry[jnp.bitwise_xor(chip, number)]

    scratch = [pltpu.VMEM((chips, DV, DK), F32)] * 3
    return call(
        kernel,
        [shape(DV, DK, dtype=F32)] * chips,
        *transitions,
        *injects,
        scratch=scratch,
        name="scan_states",
    )


def exchanged(sizes, parts, needed):
    return [parts[0]] + [
        lax.ppermute(
            part,
            "chip",
            [
                (chip, chip ^ number)
                for chip in range(sizes.chips)
                if needed(chip, chip ^ number)
            ],
        )
        for number, part in enumerate(parts)
        if number
    ]


def entry_states(sizes, transitions, injects):
    if sizes.swapped:
        last = sizes.chips - 1
        transitions = exchanged(sizes, transitions, lambda source, _: 0 < source < last)
        injects = exchanged(sizes, injects, lambda source, _: source < last)
        entries = scan_states(sizes, transitions, injects)
        return exchanged(sizes, entries, lambda _, target: target > 0)
    transition = jnp.stack(transitions)
    inject = jnp.stack(injects)
    forward = [(chip, chip + 1) for chip in range(sizes.chips - 1)]

    def advance(_, entry):
        left = jnp.einsum("hvd,hde->hve", entry, transition, precision=lax.Precision.HIGHEST)
        return lax.ppermute(left + inject, "chip", forward)

    entry = lax.fori_loop(0, sizes.chips - 1, advance, jnp.zeros_like(inject))
    return [entry[head] for head in range(sizes.heads)]


def query_stage(sizes, pieces, values, before, keys, inverses_, ratios, rows, prefixes):
    groups = sizes.groups

    def kernel(*refs):
        pieces = refs[:groups]
        values, before, keys, inverse, ratio, rows, prefix, reader_out, inner_out, blocks = refs[
            groups:
        ]
        gather(sizes, pieces, blocks)
        for base in range(0, sizes.units, GROUP):
            members = range(base, min(base + GROUP, sizes.units))
            queries = [unit_rows(blocks, *sizes.unit(unit), TOK) for unit in members]
            scores = []
            for number, unit in enumerate(members):
                pair = inverse[unit]
                score = dot_nt(queries[number], keys[unit]) * ratio[unit]
                scores.append(product(beside(score), factor_of(pair[:, :REFL], pair[:, REFL:])))
            for number, unit in enumerate(members):
                one = slice(unit, unit + 1)
                inner = dot(beside(scores[number] * rows[0, one, :]), twice(values[unit]))
                carried = read_rows(jnp.broadcast_to(rows[2, one, :], (DK, REFL)).T)
                reader = carried * queries[number].astype(F32) - dot(
                    beside(scores[number] * rows[1, one, :]), twice(keys[unit])
                )
                high, low = split(jnp.concatenate([prefix[unit], before[unit]], 0))
                pair = beside(reader)
                both = dot_nt(pair, jnp.concatenate([high, high], 1)) + dot_nt(pair[:, :DK], low)
                reader_out[unit] = beside(both[:, :DK])
                inner_out[unit] = inner + both[:, DK:]

    outs = [
        shape(sizes.units, CHUNK, 2 * DK),
        shape(sizes.units, CHUNK, DV, dtype=F32),
    ]
    scratch = [pltpu.VMEM((2 * groups, sizes.heads * TOK, DK), BF16)]
    return call(
        kernel,
        outs,
        *pieces,
        values,
        before,
        keys,
        inverses_,
        ratios,
        rows,
        prefixes,
        scratch=scratch,
        flops=3_000_000_000,
        name="query_stage",
    )


def read_states(sizes, states, readers, inners):
    groups = sizes.groups
    half = groups // 2

    def kernel(*refs):
        states = refs[: sizes.heads]
        readers, inners, own, other, entry = refs[sizes.heads :]
        core = axis_index("core")
        chip = axis_index("chip") if sizes.swapped else 0
        for number in range(sizes.heads):
            place_ = jnp.bitwise_xor(chip, number) if sizes.swapped else number
            entry[place_] = states[number][...]
        for head in range(sizes.heads):
            high, low = split(entry[head])
            stack = jnp.concatenate(
                [
                    jnp.concatenate([high, high], 1),
                    jnp.concatenate([low, jnp.zeros_like(low)], 1),
                ],
                0,
            )
            for side, out in enumerate((own, other)):
                first = head * groups + jnp.bitwise_xor(core, side) * half
                pair = readers[pl.ds(first, half)].reshape(half * CHUNK, 2 * DK)
                both = dot_nt(pair, stack)
                inner = inners[pl.ds(first, half)].reshape(half * CHUNK, DV)
                result = inner + both[:, :DV] + both[:, DV:]
                out[:, head * DV : (head + 1) * DV] = result.astype(BF16)

    outs = [shape(half * CHUNK, sizes.heads * DV)] * 2
    scratch = [pltpu.VMEM((sizes.heads, DV, DK), F32)]
    return call(kernel, outs, *states, readers, inners, scratch=scratch, name="read_states")


def join(sizes, own, other):
    width = sizes.heads * DV

    def kernel(own, other, out):
        first = axis_index("core") * width
        out[:, pl.ds(pl.multiple_of(first, width), width)] = own[...]
        out[:, pl.ds(pl.multiple_of(width - first, width), width)] = other[...]

    return call(kernel, shape(own.shape[0], 2 * width), own, other, name="join")


def local(queries, keys, values, betas, log_gates, starts):
    groups = lax.axis_size("head")
    sizes = Sizes(groups, log_gates.shape[1] // groups, lax.axis_size("chip"))

    def spread(parts):
        return [parts[0]] + [
            lax.ppermute(part, "head", [(z, (z + ahead) % groups) for z in range(groups)])
            for ahead, part in enumerate(parts)
            if ahead
        ]

    def swapped(part):
        return lax.ppermute(part, "core", [(0, 1), (1, 0)])

    arrived = spread(pack_keys(sizes, keys, betas, log_gates, starts.reshape(1, -1)))
    kept, sent = pack_reads(sizes, values, queries)
    value_parts, query_parts = merge_reads(sizes, kept, swapped(sent))
    value_parts = spread(value_parts)
    query_parts = spread(query_parts)
    other_keys = swapped(swap_keys(sizes, arrived))
    (unit_keys, inverse, ends, ratios, rows, steps, prefixes), transitions = key_stage(
        sizes, arrived, other_keys
    )
    unit_values, before, injects = value_stage(sizes, value_parts, ends, steps)
    states = entry_states(sizes, transitions, injects)
    readers, inners = query_stage(
        sizes, query_parts, unit_values, before, unit_keys, inverse, ratios, rows, prefixes
    )
    own, other = read_states(sizes, states, readers, inners)
    return join(sizes, own, swapped(other))


def solution(mesh):
    devices = mesh.devices
    rows = P(("chip", "core", "head"), None)
    return jax.shard_map(
        local,
        mesh=Mesh(
            devices.reshape(devices.shape[0] // 2, 2, devices.shape[1]), ("chip", "core", "head")
        ),
        in_specs=(rows, rows, rows, rows, rows, P(("chip", "core"))),
        out_specs=P(("chip", "core"), "head"),
        check_vma=False,
    )
```

```python
import jax
import jax.numpy as jnp
from jax import lax
from jax.experimental import pallas as pl
from jax.experimental.pallas import tpu as pltpu
from jax.sharding import Mesh
from jax.sharding import PartitionSpec as P

DK = 128
DV = 128
NH = 2
TOK = 32
CHUNK = 2 * TOK
REFL = CHUNK * NH
GROUP = 8
EPSILON = 1e-06

KEY_ROWS = NH * TOK
SCALE_ROWS = 16

BF16 = jnp.bfloat16
F32 = jnp.float32
NT = (((1,), (1,)), ((), ()))


def iota(shape, axis):
    return lax.broadcasted_iota(jnp.int32, shape, axis)


def dot(left, right):
    return jnp.dot(left, right, preferred_element_type=F32)


def dot_nt(left, right):
    return lax.dot_general(left, right, NT, preferred_element_type=F32)


def split(value):
    high = value.astype(BF16)
    low = (value - high.astype(F32)).astype(BF16)
    return high, low


def beside(value):
    return jnp.concatenate(split(value), 1)


def twice(value):
    return jnp.concatenate([value, value], 0)


def factor(value):
    return factor_of(*split(value))


def factor_of(high, low):
    return jnp.concatenate(
        [jnp.concatenate([high, low], 1), jnp.concatenate([high, jnp.zeros_like(low)], 1)], 0
    )


def product(left_pair, right_factor):
    both = dot(left_pair, right_factor)
    half = both.shape[1] // 2
    return both[:, :half] + both[:, half:]


def place(index):
    block = index // (NH * TOK)
    step = (index // TOK) % NH
    token = index % TOK
    return block, step, token, (block * TOK + token) * NH + step


def scale_maps():
    shape = (REFL, 8 * TOK)
    block, step, token, _ = place(iota(shape, 0))
    column = iota(shape, 1)
    source_block = column // (4 * TOK)
    kind = (column // TOK) % 4
    source = source_block * TOK + column % TOK
    now = block * TOK + token
    decay = (kind == NH) & (source <= now)
    segment = (kind == NH + 1) & (source <= now)
    beta = (kind == step) & (source == now)
    return jnp.concatenate([part.astype(F32) for part in (decay, segment, beta)], 0).astype(BF16)


def piece_rows(size):
    if size == TOK:
        return [slice(NH * TOK, 2 * NH * TOK)]
    return [
        slice(start, start + size)
        for part in range(2 * NH)
        for start in range(part * TOK + size, (part + 1) * TOK, 2 * size)
    ]


def taken(value, slices):
    return jnp.concatenate([value[each] for each in slices], 0) if len(slices) > 1 else value[slices[0]]


def put(base, rows, slices):
    pieces = []
    at = 0
    done = 0
    for each in slices:
        if each.start > at:
            pieces.append(base[at : each.start])
        size = each.stop - each.start
        pieces.append(base[each] + rows[done : done + size])
        done += size
        at = each.stop
    if at < REFL:
        pieces.append(base[at:])
    return jnp.concatenate(pieces, 0)


def inverses(lowers):
    small = 8
    count = len(lowers)
    lane = iota((small, REFL), 1)
    group_of = (lane // (NH * TOK)) * (TOK // small) + (lane % TOK) // small
    groups = [(block, piece) for block in range(2) for piece in range(TOK // small)]

    def start_row(block, step, piece):
        return block * NH * TOK + step * TOK + piece * small

    folded = []
    for lower in lowers:
        for step in range(NH):
            rows = jnp.zeros((small, REFL), F32)
            for number, (block, piece) in enumerate(groups):
                first = start_row(block, step, piece)
                rows = jnp.where(group_of == number, lower[first : first + small], rows)
            folded.append(rows)
    height = NH * small
    lower_fold = jnp.concatenate(folded, 0)
    wide = iota((count * height, REFL), 1)
    high = iota((count * height, REFL), 0) % height
    inverse = ((wide // TOK) % NH == high // small) & (wide % small == high % small)
    inverse = inverse.astype(F32).reshape(count, height, REFL)
    for token in range(small):
        for step in range(NH):
            if token == small - 1 and step == NH - 1:
                continue
            source = (wide // (NH * TOK)) * (NH * TOK) + step * TOK + (wide % TOK) // small * small + token
            column = jnp.take_along_axis(lower_fold, source, axis=1, mode="promise_in_bounds")
            row = step * small + token
            inverse = inverse - column.reshape(count, height, REFL) * inverse[:, row : row + 1, :]
    results = []
    for number in range(count):
        pieces = []
        for block in range(2):
            for step in range(NH):
                rows = inverse[number, step * small : (step + 1) * small]
                for piece in range(TOK // small):
                    mine = group_of == block * (TOK // small) + piece
                    pieces.append(jnp.where(mine, rows, 0.0))
        results.append(jnp.concatenate(pieces, 0))
    size = small
    zero = jnp.zeros((REFL, REFL), F32)
    while size < CHUNK:
        slices = piece_rows(size)
        row_block, _, row_token, _ = place(iota((REFL, REFL), 0))
        column_block, _, column_token, _ = place(iota((REFL, REFL), 1))
        row_piece = (row_block * TOK + row_token) // size
        column_piece = (column_block * TOK + column_token) // size
        linked = taken(row_piece, slices) == taken(column_piece, slices) + 1
        crossings = [
            product(beside(jnp.where(linked, taken(lower, slices), 0.0)), factor(result))
            for lower, result in zip(lowers, results)
        ]
        changes = [
            product(beside(taken(result, slices)), factor(put(zero, crossing, slices)))
            for crossing, result in zip(crossings, results)
        ]
        results = [put(result, -change, slices) for change, result in zip(changes, results)]
        size *= 2
    return results


def read_rows(value):
    return jnp.concatenate(
        [
            value[(NH - 1) * TOK : NH * TOK],
            value[(2 * NH - 1) * TOK : 2 * NH * TOK],
        ],
        0,
    )


def call(kernel, outs, *args, scratch=(), flops=0, far=0, name=None):
    specs = [pl.BlockSpec(memory_space=pltpu.HBM)] * far
    specs += [pl.BlockSpec(memory_space=pltpu.VMEM)] * (len(args) - far)
    return pl.pallas_call(
        kernel,
        out_shape=outs,
        in_specs=specs,
        scratch_shapes=scratch,
        compiler_params=pltpu.CompilerParams(vmem_limit_bytes=24 * 2**20),
        cost_estimate=pl.CostEstimate(flops=flops, bytes_accessed=0, transcendentals=0),
        name=name,
    )(*args)


def shape(*sizes, dtype=BF16):
    return jax.ShapeDtypeStruct(sizes, dtype)


def axis_index(axis):
    return lax.axis_index(axis).astype(jnp.int32)


class Sizes:
    def __init__(self, groups, group_heads, chips):
        self.groups = groups
        self.group_heads = group_heads
        self.heads = group_heads // 2
        self.chips = chips
        self.units = self.heads * groups
        self.swapped = chips == self.heads and chips & (chips - 1) == 0

    def unit(self, number):
        return number // self.groups, number % self.groups


def shifted(index, by, size):
    moved = index + by
    return jnp.where(moved >= size, moved - size, moved)


def block_columns(source, first, count):
    return [
        source[:, pl.ds(pl.multiple_of(first + number * DK, DK), DK)] for number in range(count)
    ]


def pack_keys(sizes, keys, betas, log_gates, starts):
    rows = sizes.heads * KEY_ROWS
    count = sizes.heads * NH

    def kernel(far_keys, far_betas, far_gates, far_starts, *refs):
        outs = refs[: sizes.groups]
        keys, betas, log_gates, starts, done = refs[sizes.groups :]
        width = sizes.group_heads * NH * DK
        pairs = [(far_betas, betas), (far_gates, log_gates), (far_starts, starts)]
        for group in range(sizes.groups):
            part = slice(group * width, (group + 1) * width)
            pairs.append((far_keys.at[:, part], keys.at[:, part]))
        copies = [
            pltpu.make_async_copy(far, near, done.at[number])
            for number, (far, near) in enumerate(pairs)
        ]
        for copy in copies:
            copy.start()
        for copy in copies[:3]:
            copy.wait()
        z = axis_index("head")
        core = axis_index("core")
        heads = log_gates.shape[1]
        pieces = []
        for step in range(NH):
            extent = (heads, heads * NH)
            pick = iota(extent, 1) == iota(extent, 0) * NH + step
            pieces.append(dot_nt(pick.astype(BF16), betas[...]))
        same = iota((heads, heads), 0) == iota((heads, heads), 1)
        pieces.append(dot_nt(same.astype(BF16), log_gates[...]))
        length = sizes.groups * TOK
        own = iota((length, TOK), 0) == z * TOK + iota((length, TOK), 1)
        own_starts = jnp.broadcast_to(starts[...].astype(F32), (heads, length)).astype(BF16)
        pieces.append(dot(own_starts, own.astype(BF16)))
        scales = jnp.concatenate(pieces, 1).astype(BF16)
        for copy in copies[3:]:
            copy.wait()
        for ahead, out in enumerate(outs):
            target = shifted(z, ahead, sizes.groups)
            for side in range(2):
                owner = jnp.bitwise_xor(core, side)
                first = ((target * 2 + owner) * sizes.heads) * NH * DK
                for number, piece in enumerate(block_columns(keys, first, count)):
                    at = side * rows + number * TOK
                    out[at : at + TOK, :] = piece
            extent = (SCALE_ROWS, heads)
            pick = (iota(extent, 1) == target * sizes.group_heads + iota(extent, 0)) & (
                iota(extent, 0) < sizes.group_heads
            )
            out[2 * rows :, :] = dot(pick.astype(BF16), scales).astype(BF16)

    outs = [shape(2 * rows + SCALE_ROWS, DK)] * sizes.groups
    loaded = (keys, betas, log_gates, starts)
    scratch = [pltpu.VMEM(each.shape, each.dtype) for each in loaded]
    return call(
        kernel,
        outs,
        *[pltpu.with_memory_space_constraint(each, pltpu.HBM) for each in loaded],
        scratch=scratch + [pltpu.SemaphoreType.DMA((3 + sizes.groups,))],
        far=4,
        name="pack_keys",
    )


def swap_keys(sizes, arrived):
    rows = sizes.heads * KEY_ROWS

    def kernel(*refs):
        out = refs[-1]
        z = axis_index("head")
        for behind, piece in enumerate(refs[:-1]):
            source = shifted(z, sizes.groups - behind, sizes.groups) if behind else z
            out[source] = piece[rows:, :]

    return call(kernel, shape(sizes.groups, rows + SCALE_ROWS, DK), *arrived, name="swap_keys")


def pack_reads(sizes, values, queries):
    value_rows = sizes.heads * KEY_ROWS
    rows = value_rows + sizes.heads * TOK

    def kernel(values, queries, kept, sent):
        z = axis_index("head")
        core = axis_index("core")
        for ahead in range(sizes.groups):
            target = shifted(z, ahead, sizes.groups)
            for side, out in enumerate((kept, sent)):
                first = (target * 2 + jnp.bitwise_xor(core, side)) * sizes.heads * DK
                pieces = block_columns(values, first * NH, sizes.heads * NH)
                pieces += block_columns(queries, first, sizes.heads)
                for number, piece in enumerate(pieces):
                    out[ahead, number * TOK : (number + 1) * TOK, :] = piece

    return call(
        kernel, [shape(sizes.groups, rows, DK)] * 2, values, queries, name="pack_reads"
    )


def merge_reads(sizes, kept, swapped):
    value_rows = sizes.heads * KEY_ROWS
    query_rows = sizes.heads * TOK

    def kernel(kept, swapped, *outs):
        for ahead in range(sizes.groups):
            for side, source in enumerate((kept, swapped)):
                outs[ahead][side] = source[ahead, :value_rows, :]
                outs[sizes.groups + ahead][side] = source[ahead, value_rows:, :]

    outs = [shape(2, value_rows, DK)] * sizes.groups + [shape(2, query_rows, DK)] * sizes.groups
    merged = call(kernel, outs, kept, swapped, name="merge_reads")
    return merged[: sizes.groups], merged[sizes.groups :]


def gather(sizes, pieces, scratch):
    z = axis_index("head")
    core = axis_index("core")
    for behind, piece in enumerate(pieces):
        source = shifted(z, sizes.groups - behind, sizes.groups) if behind else z
        for side in range(2):
            scratch[jnp.bitwise_xor(core, side) * sizes.groups + source] = piece[side]


def unit_rows(scratch, head, chunk, count):
    first = head * count
    return jnp.concatenate(
        [
            scratch[2 * chunk, first : first + count, :],
            scratch[2 * chunk + 1, first : first + count, :],
        ],
        0,
    )


def key_stage(sizes, arrived, swapped):
    rows = sizes.heads * KEY_ROWS
    units = sizes.units
    groups = sizes.groups

    def kernel(*refs):
        pieces = refs[:groups]
        swapped = refs[groups]
        keys_out, inverse_out, end_out, ratio_out, row_out, step_out, prefix_out = refs[
            groups + 1 : groups + 8
        ]
        totals = refs[groups + 8 : groups + 8 + sizes.heads]
        blocks, scales, every = refs[groups + 8 + sizes.heads :]
        z = axis_index("head")
        core = axis_index("core")
        for behind, piece in enumerate(pieces):
            source = shifted(z, groups - behind, groups) if behind else z
            blocks[core * groups + source] = piece[:rows, :]
            scales[core * groups + source] = piece[2 * rows :, :]
        other = (1 - core) * groups
        for source in range(groups):
            blocks[other + source] = swapped[source, :rows, :]
            scales[other + source] = swapped[source, rows:, :]
        flat = scales[...].reshape(2 * groups * SCALE_ROWS, 4 * TOK)
        picks = []
        for block in range(2):
            extent = (units, 2 * groups * SCALE_ROWS)
            unit = iota(extent, 0)
            row = (unit % groups * 2 + block) * SCALE_ROWS + unit // groups
            pick = iota(extent, 1) == row + core * sizes.heads
            picks.append(dot(pick.astype(BF16), flat))
        by_unit = jnp.concatenate(picks, 1).astype(BF16)
        maps = scale_maps()
        as_rows = dot_nt(by_unit, maps)
        as_columns = dot_nt(maps, by_unit)
        decay_row, segment_row, beta_row = (
            as_rows[:, number * REFL : (number + 1) * REFL] for number in range(3)
        )
        decay_column, segment_column, beta_column = (
            as_columns[number * REFL : (number + 1) * REFL] for number in range(3)
        )
        carried_row = jnp.exp(decay_row) * (segment_row == 0).astype(F32)
        last = REFL - 1
        end_row = jnp.exp(decay_row[:, last:] - decay_row)
        end_row = end_row * (segment_row[:, last:] == segment_row).astype(F32)
        square = (REFL, REFL)
        _, _, _, row_time = place(iota(square, 0))
        _, _, _, column_time = place(iota(square, 1))
        causal = row_time >= column_time
        strict = row_time > column_time
        diagonal = row_time == column_time
        same = (iota((DK, DK), 0) == iota((DK, DK), 1)).astype(F32)
        row_out[0] = beta_row
        row_out[2] = carried_row
        for base in range(0, units, GROUP):
            members = range(base, min(base + GROUP, units))
            keys = [unit_rows(blocks, *sizes.unit(unit), KEY_ROWS) for unit in members]
            grams = [dot_nt(key, key) for key in keys]
            squares = [jnp.where(diagonal, gram, 0.0) for gram in grams]
            norm_rows = [lax.rsqrt(jnp.sum(each, 0, keepdims=True) + EPSILON) for each in squares]
            norm_columns = [
                lax.rsqrt(jnp.sum(each, 1, keepdims=True) + EPSILON) for each in squares
            ]
            lowers = []
            for number, unit in enumerate(members):
                keys_out[unit] = keys[number]
                one = slice(unit, unit + 1)
                linked = causal & (segment_column[:, one] == segment_row[one])
                gap = decay_column[:, one] - decay_row[one]
                ratio = jnp.where(linked, jnp.exp(jnp.minimum(gap, 0.0)), 0.0) * norm_rows[number]
                ratio_out[unit] = read_rows(ratio)
                strengths = beta_column[:, one] * norm_columns[number]
                lowers.append(jnp.where(strict, strengths * ratio * grams[number], 0.0))
            solved = inverses(lowers)
            pairs = [split(each) for each in solved]
            kept_rows = [
                beta_row[unit : unit + 1] * carried_row[unit : unit + 1] * norm
                for unit, norm in zip(members, norm_rows)
            ]
            turned_keys = [key.T for key in keys]
            ends = []
            for number, unit in enumerate(members):
                high, low = pairs[number]
                inverse_out[unit] = jnp.concatenate([high, low], 1)
                row_out[1, unit : unit + 1, :] = kept_rows[number]
                weights = end_row[unit : unit + 1] * norm_rows[number]
                ends.append(
                    product(
                        beside(turned_keys[number].astype(F32) * weights), factor_of(high, low)
                    )
                )
            for number, unit in enumerate(members):
                turned = turned_keys[number]
                end_out[unit] = beside(ends[number] * beta_row[unit : unit + 1])
                every[unit] = carried_row[unit : unit + 1, last:] * same - dot_nt(
                    jnp.concatenate([turned, turned], 1), beside(ends[number] * kept_rows[number])
                )
        prefixes = [same] * sizes.heads
        for chunk in range(groups):
            for head in range(sizes.heads):
                unit = head * groups + chunk
                step = every[unit]
                high, low = split(step)
                step_out[unit] = jnp.concatenate([high, low], 1)
                prefix_out[unit] = prefixes[head]
                if chunk == 0:
                    prefixes[head] = step
                else:
                    prefixes[head] = product(beside(prefixes[head]), factor_of(high, low))
        if sizes.swapped:
            for head in range(sizes.heads):
                every[head] = prefixes[head]
            chip = axis_index("chip")
            for number in range(sizes.heads):
                totals[number][...] = every[jnp.bitwise_xor(chip, number)]
        else:
            for head in range(sizes.heads):
                totals[head][...] = prefixes[head]

    outs = [
        shape(units, REFL, DK),
        shape(units, REFL, 2 * REFL),
        shape(units, DK, 2 * REFL),
        shape(units, CHUNK, REFL, dtype=F32),
        shape(3, units, REFL, dtype=F32),
        shape(units, DK, 2 * DK),
        shape(units, DK, DK, dtype=F32),
    ] + [shape(DK, DK, dtype=F32)] * sizes.heads
    scratch = [
        pltpu.VMEM((2 * groups, rows, DK), BF16),
        pltpu.VMEM((2 * groups, SCALE_ROWS, DK), BF16),
        pltpu.VMEM((units, DK, DK), F32),
    ]
    results = call(
        kernel, outs, *arrived, swapped, scratch=scratch, flops=6_000_000_000, name="key_stage"
    )
    return results[:7], results[7:]


def value_stage(sizes, pieces, ends, steps):
    groups = sizes.groups

    def kernel(*refs):
        pieces = refs[:groups]
        ends, steps, values_out, before_out = refs[groups : groups + 4]
        totals = refs[groups + 4 : groups + 4 + sizes.heads]
        blocks, every = refs[groups + 4 + sizes.heads :]
        gather(sizes, pieces, blocks)
        injects = []
        for unit in range(sizes.units):
            value = unit_rows(blocks, *sizes.unit(unit), KEY_ROWS)
            values_out[unit] = value
            turned = value.T
            injects.append(dot_nt(jnp.concatenate([turned, turned], 1), ends[unit]))
        sums = [jnp.zeros((DV, DK), F32)] * sizes.heads
        for chunk in range(groups):
            for head in range(sizes.heads):
                unit = head * groups + chunk
                before_out[unit] = sums[head]
                if chunk == 0:
                    sums[head] = injects[unit]
                else:
                    step = steps[unit]
                    sums[head] = injects[unit] + product(
                        beside(sums[head]), factor_of(step[:, :DK], step[:, DK:])
                    )
        if sizes.swapped:
            for head in range(sizes.heads):
                every[head] = sums[head]
            chip = axis_index("chip")
            for number in range(sizes.heads):
                totals[number][...] = every[jnp.bitwise_xor(chip, number)]
        else:
            for head in range(sizes.heads):
                totals[head][...] = sums[head]

    outs = [shape(sizes.units, REFL, DV), shape(sizes.units, DV, DK, dtype=F32)]
    outs += [shape(DV, DK, dtype=F32)] * sizes.heads
    scratch = [
        pltpu.VMEM((2 * groups, sizes.heads * KEY_ROWS, DV), BF16),
        pltpu.VMEM((sizes.heads, DV, DK), F32),
    ]
    results = call(
        kernel, outs, *pieces, ends, steps, scratch=scratch, flops=2_000_000_000, name="value_stage"
    )
    return results[0], results[1], results[2:]


def scan_states(sizes, transitions, injects):
    chips = sizes.chips

    def kernel(*refs):
        transitions = refs[:chips]
        injects = refs[chips : 2 * chips]
        outs = refs[2 * chips : 3 * chips]
        step, inject, entry = refs[3 * chips :]
        chip = axis_index("chip")
        for number in range(chips):
            source = jnp.bitwise_xor(chip, number)
            step[source] = transitions[number][...]
            inject[source] = injects[number][...]
        state = jnp.zeros((DV, DK), F32)
        for index in range(chips):
            entry[index] = state
            if index == 0:
                state = inject[index]
            elif index < chips - 1:
                state = product(beside(state), factor(step[index])) + inject[index]
        for number in range(chips):
            outs[number][...] = entry[jnp.bitwise_xor(chip, number)]

    scratch = [pltpu.VMEM((chips, DV, DK), F32)] * 3
    return call(
        kernel,
        [shape(DV, DK, dtype=F32)] * chips,
        *transitions,
        *injects,
        scratch=scratch,
        name="scan_states",
    )


def exchanged(sizes, parts):
    return [parts[0]] + [
        lax.ppermute(part, "chip", [(chip, chip ^ number) for chip in range(sizes.chips)])
        for number, part in enumerate(parts)
        if number
    ]


def entry_states(sizes, transitions, injects):
    if sizes.swapped:
        arrived = exchanged(sizes, transitions), exchanged(sizes, injects)
        return exchanged(sizes, scan_states(sizes, *arrived))
    transition = jnp.stack(transitions)
    inject = jnp.stack(injects)
    forward = [(chip, chip + 1) for chip in range(sizes.chips - 1)]

    def advance(_, entry):
        left = jnp.einsum("hvd,hde->hve", entry, transition, precision=lax.Precision.HIGHEST)
        return lax.ppermute(left + inject, "chip", forward)

    entry = lax.fori_loop(0, sizes.chips - 1, advance, jnp.zeros_like(inject))
    return [entry[head] for head in range(sizes.heads)]


def query_stage(sizes, pieces, values, before, keys, inverses_, ratios, rows, prefixes):
    groups = sizes.groups

    def kernel(*refs):
        pieces = refs[:groups]
        values, before, keys, inverse, ratio, rows, prefix, reader_out, inner_out, blocks = refs[
            groups:
        ]
        gather(sizes, pieces, blocks)
        for base in range(0, sizes.units, GROUP):
            members = range(base, min(base + GROUP, sizes.units))
            queries = [unit_rows(blocks, *sizes.unit(unit), TOK) for unit in members]
            scores = []
            for number, unit in enumerate(members):
                pair = inverse[unit]
                score = dot_nt(queries[number], keys[unit]) * ratio[unit]
                scores.append(product(beside(score), factor_of(pair[:, :REFL], pair[:, REFL:])))
            for number, unit in enumerate(members):
                one = slice(unit, unit + 1)
                inner = dot(beside(scores[number] * rows[0, one, :]), twice(values[unit]))
                carried = read_rows(jnp.broadcast_to(rows[2, one, :], (DK, REFL)).T)
                reader = carried * queries[number].astype(F32) - dot(
                    beside(scores[number] * rows[1, one, :]), twice(keys[unit])
                )
                high, low = split(jnp.concatenate([prefix[unit], before[unit]], 0))
                pair = beside(reader)
                both = dot_nt(pair, jnp.concatenate([high, high], 1)) + dot_nt(pair[:, :DK], low)
                reader_out[unit] = beside(both[:, :DK])
                inner_out[unit] = inner + both[:, DK:]

    outs = [
        shape(sizes.units, CHUNK, 2 * DK),
        shape(sizes.units, CHUNK, DV, dtype=F32),
    ]
    scratch = [pltpu.VMEM((2 * groups, sizes.heads * TOK, DK), BF16)]
    return call(
        kernel,
        outs,
        *pieces,
        values,
        before,
        keys,
        inverses_,
        ratios,
        rows,
        prefixes,
        scratch=scratch,
        flops=3_000_000_000,
        name="query_stage",
    )


def read_states(sizes, states, readers, inners, side):
    groups = sizes.groups
    half = groups // 2

    def kernel(*refs):
        states = refs[: sizes.heads]
        readers, inners, out, entry = refs[sizes.heads :]
        core = axis_index("core")
        chip = axis_index("chip") if sizes.swapped else 0
        for number in range(sizes.heads):
            place_ = jnp.bitwise_xor(chip, number) if sizes.swapped else number
            entry[place_] = states[number][...]
        for head in range(sizes.heads):
            high, low = split(entry[head])
            stack = jnp.concatenate(
                [
                    jnp.concatenate([high, high], 1),
                    jnp.concatenate([low, jnp.zeros_like(low)], 1),
                ],
                0,
            )
            first = head * groups + jnp.bitwise_xor(core, side) * half
            pair = readers[pl.ds(first, half)].reshape(half * CHUNK, 2 * DK)
            both = dot_nt(pair, stack)
            inner = inners[pl.ds(first, half)].reshape(half * CHUNK, DV)
            result = inner + both[:, :DV] + both[:, DV:]
            out[:, head * DV : (head + 1) * DV] = result.astype(BF16)

    out = shape(half * CHUNK, sizes.heads * DV)
    scratch = [pltpu.VMEM((sizes.heads, DV, DK), F32)]
    return call(kernel, out, *states, readers, inners, scratch=scratch, name="read_states")


def join(sizes, own, other):
    width = sizes.heads * DV

    def kernel(own, other, out):
        first = axis_index("core") * width
        out[:, pl.ds(pl.multiple_of(first, width), width)] = own[...]
        out[:, pl.ds(pl.multiple_of(width - first, width), width)] = other[...]

    return call(kernel, shape(own.shape[0], 2 * width), own, other, name="join")


def local(queries, keys, values, betas, log_gates, starts):
    groups = lax.axis_size("head")
    sizes = Sizes(groups, log_gates.shape[1] // groups, lax.axis_size("chip"))

    def spread(parts):
        return [parts[0]] + [
            lax.ppermute(part, "head", [(z, (z + ahead) % groups) for z in range(groups)])
            for ahead, part in enumerate(parts)
            if ahead
        ]

    def swapped(part):
        return lax.ppermute(part, "core", [(0, 1), (1, 0)])

    arrived = spread(pack_keys(sizes, keys, betas, log_gates, starts.reshape(1, -1)))
    kept, sent = pack_reads(sizes, values, queries)
    value_parts, query_parts = merge_reads(sizes, kept, swapped(sent))
    value_parts = spread(value_parts)
    query_parts = spread(query_parts)
    other_keys = swapped(swap_keys(sizes, arrived))
    (unit_keys, inverse, ends, ratios, rows, steps, prefixes), transitions = key_stage(
        sizes, arrived, other_keys
    )
    unit_values, before, injects = value_stage(sizes, value_parts, ends, steps)
    states = entry_states(sizes, transitions, injects)
    readers, inners = query_stage(
        sizes, query_parts, unit_values, before, unit_keys, inverse, ratios, rows, prefixes
    )
    other = swapped(read_states(sizes, states, readers, inners, 1))
    own = read_states(sizes, states, readers, inners, 0)
    return join(sizes, own, other)


def solution(mesh):
    devices = mesh.devices
    rows = P(("chip", "core", "head"), None)
    return jax.shard_map(
        local,
        mesh=Mesh(
            devices.reshape(devices.shape[0] // 2, 2, devices.shape[1]), ("chip", "core", "head")
        ),
        in_specs=(rows, rows, rows, rows, rows, P(("chip", "core"))),
        out_specs=P(("chip", "core"), "head"),
        check_vma=False,
    )
```
